32 devices in a mesh: utt: 8 (over z, core), wide: 4 (over y, x).
Axes of the slice: x: 2, y: 2, z: 4, core: 2. Of those that a mesh axis runs over, the one named last changes fastest.
Arguments:
- frames: bfloat16 [16, 1024, 1024], P('utt', 'wide'), may hold values from -6 to 6
- lengths: int32 [16], P('utt'), may hold values from 512 to 1024, as said below
- masked: int32 [16, 1024], P('utt', 'wide'), may hold values from 0 to 1, as said below
- cotangent: bfloat16 [16, 1024, 1024], P('utt', 'wide'), may hold values from -6 to 6
- first_gain: bfloat16 [1024], replicated, may hold values from 0.25 to 1.75
- first_up: bfloat16 [4096, 1024], P(('utt', 'wide')), may hold values from -0.1875 to 0.1875
- first_down: bfloat16 [4096, 1024], P(('utt', 'wide')), may hold values from -0.09375 to 0.09375
- attn_gain: bfloat16 [1024], replicated, may hold values from 0.25 to 1.75
- query_weight: bfloat16 [1024, 1024], P('wide'), may hold values from -0.1875 to 0.1875
- key_weight: bfloat16 [1024, 1024], P('wide'), may hold values from -0.1875 to 0.1875
- value_weight: bfloat16 [1024, 1024], P('wide'), may hold values from -0.1875 to 0.1875
- out_weight: bfloat16 [1024, 1024], P('wide'), may hold values from -2 to 2
- place_weight: bfloat16 [1024, 1024], P('wide'), may hold values from -0.1875 to 0.1875
- content_bias: bfloat16 [1024], P('wide'), may hold values from -3 to 3
- place_bias: bfloat16 [1024], P('wide'), may hold values from -3 to 3
- conv_gain: bfloat16 [1024], replicated, may hold values from 0.25 to 1.75
- glu_weight: bfloat16 [2048, 1024], P('wide'), may hold values from -0.1875 to 0.1875
- depth_kernel: bfloat16 [31, 1024], replicated, may hold values from -1 to 1
- middle_gain: bfloat16 [1024], replicated, may hold values from 0.25 to 1.75
- point_weight: bfloat16 [1024, 1024], P('wide'), may hold values from -0.1875 to 0.1875
- second_gain: bfloat16 [1024], replicated, may hold values from 0.25 to 1.75
- second_up: bfloat16 [4096, 1024], P(('utt', 'wide')), may hold values from -0.1875 to 0.1875
- second_down: bfloat16 [4096, 1024], P(('utt', 'wide')), may hold values from -0.09375 to 0.09375
- final_gain: bfloat16 [1024], replicated, may hold values from 0.25 to 1.75
Outputs:
- output: bfloat16 [16, 1024, 1024], P('utt', 'wide')
- grad_frames: bfloat16 [16, 1024, 1024], P('utt', 'wide')
- grad_first_gain: float32 [1024], replicated
- grad_first_up: float32 [4096, 1024], P(('utt', 'wide'))
- grad_first_down: float32 [4096, 1024], P(('utt', 'wide'))
- grad_attn_gain: float32 [1024], replicated
- grad_query_weight: float32 [1024, 1024], P('wide')
- grad_key_weight: float32 [1024, 1024], P('wide')
- grad_value_weight: float32 [1024, 1024], P('wide')
- grad_out_weight: float32 [1024, 1024], P('wide')
- grad_place_weight: float32 [1024, 1024], P('wide')
- grad_content_bias: float32 [1024], P('wide')
- grad_place_bias: float32 [1024], P('wide')
- grad_conv_gain: float32 [1024], replicated
- grad_glu_weight: float32 [2048, 1024], P('wide')
- grad_depth_kernel: float32 [31, 1024], replicated
- grad_middle_gain: float32 [1024], replicated
- grad_point_weight: float32 [1024, 1024], P('wide')
- grad_second_gain: float32 [1024], replicated
- grad_second_up: float32 [4096, 1024], P(('utt', 'wide'))
- grad_second_down: float32 [4096, 1024], P(('utt', 'wide'))
- grad_final_gain: float32 [1024], replicated
The draws below stay inside these ranges and needn't reach their ends.
Inputs may be any that keep to these rules, and one draw needn't show every extreme that they name: `lengths`: in each aligned block of 2 utterances (one index of utt) one utterance has exactly 1024 frames. Each utterance has its own share of masked frames; most shares are small, a few are large; frames past an utterance's length may be marked and count as unmasked.
All inputs are finite; a program needn't handle non-finite values.
Results may differ from the reference program's by a relative error of at most 0.023.
Values may be sent and summed in bfloat16 or wider, within the bound.
A program may use at most 320 MiB of HBM per device.

```python
import math
import jax
import jax.numpy as jnp
from jax import lax

D = 1024
HEADS = 16
HEAD_DIM = 64
FF = 4096
KERNEL = 31
LEN = 1024
QBLK = 512
UTTS = 2
BATCH = 16
RIM = 15


def draw_lengths(key, part):
    base_key, pick_key = jax.random.split(jax.random.fold_in(key, 7))
    uniform_len = jax.random.randint(base_key, (BATCH,), LEN // 2, LEN + 1)
    chosen = jax.random.randint(pick_key, (BATCH // UTTS,), 0, UTTS)
    position = jnp.arange(BATCH, dtype=jnp.int32)
    is_full = position % UTTS == jnp.repeat(chosen, UTTS)
    return jnp.where(is_full, LEN, uniform_len).astype(jnp.int32)


def draw_masked(key, part):
    level_key, frame_key = jax.random.split(jax.random.fold_in(key, 11))
    steepness = jax.random.randint(level_key, (BATCH, 1), 0, 16)
    mask_level = 3 + steepness * steepness * steepness // 64
    ticket = jax.random.randint(frame_key, (BATCH, LEN), 0, 64)
    return (ticket < mask_level).astype(jnp.int32)


def steps_of(own_key, extent, pieces, least, top_value):
    gain, own = 1.0, jax.random.fold_in(own_key, 6)
    for axis_at, shards_of in pieces:
        draws = jnp.exp(jax.random.uniform(jax.random.fold_in(own, axis_at), (shards_of,), jnp.float32, least / len(pieces), top_value / len(pieces)))
        gain = gain * jnp.repeat(draws, extent[axis_at] // shards_of).reshape([-1 if axis == axis_at else 1 for axis in range(len(extent))])
    return gain


def gaussian(rng, dims, width, reach, cuts=(), kind=jnp.bfloat16):
    values = width * jax.random.normal(rng, dims, jnp.float32)
    if cuts:
        values = values * steps_of(rng, dims, cuts, -0.22, 0.18)
    return jnp.clip(values, -reach, reach).astype(kind)


def setup_inputs(seed: int = 0) -> dict:
    arg_keys = jax.random.split(jax.random.key(seed), 25)
    return {
        "frames": gaussian(arg_keys[0], (BATCH, LEN, D), 1.0, 6.0, ((0, 8), (1, 4))),
        "lengths": draw_lengths(jax.random.fold_in(arg_keys[24], 71), 0),
        "masked": draw_masked(jax.random.fold_in(arg_keys[24], 71), 0),
        "cotangent": gaussian(arg_keys[3], (BATCH, LEN, D), 1.0, 6.0, ((0, 8), (1, 4))),
        "first_gain": jnp.clip(1.0 + 0.15 * jax.random.normal(arg_keys[4], (D,), jnp.float32), 0.25, 1.75).astype(jnp.bfloat16),
        "first_up": gaussian(arg_keys[5], (FF, D), D ** -0.5, 0.1875, ((0, 32),)),
        "first_down": gaussian(arg_keys[6], (FF, D), FF ** -0.5, 0.09375, ((0, 32),)),
        "attn_gain": jnp.clip(1.0 + 0.15 * jax.random.normal(arg_keys[7], (D,), jnp.float32), 0.25, 1.75).astype(jnp.bfloat16),
        "query_weight": gaussian(arg_keys[8], (HEADS * HEAD_DIM, D), D ** -0.5, 0.1875, ((0, 4),)),
        "key_weight": gaussian(arg_keys[9], (HEADS * HEAD_DIM, D), D ** -0.5, 0.1875, ((0, 4),)),
        "value_weight": gaussian(arg_keys[10], (HEADS * HEAD_DIM, D), D ** -0.5, 0.1875, ((0, 4),)),
        "out_weight": gaussian(arg_keys[11], (HEADS * HEAD_DIM, D), (max(1, HEADS * HEAD_DIM * 8 // LEN)) ** -0.5, 2.0, ((0, 4),)),
        "place_weight": gaussian(arg_keys[12], (HEADS * HEAD_DIM, D), D ** -0.5, 0.1875, ((0, 4),)),
        "content_bias": gaussian(arg_keys[13], (HEADS * HEAD_DIM,), 0.5, 3.0, ((0, 4),)),
        "place_bias": gaussian(arg_keys[14], (HEADS * HEAD_DIM,), 0.5, 3.0, ((0, 4),)),
        "conv_gain": jnp.clip(1.0 + 0.15 * jax.random.normal(arg_keys[15], (D,), jnp.float32), 0.25, 1.75).astype(jnp.bfloat16),
        "glu_weight": gaussian(arg_keys[16], (2 * D, D), D ** -0.5, 0.1875, ((0, 4),)),
        "depth_kernel": gaussian(arg_keys[17], (KERNEL, D), KERNEL ** -0.5, 1.0),
        "middle_gain": jnp.clip(1.0 + 0.15 * jax.random.normal(arg_keys[18], (D,), jnp.float32), 0.25, 1.75).astype(jnp.bfloat16),
        "point_weight": gaussian(arg_keys[19], (D, D), D ** -0.5, 0.1875, ((0, 4),)),
        "second_gain": jnp.clip(1.0 + 0.15 * jax.random.normal(arg_keys[20], (D,), jnp.float32), 0.25, 1.75).astype(jnp.bfloat16),
        "second_up": gaussian(arg_keys[21], (FF, D), D ** -0.5, 0.1875, ((0, 32),)),
        "second_down": gaussian(arg_keys[22], (FF, D), FF ** -0.5, 0.09375, ((0, 32),)),
        "final_gain": jnp.clip(1.0 + 0.15 * jax.random.normal(arg_keys[23], (D,), jnp.float32), 0.25, 1.75).astype(jnp.bfloat16),
    }


@jax.custom_vjp
def low(v):
    return lax.optimization_barrier(v.astype(jnp.bfloat16)).astype(jnp.float32)

@jax.custom_vjp
def low_back(v):
    return v

def low_keep(v):
    return (low(v), None)

def low_pass(kept, grad):
    return (grad,)

def back_keep(v):
    return (v, None)

def back_low(kept, grad):
    return (low(grad),)
low.defvjp(low_keep, low_pass)
low_back.defvjp(back_keep, back_low)
EPSILON = 1e-05
MASKED_SCORE = -1e+30
PRECISE = lax.Precision.HIGHEST

def norm_rows(values, gain_vec):
    average = lax.optimization_barrier(jnp.mean(values, axis=-1, keepdims=True))
    centred = values - average
    spread = lax.optimization_barrier(jnp.mean(centred * centred, axis=-1, keepdims=True))
    return centred * lax.rsqrt(spread + EPSILON) * gain_vec

def mult_trans(first_mat, second_mat):
    return lax.dot_general(first_mat, second_mat, (((1,), (1,)), ((), ())), precision=PRECISE)

def mult_plain(first_mat, second_mat):
    return jnp.dot(first_mat, second_mat, precision=PRECISE)

def relative_table(length, channels):
    offsets = length - 1 - jnp.arange(2 * length - 1).astype(jnp.float32)
    rates = jnp.exp(jnp.arange(channels // 2).astype(jnp.float32) * (-2.0 * math.log(10000.0) / channels))
    angles = offsets[:, None] * rates[None, :]
    return jnp.concatenate([jnp.sin(angles), jnp.cos(angles)], axis=1)

def skew_rows(reversed_scores):
    block_rows, span = reversed_scores.shape
    flat = reversed_scores.reshape(-1)[block_rows - 1:block_rows - 1 + block_rows * (span - 1)]
    return flat.reshape(block_rows, span - 1)[:, :span - block_rows + 1]

def feed_forward(stream, gain_vec, up_rows, down_rows):
    normed = low(norm_rows(stream, gain_vec))
    before = low_back(mult_trans(normed, up_rows))
    active = low(jax.nn.silu(before))
    return stream + 0.5 * low_back(mult_plain(active, down_rows))

def attend_head(head_items, key_ok):
    query_rows, key_rows, value_rows, place_rows, bias_first, bias_second = head_items
    with_u = low(query_rows + bias_first)
    with_v = low(query_rows + bias_second)
    score_scale = 1.0 / math.sqrt(HEAD_DIM)

    def one_block(block_index):
        first_row = block_index * QBLK
        block_u = lax.dynamic_slice_in_dim(with_u, first_row, QBLK, 0)
        block_v = lax.dynamic_slice_in_dim(with_v, first_row, QBLK, 0)
        near_rows = lax.dynamic_slice_in_dim(place_rows, LEN - QBLK - first_row, QBLK + LEN - 1, 0)
        scores = low_back((mult_trans(block_u, key_rows) + skew_rows(mult_trans(block_v, near_rows))) * score_scale)
        scores = jnp.where(key_ok[None, :], scores, MASKED_SCORE)
        highest = lax.optimization_barrier(jnp.max(scores, axis=1, keepdims=True))
        weights = jnp.exp(scores - highest)
        attend_prob = weights / lax.optimization_barrier(jnp.sum(weights, axis=1, keepdims=True))
        return mult_plain(low(attend_prob), value_rows)
    blocks = lax.map(jax.checkpoint(one_block), jnp.arange(LEN // QBLK, dtype=jnp.int32))
    return blocks.reshape(LEN, HEAD_DIM)

def attention(stream, gain_vec, query_weight, key_weight, value_weight, out_weight, place_weight, content_bias, place_bias, frame_ok, rel_table):
    normed = low(norm_rows(stream, gain_vec))
    query_all = low(low_back(mult_trans(normed, query_weight)))
    key_all = low(low_back(mult_trans(normed, key_weight)))
    value_all = low(low_back(mult_trans(normed, value_weight)))
    place_all = low(low_back(mult_trans(rel_table, place_weight)))
    key_ok = frame_ok > 0.5

    def by_heads(matrix):
        return matrix.reshape(matrix.shape[0], HEADS, HEAD_DIM).transpose(1, 0, 2)
    head_items = (by_heads(query_all), by_heads(key_all), by_heads(value_all), by_heads(place_all), content_bias.reshape(HEADS, HEAD_DIM), place_bias.reshape(HEADS, HEAD_DIM))
    attended = lax.map(lambda items_one: attend_head(items_one, key_ok), head_items)
    attended = low(low_back(attended.transpose(1, 0, 2).reshape(LEN, HEADS * HEAD_DIM)))
    return stream + low_back(mult_plain(attended, out_weight))

def convolve(stream, gain_vec, glu_weight, depth_kernel, middle_gain, point_weight, frame_ok):
    normed = low(norm_rows(stream, gain_vec))
    glu_in = low_back(mult_trans(normed, glu_weight))
    gated = low(glu_in[:, :D] * jax.nn.sigmoid(glu_in[:, D:]) * frame_ok[:, None])
    padded = jnp.pad(gated, ((RIM, RIM), (0, 0)))
    conv_out = jnp.zeros((LEN, D), jnp.float32)
    for offset in range(KERNEL):
        conv_out = conv_out + padded[offset:offset + LEN] * depth_kernel[offset]
    conv_out = low_back(conv_out)
    swished = low(jax.nn.silu(norm_rows(conv_out, middle_gain)))
    return stream + low_back(mult_trans(swished, point_weight))

def conformer(stream0, weight_list, frame_ok, rel_table):
    first_gain, first_up, first_down, attn_gain, query_weight, key_weight, value_weight, out_weight, place_weight, content_bias, place_bias, conv_gain, glu_weight, depth_kernel, middle_gain, point_weight, second_gain, second_up, second_down, final_gain = weight_list
    stream1 = feed_forward(stream0, first_gain, first_up, first_down)
    stream2 = attention(stream1, attn_gain, query_weight, key_weight, value_weight, out_weight, place_weight, content_bias, place_bias, frame_ok, rel_table)
    stream3 = convolve(stream2, conv_gain, glu_weight, depth_kernel, middle_gain, point_weight, frame_ok)
    stream4 = feed_forward(stream3, second_gain, second_up, second_down)
    return norm_rows(stream4, final_gain)

def reference(frames, lengths, masked, cotangent, first_gain, first_up, first_down, attn_gain, query_weight, key_weight, value_weight, out_weight, place_weight, content_bias, place_bias, conv_gain, glu_weight, depth_kernel, middle_gain, point_weight, second_gain, second_up, second_down, final_gain):
    weight_list = tuple((weight_arg.astype(jnp.float32) for weight_arg in (first_gain, first_up, first_down, attn_gain, query_weight, key_weight, value_weight, out_weight, place_weight, content_bias, place_bias, conv_gain, glu_weight, depth_kernel, middle_gain, point_weight, second_gain, second_up, second_down, final_gain)))
    rel_table = low(relative_table(LEN, D))

    def scan_step(running, utter_item):
        utt_frames, utt_length, utt_mask, utt_cot = utter_item
        frame_ok = (jnp.arange(LEN, dtype=jnp.int32) < utt_length).astype(jnp.float32)

        def run_layer(frames_in, *weights_in):
            return conformer(frames_in, weights_in, frame_ok, rel_table)
        layer_out, layer_pull = jax.vjp(run_layer, utt_frames.astype(jnp.float32), *weight_list)
        seed_grad = utt_cot.astype(jnp.float32) * (utt_mask.astype(jnp.float32) * frame_ok)[:, None]
        gradients = layer_pull(seed_grad)
        running = tuple((held_grad + new_grad for held_grad, new_grad in zip(running, gradients[1:])))
        return (running, (layer_out.astype(jnp.bfloat16), gradients[0].astype(jnp.bfloat16)))
    zero_grads = tuple((jnp.zeros(weight_arg.shape, jnp.float32) for weight_arg in weight_list))
    running, (outputs, grad_frames) = lax.scan(scan_step, zero_grads, (frames, lengths, masked, cotangent))
    return (outputs, grad_frames, running[0], running[1], running[2], running[3], running[4], running[5], running[6], running[7], running[8], running[9], running[10], running[11], running[12], running[13], running[14], running[15], running[16], running[17], running[18], running[19])
```

```python
from functools import partial
import math

import jax
import jax.numpy as jnp
from jax import lax
from jax.experimental import pallas as pl
from jax.experimental.pallas import tpu as pltpu
from jax.sharding import PartitionSpec as P

HEAD_DIM = 64
KERNEL = 31
QBLK = 512
RIM = 15
PAIR = 128
ROWS_FWD = 512
ROWS_BWD = 256
VMEM = 56 * 2**20


EPSILON = 1e-05
MASKED_SCORE = -1e30


def with_halo(block, sides, width):
    for axis, dim in sides:
        count = lax.axis_size(axis)
        forward = [(i, i + 1) for i in range(count - 1)]
        backward = [(target, source) for source, target in forward]
        low = lax.ppermute(
            lax.slice_in_dim(block, block.shape[dim] - width, None, axis=dim), axis, forward
        )
        high = lax.ppermute(lax.slice_in_dim(block, 0, width, axis=dim), axis, backward)
        block = jnp.concatenate([low, block, high], axis=dim)
    return block


def norm_rows(values, gain_vec):
    average = jnp.mean(values, axis=-1, keepdims=True)
    centred = values - average
    spread = jnp.mean(centred * centred, axis=-1, keepdims=True)
    return centred * lax.rsqrt(spread + EPSILON) * gain_vec


def silu_slope(before):
    squash = jax.nn.sigmoid(before)
    return squash * (1.0 + before * (1.0 - squash))


def mult_trans(first_mat, second_mat):
    return lax.dot_general(
        first_mat, second_mat, (((1,), (1,)), ((), ())), preferred_element_type=jnp.float32
    )


def mult_plain(first_mat, second_mat):
    return jnp.dot(first_mat, second_mat, preferred_element_type=jnp.float32)


def mult_rows(first_mat, second_mat):
    return lax.dot_general(
        first_mat, second_mat, (((0,), (0,)), ((), ())), preferred_element_type=jnp.float32
    )


def relative_table(length, channels):
    offsets = length - 1 - jnp.arange(2 * length - 1).astype(jnp.float32)
    rates = jnp.exp(
        jnp.arange(channels // 2).astype(jnp.float32) * (-2.0 * math.log(10000.0) / channels)
    )
    angles = offsets[:, None] * rates[None, :]
    return jnp.concatenate([jnp.sin(angles), jnp.cos(angles)], axis=1)


def skew_rows(reversed_scores):
    block_rows, span = reversed_scores.shape
    flat = reversed_scores.reshape(-1)[block_rows - 1 : block_rows - 1 + block_rows * (span - 1)]
    return flat.reshape(block_rows, span - 1)[:, : span - block_rows + 1]


def unskew_rows(grad_scores, span):
    block_rows, length = grad_scores.shape
    padded = jnp.pad(grad_scores, ((0, 0), (0, span - 1 - length)))
    flat = jnp.pad(padded.reshape(-1), (block_rows - 1, 1))
    return flat.reshape(block_rows, span)


def gather_ffn(up_rows, down_rows):
    return (
        lax.all_gather(up_rows, ("utt", "wide"), axis=0, tiled=True),
        lax.all_gather(down_rows, ("utt", "wide"), axis=0, tiled=True),
    )


def sum_ffn(grad_up, grad_down):
    return (
        lax.psum_scatter(grad_up, ("utt", "wide"), scatter_dimension=0, tiled=True),
        lax.psum_scatter(grad_down, ("utt", "wide"), scatter_dimension=0, tiled=True),
    )


def ffn_forward(stream, gain_vec, up_full, down_full):
    normed, norm_pull = jax.vjp(norm_rows, stream, gain_vec)
    normed_low = normed.astype(jnp.bfloat16)
    before = mult_trans(normed_low, up_full)
    active_low = jax.nn.silu(before).astype(jnp.bfloat16)
    return (
        stream + 0.5 * mult_plain(active_low, down_full),
        (norm_pull, normed_low, before, active_low),
    )


def ffn_backward(grad_stream, saved_ffn, up_full, down_full):
    norm_pull, normed_low, before, active_low = saved_ffn
    grad_out = (0.5 * grad_stream).astype(jnp.bfloat16)
    grad_down = mult_rows(active_low, grad_out)
    grad_before = (mult_trans(grad_out, down_full) * silu_slope(before)).astype(jnp.bfloat16)
    grad_up = mult_rows(grad_before, normed_low)
    grad_input, grad_gain = norm_pull(mult_plain(grad_before, up_full))
    return (grad_stream + grad_input, grad_gain, grad_up, grad_down)


def head_forward(
    query_rows,
    key_rows,
    value_rows,
    place_rows,
    bias_first,
    bias_second,
    key_ok,
    block_rows,
    score_scale,
):
    length, head_width = query_rows.shape
    with_u = (query_rows.astype(jnp.float32) + bias_first).astype(jnp.bfloat16)
    with_v = (query_rows.astype(jnp.float32) + bias_second).astype(jnp.bfloat16)

    def one_block(block_index):
        first_row = block_index * block_rows
        block_u = lax.dynamic_slice_in_dim(with_u, first_row, block_rows, 0)
        block_v = lax.dynamic_slice_in_dim(with_v, first_row, block_rows, 0)
        near_rows = lax.dynamic_slice_in_dim(
            place_rows, length - block_rows - first_row, block_rows + length - 1, 0
        )
        scores = (
            mult_trans(block_u, key_rows) + skew_rows(mult_trans(block_v, near_rows))
        ) * score_scale
        scores = jnp.where(key_ok[None, :], scores, MASKED_SCORE)
        highest = jnp.max(scores, axis=1, keepdims=True)
        weights = jnp.exp(scores - highest)
        running = jnp.sum(weights, axis=1, keepdims=True)
        attend_prob = (weights / running).astype(jnp.bfloat16)
        return (
            mult_plain(attend_prob, value_rows).astype(jnp.bfloat16),
            (highest + jnp.log(running))[:, 0],
        )

    attended, log_total = lax.map(one_block, jnp.arange(length // block_rows, dtype=jnp.int32))
    return (attended.reshape(length, head_width), log_total.reshape(length))


def head_backward(
    query_rows,
    key_rows,
    value_rows,
    place_rows,
    bias_first,
    bias_second,
    key_ok,
    log_total,
    grad_mixed,
    block_rows,
    score_scale,
):
    length, head_width = query_rows.shape
    span = block_rows + length - 1
    with_u = (query_rows.astype(jnp.float32) + bias_first).astype(jnp.bfloat16)
    with_v = (query_rows.astype(jnp.float32) + bias_second).astype(jnp.bfloat16)

    def one_block(carried, block_index):
        grad_key, grad_value, grad_place = carried
        first_row = block_index * block_rows
        place_first = length - block_rows - first_row
        block_u = lax.dynamic_slice_in_dim(with_u, first_row, block_rows, 0)
        block_v = lax.dynamic_slice_in_dim(with_v, first_row, block_rows, 0)
        near_rows = lax.dynamic_slice_in_dim(place_rows, place_first, span, 0)
        block_total = lax.dynamic_slice_in_dim(log_total, first_row, block_rows, 0)
        block_grad = lax.dynamic_slice_in_dim(grad_mixed, first_row, block_rows, 0)
        scores = (
            mult_trans(block_u, key_rows) + skew_rows(mult_trans(block_v, near_rows))
        ) * score_scale
        scores = jnp.where(key_ok[None, :], scores, MASKED_SCORE)
        attend_prob = jnp.exp(scores - block_total[:, None])
        grad_prob = mult_trans(block_grad, value_rows)
        inner = jnp.sum(attend_prob * grad_prob, axis=1, keepdims=True)
        grad_score = jnp.where(key_ok[None, :], attend_prob * (grad_prob - inner), 0.0).astype(
            jnp.bfloat16
        )
        grad_value = grad_value + mult_rows(attend_prob.astype(jnp.bfloat16), block_grad)
        grad_with_u = mult_plain(grad_score, key_rows) * score_scale
        grad_key = grad_key + mult_rows(grad_score, block_u) * score_scale
        spread_grad = unskew_rows(grad_score, span)
        grad_with_v = mult_plain(spread_grad, near_rows) * score_scale
        place_part = (
            lax.dynamic_slice_in_dim(grad_place, place_first, span, 0)
            + mult_rows(spread_grad, block_v) * score_scale
        )
        grad_place = lax.dynamic_update_slice_in_dim(grad_place, place_part, place_first, 0)
        return ((grad_key, grad_value, grad_place), (grad_with_u, grad_with_v))

    zero_rows = jnp.zeros((length, head_width), jnp.float32)
    zero_place = jnp.zeros((2 * length - 1, head_width), jnp.float32)
    (grad_key, grad_value, grad_place), (grad_with_u, grad_with_v) = lax.scan(
        one_block,
        (zero_rows, zero_rows, zero_place),
        jnp.arange(length // block_rows, dtype=jnp.int32),
    )
    grad_with_u = grad_with_u.reshape(length, head_width)
    grad_with_v = grad_with_v.reshape(length, head_width)
    grad_query = (grad_with_u + grad_with_v).astype(jnp.bfloat16)
    return (
        grad_query,
        grad_key.astype(jnp.bfloat16),
        grad_value.astype(jnp.bfloat16),
        grad_place.astype(jnp.bfloat16),
        jnp.sum(grad_with_u, axis=0),
        jnp.sum(grad_with_v, axis=0),
    )


def biased(q_ref, bias_ref, scale):
    return ((q_ref[...].astype(jnp.float32) + bias_ref[...].astype(jnp.float32)).astype(jnp.bfloat16).astype(jnp.float32) * scale).astype(jnp.bfloat16)

def attend_fwd_kernel(len_ref, q_ref, k_ref, v_ref, place_ref, cb_ref, pb_ref, out_ref, prob_ref, *, scale):
    rows = q_ref.shape[0]
    length = k_ref.shape[0]
    span = rows + length
    first = pl.multiple_of(length - rows - pl.program_id(1) * rows, rows)
    lanes = lax.broadcasted_iota(jnp.int32, (rows, PAIR), 1)
    with_u = biased(q_ref, cb_ref, scale)
    with_v = biased(q_ref, pb_ref, scale)
    window = place_ref[pl.ds(first, span), :]
    key_ok = lax.broadcasted_iota(jnp.int32, (rows, length), 1) < len_ref[0]
    zero = jnp.zeros_like(with_u)
    mixed = []
    for head in range(2):
        mine = (lanes // HEAD_DIM) == head
        place_part = mult_trans(jnp.where(mine, with_v, zero), window)
        place_part = pltpu.roll(place_part, span - rows + 1, 1, stride=1, stride_axis=0)
        scores = mult_trans(jnp.where(mine, with_u, zero), k_ref[...]) + place_part[:, :length]
        scores = jnp.where(key_ok, scores, MASKED_SCORE)
        weights = jnp.exp(scores - jnp.max(scores, axis=1, keepdims=True))
        total = jnp.sum(weights, axis=1, keepdims=True)
        prob = (weights * (1.0 / total)).astype(jnp.bfloat16)
        prob_ref[head] = prob
        mixed.append(mult_plain(prob, v_ref[...]))
    out_ref[...] = jnp.where(lanes < HEAD_DIM, mixed[0], mixed[1]).astype(jnp.bfloat16)

def attend_fwd(length_arr, q, k, v, place, cb, pb, rows):
    length, width = q.shape
    pairs = width // PAIR
    return pl.pallas_call(
        partial(attend_fwd_kernel, scale=1.0 / math.sqrt(HEAD_DIM)),
        grid=(pairs, length // rows),
        in_specs=[
            pl.BlockSpec(memory_space=pltpu.SMEM),
            pl.BlockSpec((rows, PAIR), lambda p, i: (i, p)),
            pl.BlockSpec((length, PAIR), lambda p, i: (0, p)),
            pl.BlockSpec((length, PAIR), lambda p, i: (0, p)),
            pl.BlockSpec((2 * length, PAIR), lambda p, i: (0, p)),
            pl.BlockSpec((1, PAIR), lambda p, i: (0, p)),
            pl.BlockSpec((1, PAIR), lambda p, i: (0, p)),
        ],
        out_specs=[
            pl.BlockSpec((rows, PAIR), lambda p, i: (i, p)),
            pl.BlockSpec((2, rows, length), lambda p, i: (p, i, 0)),
        ],
        out_shape=[
            jax.ShapeDtypeStruct((length, width), jnp.bfloat16),
            jax.ShapeDtypeStruct((2 * pairs, length, length), jnp.bfloat16),
        ],
        compiler_params=pltpu.CompilerParams(vmem_limit_bytes=VMEM),
        cost_estimate=pl.CostEstimate(flops=40 * 10**9, bytes_accessed=20 * 2**20, transcendentals=pairs * 2 * length * length),
        name="attend_fwd",
    )(length_arr, q, k, v, place, cb, pb)

def attend_bwd_kernel(q_ref, k_ref, v_ref, place_ref, cb_ref, pb_ref, prob_ref, g_ref, gq_ref, gk_ref, gv_ref, gp_ref, gb_ref, gk_s, gv_s, gp_s, *, scale, trans):
    rows = q_ref.shape[0]
    length = k_ref.shape[0]
    span = rows + length
    step = pl.program_id(1)
    first = pl.multiple_of(length - rows - step * rows, rows)
    lanes = lax.broadcasted_iota(jnp.int32, (rows, PAIR), 1)
    flip = (lax.broadcasted_iota(jnp.int32, (rows, rows), 0) + lax.broadcasted_iota(jnp.int32, (rows, rows), 1) == rows - 1).astype(jnp.bfloat16)
    with_u = biased(q_ref, cb_ref, scale)
    with_v = mult_plain(flip, biased(q_ref, pb_ref, scale)).astype(jnp.bfloat16)
    grad = g_ref[...]
    window = place_ref[pl.ds(first, span), :]
    zero = jnp.zeros_like(with_u)

    @pl.when(step == 0)
    def _():
        gk_s[...] = jnp.zeros_like(gk_s)
        gv_s[...] = jnp.zeros_like(gv_s)
        gp_s[...] = jnp.zeros_like(gp_s)
        gb_ref[...] = jnp.zeros_like(gb_ref)

    if trans:
        grad_t, with_u_t, with_v_t = grad.T, with_u.T, with_v.T
    gu = []
    gw = []
    for head in range(2):
        mine = (lanes // HEAD_DIM) == head
        prob = prob_ref[head]
        grad_h = jnp.where(mine, grad, zero)
        grad_prob = mult_trans(grad_h, v_ref[...])
        weighted = prob.astype(jnp.float32) * grad_prob
        inner = jnp.sum(weighted, axis=1, keepdims=True)
        grad_score = (weighted - prob.astype(jnp.float32) * inner).astype(jnp.bfloat16)
        turned = mult_plain(flip, grad_score).astype(jnp.bfloat16)
        turned = jnp.concatenate([turned, jnp.zeros((rows, rows), jnp.bfloat16)], axis=1)
        turned = pltpu.roll(turned, 0, 1, stride=1, stride_axis=0)
        gu.append(mult_plain(grad_score, k_ref[...]))
        gw.append(mult_plain(turned, window))
        if trans:
            band = slice(head * HEAD_DIM, (head + 1) * HEAD_DIM)
            gv_s[band, :] += mult_plain(grad_t[band, :], prob)
            gk_s[band, :] += mult_plain(with_u_t[band, :], grad_score)
            gp_s[band, pl.ds(first, span)] += mult_plain(with_v_t[band, :], turned)
        else:
            gv_s[...] += mult_rows(prob, grad_h)
            gk_s[...] += mult_rows(grad_score, jnp.where(mine, with_u, zero))
            gp_s[pl.ds(first, span), :] += mult_rows(turned, jnp.where(mine, with_v, zero))
    grad_u = jnp.where(lanes < HEAD_DIM, gu[0], gu[1]) * scale
    grad_w = jnp.where(lanes < HEAD_DIM, gw[0], gw[1]) * scale
    gb_ref[0:1, :] += jnp.sum(grad_u, axis=0, keepdims=True)
    gb_ref[1:2, :] += jnp.sum(grad_w, axis=0, keepdims=True)
    high = grad_w.astype(jnp.bfloat16)
    rest = (grad_w - high.astype(jnp.float32)).astype(jnp.bfloat16)
    gq_ref[...] = (grad_u + mult_plain(flip, high) + mult_plain(flip, rest)).astype(jnp.bfloat16)

    @pl.when(step == pl.num_programs(1) - 1)
    def _():
        if trans:
            gk_ref[...] = gk_s[...].T.astype(jnp.bfloat16)
            gv_ref[...] = gv_s[...].T.astype(jnp.bfloat16)
            gp_ref[...] = gp_s[...].T.astype(jnp.bfloat16)
        else:
            gk_ref[...] = gk_s[...].astype(jnp.bfloat16)
            gv_ref[...] = gv_s[...].astype(jnp.bfloat16)
            gp_ref[...] = gp_s[...].astype(jnp.bfloat16)

def attend_bwd(q, k, v, place, cb, pb, prob, grad, rows, trans=True):
    length, width = q.shape
    pairs = width // PAIR
    full = pl.BlockSpec((length, PAIR), lambda p, i: (0, p))
    part = pl.BlockSpec((rows, PAIR), lambda p, i: (i, p))
    vec = pl.BlockSpec((1, PAIR), lambda p, i: (0, p))
    tall = pl.BlockSpec((2 * length, PAIR), lambda p, i: (0, p))
    shape = (lambda n: (PAIR, n)) if trans else (lambda n: (n, PAIR))
    return pl.pallas_call(
        partial(attend_bwd_kernel, scale=1.0 / math.sqrt(HEAD_DIM), trans=trans),
        grid=(pairs, length // rows),
        in_specs=[part, full, full, tall, vec, vec, pl.BlockSpec((2, rows, length), lambda p, i: (p, i, 0)), part],
        out_specs=[part, full, full, tall, pl.BlockSpec((8, PAIR), lambda p, i: (0, p))],
        out_shape=[
            jax.ShapeDtypeStruct((length, width), jnp.bfloat16),
            jax.ShapeDtypeStruct((length, width), jnp.bfloat16),
            jax.ShapeDtypeStruct((length, width), jnp.bfloat16),
            jax.ShapeDtypeStruct((2 * length, width), jnp.bfloat16),
            jax.ShapeDtypeStruct((8, width), jnp.float32),
        ],
        scratch_shapes=[
            pltpu.VMEM(shape(length), jnp.float32),
            pltpu.VMEM(shape(length), jnp.float32),
            pltpu.VMEM(shape(2 * length), jnp.float32),
        ],
        compiler_params=pltpu.CompilerParams(vmem_limit_bytes=VMEM),
        cost_estimate=pl.CostEstimate(flops=80 * 10**9, bytes_accessed=20 * 2**20, transcendentals=0),
        name="attend_bwd",
    )(q, k, v, place, cb, pb, prob, grad)


class Hops:
    def __init__(self, layers):
        self.layers = layers

    def send(self, block, dz=0, dc=0, dy=0, dx=0):
        pairs = []
        for z in range(self.layers):
            for c in range(2):
                for w in range(4):
                    to = ((z + dz) % self.layers * 2 + (c ^ dc)) * 4 + (w ^ (2 * dy + dx))
                    pairs.append(((z * 2 + c) * 4 + w, to))
        return lax.ppermute(block, ("utt", "wide"), pairs)

    def turn(self, block, step):
        pairs = []
        for z in range(self.layers):
            for c in range(2):
                for w in range(4):
                    to = (z * 2 + w // 2) * 4 + 2 * c + ((w % 2) ^ step)
                    pairs.append(((z * 2 + c) * 4 + w, to))
        return lax.ppermute(block, ("utt", "wide"), pairs)

    def gather_rows(self, chunk):
        half = self.layers // 2
        along = [chunk] + [self.send(chunk, dz=k) for k in range(1, self.layers)]
        low = jnp.concatenate(along[:half])
        high = jnp.concatenate(along[half:])
        low_y = self.send(low, dy=1)
        high_x = self.send(high, dx=1)
        near = [low, low_y, high, high_x]
        far = [
            self.send(low, dx=1),
            self.send(low_y, dx=1),
            self.send(high, dy=1),
            self.send(high_x, dy=1),
        ]
        mine = near + far
        return mine + [self.send(block, dc=1) for block in mine]

    def reduce_rows(self, own, other):
        swapped = self.send(other(), dc=1)
        total = own(swapped)
        size = total.shape[0] // 8
        part = lambda block, at, count=1: lax.slice_in_dim(block, at * size, (at + count) * size)
        plus = lambda a, b: (a.astype(jnp.float32) + b.astype(jnp.float32)).astype(jnp.bfloat16)
        low_far = self.send(part(total, 4, 2), dx=1)
        high_far = self.send(part(total, 6, 2), dy=1)
        low = plus(part(total, 0, 2), low_far)
        high = plus(part(total, 2, 2), high_far)
        low_y = self.send(part(low, 1), dy=1)
        high_x = self.send(part(high, 1), dx=1)
        both = jnp.concatenate([plus(part(low, 0), low_y), plus(part(high, 0), high_x)])
        return self.reduce_layers(both)

    def reduce_layers(self, block):
        size = block.shape[0] // self.layers
        result = block[:size].astype(jnp.float32)
        for k in range(1, self.layers):
            result = result + self.send(block[k * size : (k + 1) * size], dz=-k).astype(jnp.float32)
        return result

    def gather_plane(self, first, second):
        first_x = self.send(first, dx=1)
        second_y = self.send(second, dy=1)
        return (
            [first, first_x, self.send(first, dy=1), self.send(first_x, dy=1)],
            [second, self.send(second, dx=1), second_y, self.send(second_y, dx=1)],
        )

    def reduce_plane(self, first, second):
        plus = lambda a, b: (a.astype(jnp.float32) + b.astype(jnp.float32)).astype(jnp.bfloat16)
        first_got = self.send(jnp.concatenate(first[2:]), dy=1)
        second_got = self.send(jnp.concatenate([second[1], second[3]]), dx=1)
        rows = first[0].shape[0]
        first_own = plus(first[0], first_got[:rows])
        first_x = plus(first[1], first_got[rows:])
        rows = second[0].shape[0]
        second_own = plus(second[0], second_got[:rows])
        second_y = plus(second[2], second_got[rows:])
        return (
            plus(first_own, self.send(first_x, dx=1)),
            plus(second_own, self.send(second_y, dy=1)),
        )

    def sum_layers(self, block):
        z = lax.axis_index("utt") // 2
        size = block.shape[0] // self.layers
        piece = lambda k: lax.dynamic_slice_in_dim(block, (z + k) % self.layers * size, size)
        total = piece(0).astype(jnp.float32)
        for k in range(1, self.layers):
            total = total + self.send(piece(k), dz=k).astype(jnp.float32)
        total = total.astype(jnp.bfloat16)
        result = jnp.zeros(block.shape, jnp.bfloat16)
        for k in range(self.layers):
            got = total if k == 0 else self.send(total, dz=k)
            result = lax.dynamic_update_slice_in_dim(result, got, (z - k) % self.layers * size, 0)
        return result


def taps_forward(padded, kernel_f, count):
    total = jnp.zeros((count, padded.shape[1]), jnp.float32)
    for offset in range(KERNEL):
        total = total + padded[offset : offset + count] * kernel_f[offset]
    return total


def with_rim(hops, block, core):
    edge = jnp.where(core == 0, block[-16:], block[:16])
    got = hops.send(edge, dc=1)
    zero = jnp.zeros_like(got)
    low = jnp.where(core == 0, zero, got)[1:]
    high = jnp.where(core == 0, got, zero)[:RIM]
    return jnp.concatenate([low, block, high])


def per_chip(
    frames,
    lengths,
    masked,
    cotangent,
    first_gain,
    first_up,
    first_down,
    attn_gain,
    query_weight,
    key_weight,
    value_weight,
    out_weight,
    place_weight,
    content_bias,
    place_bias,
    conv_gain,
    glu_weight,
    depth_kernel,
    middle_gain,
    point_weight,
    second_gain,
    second_up,
    second_down,
    final_gain,
):
    utt_at, wide_at = lax.axis_index("utt"), lax.axis_index("wide")
    core, y, x = utt_at % 2, wide_at // 2, wide_at % 2
    hops = Hops(lax.axis_size("utt") // 2)
    groups, quarter, channels = frames.shape
    rows = groups * quarter
    length = 2 * rows
    f32 = lambda v: v.astype(jnp.float32)
    low = lambda v: v.astype(jnp.bfloat16)

    def pick(flag, one, two):
        return jnp.where(flag, one, two), jnp.where(flag, two, one)

    def turn_in(block):
        swap = [lax.dynamic_index_in_dim(block, x ^ step, 0, keepdims=False) for step in range(2)]
        got = [hops.turn(swap[step], step) for step in range(2)]
        return jnp.concatenate(pick(x == 0, *got))

    def turn_out(block):
        parts = pick(x == 0, block[:quarter], block[quarter:])
        got = [hops.turn(parts[step], step) for step in range(2)]
        return jnp.stack(pick(x == 0, *got))

    frames_own = turn_in(frames)
    first_pieces = hops.gather_rows(first_up)
    first_pieces_down = hops.gather_rows(first_down)
    positions = wide_at * quarter + jnp.arange(quarter, dtype=jnp.int32)
    seed_weight = f32(masked) * f32(positions[None, :] < lengths[:, None])
    seed_own_low = low(f32(cotangent) * seed_weight[:, :, None])
    all_lengths = lax.all_gather(lengths, "utt", axis=0, tiled=True)
    own_length = lax.dynamic_slice_in_dim(all_lengths, utt_at // 2 * 4 + wide_at, 1)
    own_rows = core * rows + jnp.arange(rows, dtype=jnp.int32)
    frame_ok = f32(own_rows < own_length[0])[:, None]

    def own_half(weight):
        count = weight.shape[0] // 2
        return lax.dynamic_slice_in_dim(weight, core * count, count)

    band = query_weight.shape[0] // 2
    qk_pieces, vp_pieces = hops.gather_plane(
        jnp.concatenate([own_half(query_weight), own_half(key_weight)]),
        jnp.concatenate([own_half(value_weight), own_half(place_weight)]),
    )
    query_own = jnp.concatenate([piece[:band] for piece in qk_pieces])
    key_own = jnp.concatenate([piece[band:] for piece in qk_pieces])
    value_own = jnp.concatenate([piece[:band] for piece in vp_pieces])
    place_own = jnp.concatenate([piece[band:] for piece in vp_pieces])
    op_pieces, glu_pieces = hops.gather_plane(
        jnp.concatenate([own_half(out_weight), own_half(point_weight)]),
        own_half(glu_weight),
    )
    op_both = op_pieces + [hops.send(piece, dc=1) for piece in op_pieces]
    glu_both = glu_pieces + [hops.send(piece, dc=1) for piece in glu_pieces]
    here = wide_at * 2 + core
    place_at = [((piece % 4) * 2 + piece // 4) ^ here for piece in range(8)]

    def in_order(pieces):
        size = pieces[0].shape[0]
        result = jnp.zeros((8 * size, channels), jnp.bfloat16)
        for piece, at in zip(pieces, place_at):
            result = lax.dynamic_update_slice_in_dim(result, piece, at * size, 0)
        return result

    def by_piece(matrix):
        size = matrix.shape[0] // 8
        return [lax.dynamic_slice_in_dim(matrix, at * size, size) for at in place_at]

    full_out = jnp.concatenate([piece[:band] for piece in op_both])
    full_point = in_order([piece[band:] for piece in op_both])
    full_glu = in_order(glu_both)

    biases = jnp.stack([content_bias, place_bias])
    all_biases = lax.all_gather(biases, "wide", axis=1, tiled=True)
    pair_at = [((piece * 2) ^ (wide_at * 2)) + core for piece in range(4)]
    own_biases = jnp.concatenate(
        [lax.dynamic_slice_in_dim(all_biases, at * band, band, 1) for at in pair_at], axis=1
    )

    stream0 = f32(frames_own)
    up_first, down_first = jnp.concatenate(first_pieces), jnp.concatenate(first_pieces_down)
    stream1, saved_first = ffn_forward(stream0, f32(first_gain), up_first, down_first)
    normed_attn, attn_pull = jax.vjp(norm_rows, stream1, f32(attn_gain))
    attn_half = low(normed_attn)
    attn_other = hops.send(attn_half, dc=1)
    attn_low = jnp.concatenate(pick(core == 0, attn_half, attn_other))
    rel_table = low(relative_table(length, channels))
    rel_table = jnp.concatenate([rel_table, jnp.zeros((1, channels), jnp.bfloat16)])
    query = low(mult_trans(attn_low, query_own))
    key = low(mult_trans(attn_low, key_own))
    value = low(mult_trans(attn_low, value_own))
    place = low(mult_trans(rel_table, place_own))
    attended, prob = attend_fwd(
        own_length, query, key, value, place, own_biases[:1], own_biases[1:], ROWS_FWD
    )

    def halves(matrix):
        own = lax.dynamic_slice_in_dim(matrix, core * rows, rows)
        other = lax.dynamic_slice_in_dim(matrix, (1 - core) * rows, rows)
        return own, other

    att_own, att_other = halves(attended)
    framed = jnp.concatenate([att_own, hops.send(att_other, dc=1)], axis=1)
    stream2 = stream1 + mult_plain(framed, full_out)
    normed_conv, conv_pull = jax.vjp(norm_rows, stream2, f32(conv_gain))
    conv_low = low(normed_conv)
    glu_in = mult_trans(conv_low, full_glu)
    linear = glu_in[:, :channels]
    gating = jax.nn.sigmoid(glu_in[:, channels:])
    gated = low(linear * gating * frame_ok)
    padded = with_rim(hops, gated, core)
    kernel_f = f32(depth_kernel)
    conv_out = taps_forward(padded, kernel_f, rows)
    middle, middle_pull = jax.vjp(norm_rows, conv_out, f32(middle_gain))
    swished = low(jax.nn.silu(middle))
    stream3 = stream2 + mult_trans(swished, full_point)
    up_second = jnp.concatenate(hops.gather_rows(second_up))
    down_second = jnp.concatenate(hops.gather_rows(second_down))
    stream4, saved_second = ffn_forward(stream3, f32(second_gain), up_second, down_second)
    final_rows, final_pull = jax.vjp(norm_rows, stream4, f32(final_gain))
    output = turn_out(low(final_rows))

    seed_own = turn_in(seed_own_low)
    grad4, grad_final_gain = final_pull(f32(seed_own))

    def ffn_back(grad_stream, saved_ffn, up_full, down_full):
        norm_pull, normed_low, before, active_low = saved_ffn
        grad_out = low(0.5 * grad_stream)
        side = active_low.shape[1] // 2

        def reduced(left, right):
            def half(at):
                return mult_rows(lax.slice_in_dim(left, at * side, (at + 1) * side, axis=1), right)

            return hops.reduce_rows(
                lambda got: low(half(0) + f32(got)), lambda: low(half(1))
            )

        sum_down = reduced(active_low, grad_out)
        grad_before = low(mult_trans(grad_out, down_full) * silu_slope(before))
        sum_up = reduced(grad_before, normed_low)
        grad_input, grad_gain = norm_pull(mult_plain(grad_before, up_full))
        return grad_stream + grad_input, grad_gain, sum_up, sum_down

    grad3, grad_second_gain, sum_up_second, sum_down_second = ffn_back(
        grad4, saved_second, up_second, down_second
    )
    grad_branch = low(grad3)
    grad_point = mult_rows(grad_branch, swished)
    grad_middle = mult_plain(grad_branch, full_point) * silu_slope(middle)
    grad_conv, grad_middle_gain = middle_pull(grad_middle)
    conv_grad_low = low(grad_conv)
    grad_padded = with_rim(hops, conv_grad_low, core)
    grad_gated = taps_forward(grad_padded, kernel_f[::-1], rows)
    grad_kernel = jnp.stack(
        [
            jnp.sum(f32(padded[offset : offset + rows]) * f32(conv_grad_low), axis=0)
            for offset in range(KERNEL)
        ]
    )
    grad_gated = grad_gated * frame_ok
    grad_glu_in = low(
        jnp.concatenate(
            [grad_gated * gating, grad_gated * linear * gating * (1.0 - gating)], axis=1
        )
    )
    grad_glu = mult_rows(grad_glu_in, conv_low)
    grad_conv_in, grad_conv_gain = conv_pull(mult_plain(grad_glu_in, full_glu))
    grad2 = grad3 + grad_conv_in
    grad_attn = low(grad2)
    grad_out = mult_rows(framed, grad_attn)
    grad_framed = low(mult_trans(grad_attn, full_out))
    side = channels // 2
    grad_heads = jnp.concatenate(
        pick(core == 0, grad_framed[:, :side], hops.send(grad_framed[:, side:], dc=1))
    )
    grad_query, grad_key, grad_value, grad_place, grad_biases = attend_bwd(
        query, key, value, place, own_biases[:1], own_biases[1:], prob, grad_heads, ROWS_BWD
    )
    grad_query_w = mult_rows(grad_query, attn_low)
    grad_key_w = mult_rows(grad_key, attn_low)
    grad_value_w = mult_rows(grad_value, attn_low)
    grad_place_w = mult_rows(grad_place, rel_table)
    grad_normed = (
        mult_plain(grad_query, query_own)
        + mult_plain(grad_key, key_own)
        + mult_plain(grad_value, value_own)
    )
    normed_own, normed_other = halves(grad_normed)
    grad_attn_in, grad_attn_gain = attn_pull(normed_own + f32(hops.send(low(normed_other), dc=1)))
    grad1 = grad2 + grad_attn_in
    grad0, grad_first_gain, sum_up_first, sum_down_first = ffn_back(
        grad1, saved_first, up_first, down_first
    )
    grad_input = turn_out(low(grad0))

    def split4(matrix):
        size = matrix.shape[0] // 4
        return [matrix[at * size : (at + 1) * size] for at in range(4)]

    def joined(*lists):
        return [jnp.concatenate([low(part) for part in parts]) for parts in zip(*lists)]

    out_size = band
    out_pieces = [grad_out[at * out_size : (at + 1) * out_size] for at in range(8)]
    point_pieces, glu_parts = by_piece(grad_point), by_piece(grad_glu)
    sent = joined(out_pieces[4:], point_pieces[4:], glu_parts[4:])
    kept = joined(out_pieces[:4], point_pieces[:4], glu_parts[:4])
    got = hops.send(jnp.concatenate(sent), dc=1)
    summed = split4(low(f32(jnp.concatenate(kept)) + f32(got)))
    op_sum, glu_sum = hops.reduce_plane(
        [part[: 2 * band] for part in summed], [part[2 * band :] for part in summed]
    )
    op_glu = hops.sum_layers(jnp.concatenate([op_sum, glu_sum]))
    qk_sum, vp_sum = hops.reduce_plane(
        joined(split4(grad_query_w), split4(grad_key_w)),
        joined(split4(grad_value_w), split4(grad_place_w)),
    )
    qkvp = hops.sum_layers(jnp.concatenate([qk_sum, vp_sum]))
    both_core = [jnp.concatenate([op_glu, qkvp])]
    both_core.append(hops.send(both_core[0], dc=1))

    def owned(start, count):
        parts = [part[start : start + count] for part in both_core]
        return f32(jnp.concatenate(pick(core == 0, *parts)))

    total_out, total_point = owned(0, band), owned(band, band)
    total_glu = owned(2 * band, 2 * band)
    total_query, total_key = owned(4 * band, band), owned(5 * band, band)
    total_value, total_place = owned(6 * band, band), owned(7 * band, band)

    spread = jnp.zeros((2, channels), jnp.float32)
    for piece, at in enumerate(pair_at):
        spread = lax.dynamic_update_slice(
            spread, grad_biases[:2, piece * band : (piece + 1) * band], (0, at * band)
        )
    small = lax.psum(
        jnp.concatenate(
            [
                grad_first_gain[None],
                grad_attn_gain[None],
                grad_conv_gain[None],
                grad_middle_gain[None],
                grad_second_gain[None],
                grad_final_gain[None],
                spread,
                grad_kernel,
            ]
        ),
        ("utt", "wide"),
    )
    own_bias = lax.dynamic_slice_in_dim(small[6:8], wide_at * 2 * band, 2 * band, 1)
    return (
        output,
        grad_input,
        small[0],
        sum_up_first,
        sum_down_first,
        small[1],
        total_query,
        total_key,
        total_value,
        total_out,
        total_place,
        own_bias[0],
        own_bias[1],
        small[2],
        total_glu,
        small[8:],
        small[3],
        total_point,
        small[4],
        sum_up_second,
        sum_down_second,
        small[5],
    )


def per_device(
    frames,
    lengths,
    masked,
    cotangent,
    first_gain,
    first_up,
    first_down,
    attn_gain,
    query_weight,
    key_weight,
    value_weight,
    out_weight,
    place_weight,
    content_bias,
    place_bias,
    conv_gain,
    glu_weight,
    depth_kernel,
    middle_gain,
    point_weight,
    second_gain,
    second_up,
    second_down,
    final_gain,
):
    groups, frames_dev, channels = frames.shape
    row_count = groups * frames_dev
    length = frames_dev * lax.axis_size("wide")
    score_scale = 1.0 / math.sqrt(HEAD_DIM)
    positions = lax.axis_index("wide") * frames_dev + jnp.arange(frames_dev, dtype=jnp.int32)
    frame_grid = (positions[None, :] < lengths[:, None]).astype(jnp.float32)
    frame_ok = frame_grid.reshape(row_count, 1)
    key_ok = jnp.arange(length, dtype=jnp.int32)[None, :] < lengths[:, None]
    stream0 = frames.reshape(row_count, channels).astype(jnp.float32)
    up_first, down_first = gather_ffn(first_up, first_down)
    stream1, saved_first = ffn_forward(
        stream0, first_gain.astype(jnp.float32), up_first, down_first
    )
    full_query, full_key, full_value, full_out, full_glu, full_point = (
        lax.all_gather(query_weight, "wide", axis=0, tiled=True),
        lax.all_gather(key_weight, "wide", axis=0, tiled=True),
        lax.all_gather(value_weight, "wide", axis=0, tiled=True),
        lax.all_gather(out_weight, "wide", axis=0, tiled=True),
        lax.all_gather(glu_weight, "wide", axis=0, tiled=True),
        lax.all_gather(point_weight, "wide", axis=0, tiled=True),
    )
    normed_attn, attn_pull = jax.vjp(norm_rows, stream1, attn_gain.astype(jnp.float32))
    attn_low = normed_attn.astype(jnp.bfloat16)
    query_frames = (
        mult_trans(attn_low, full_query).astype(jnp.bfloat16).reshape(groups, frames_dev, -1)
    )
    key_frames = mult_trans(attn_low, full_key).astype(jnp.bfloat16).reshape(groups, frames_dev, -1)
    value_frames = (
        mult_trans(attn_low, full_value).astype(jnp.bfloat16).reshape(groups, frames_dev, -1)
    )
    heads_query, heads_key, heads_value = (
        lax.all_to_all(query_frames, "wide", split_axis=2, concat_axis=1, tiled=True),
        lax.all_to_all(key_frames, "wide", split_axis=2, concat_axis=1, tiled=True),
        lax.all_to_all(value_frames, "wide", split_axis=2, concat_axis=1, tiled=True),
    )
    local_width = heads_query.shape[2]
    head_count = local_width // HEAD_DIM
    rel_table = relative_table(length, channels).astype(jnp.bfloat16)
    place_rows = (
        mult_trans(rel_table, place_weight)
        .astype(jnp.bfloat16)
        .reshape(2 * length - 1, head_count, HEAD_DIM)
    )
    bias_first = content_bias.astype(jnp.float32).reshape(head_count, HEAD_DIM)
    bias_second = place_bias.astype(jnp.float32).reshape(head_count, HEAD_DIM)
    split_query = heads_query.reshape(groups, length, head_count, HEAD_DIM)
    split_key = heads_key.reshape(groups, length, head_count, HEAD_DIM)
    split_value = heads_value.reshape(groups, length, head_count, HEAD_DIM)
    forward_heads = jax.vmap(
        partial(head_forward, block_rows=QBLK, score_scale=score_scale),
        in_axes=(1, 1, 1, 1, 0, 0, None),
        out_axes=(1, 0),
    )

    def attend_utt(unit_items):
        return forward_heads(
            unit_items[0],
            unit_items[1],
            unit_items[2],
            place_rows,
            bias_first,
            bias_second,
            unit_items[3],
        )

    attended, log_total = lax.map(attend_utt, (split_query, split_key, split_value, key_ok))
    framed = lax.all_to_all(
        attended.reshape(groups, length, local_width),
        "wide",
        split_axis=1,
        concat_axis=2,
        tiled=True,
    ).reshape(row_count, -1)
    stream2 = stream1 + mult_plain(framed, full_out)
    normed_conv, conv_pull = jax.vjp(norm_rows, stream2, conv_gain.astype(jnp.float32))
    conv_low = normed_conv.astype(jnp.bfloat16)
    glu_in = mult_trans(conv_low, full_glu)
    linear = glu_in[:, :channels]
    gating = jax.nn.sigmoid(glu_in[:, channels:])
    gated = (linear * gating * frame_ok).astype(jnp.bfloat16).reshape(groups, frames_dev, channels)
    padded = with_halo(gated, (("wide", 1),), RIM)
    kernel_f = depth_kernel.astype(jnp.float32)
    conv_out = jnp.zeros((groups, frames_dev, channels), jnp.float32)
    for offset in range(KERNEL):
        conv_out = conv_out + padded[:, offset : offset + frames_dev, :] * kernel_f[offset]
    conv_out = conv_out.reshape(row_count, channels)
    middle, middle_pull = jax.vjp(norm_rows, conv_out, middle_gain.astype(jnp.float32))
    swished = jax.nn.silu(middle).astype(jnp.bfloat16)
    stream3 = stream2 + mult_trans(swished, full_point)
    up_second, down_second = gather_ffn(second_up, second_down)
    stream4, saved_second = ffn_forward(
        stream3, second_gain.astype(jnp.float32), up_second, down_second
    )
    final_rows, final_pull = jax.vjp(norm_rows, stream4, final_gain.astype(jnp.float32))
    output = final_rows.astype(jnp.bfloat16).reshape(groups, frames_dev, channels)
    seed_weight = (masked.astype(jnp.float32) * frame_grid).reshape(row_count, 1)
    seed_grad = cotangent.reshape(row_count, channels).astype(jnp.float32) * seed_weight
    grad4, grad_final_gain = final_pull(seed_grad)
    back_up_second, back_down_second = gather_ffn(second_up, second_down)
    grad3, grad_second_gain, grad_up_second, grad_down_second = ffn_backward(
        grad4, saved_second, back_up_second, back_down_second
    )
    summed_second = sum_ffn(grad_up_second, grad_down_second)
    grad_branch = grad3.astype(jnp.bfloat16)
    grad_point = mult_rows(grad_branch, swished)
    grad_middle = mult_plain(grad_branch, full_point) * silu_slope(middle)
    grad_conv, grad_middle_gain = middle_pull(grad_middle)
    conv_grad_low = grad_conv.astype(jnp.bfloat16).reshape(groups, frames_dev, channels)
    grad_padded = with_halo(conv_grad_low, (("wide", 1),), RIM)
    grad_gated = jnp.zeros((groups, frames_dev, channels), jnp.float32)
    kernel_rows = []
    for offset in range(KERNEL):
        grad_gated = (
            grad_gated
            + grad_padded[:, 2 * RIM - offset : 2 * RIM - offset + frames_dev, :] * kernel_f[offset]
        )
        kernel_rows.append(
            jnp.einsum(
                "rzn,rzn->n",
                padded[:, offset : offset + frames_dev, :],
                conv_grad_low,
                preferred_element_type=jnp.float32,
            )
        )
    grad_kernel = jnp.stack(kernel_rows)
    grad_gated = grad_gated.reshape(row_count, channels) * frame_ok
    grad_glu_in = jnp.concatenate(
        [grad_gated * gating, grad_gated * linear * gating * (1.0 - gating)], axis=1
    ).astype(jnp.bfloat16)
    grad_glu = mult_rows(grad_glu_in, conv_low)
    grad_conv_in, grad_conv_gain = conv_pull(mult_plain(grad_glu_in, full_glu))
    grad2 = grad3 + grad_conv_in
    grad_attn = grad2.astype(jnp.bfloat16)
    grad_out = mult_rows(framed, grad_attn)
    grad_framed = (
        mult_trans(grad_attn, full_out).astype(jnp.bfloat16).reshape(groups, frames_dev, -1)
    )
    grad_heads = lax.all_to_all(grad_framed, "wide", split_axis=2, concat_axis=1, tiled=True)
    backward_heads = jax.vmap(
        partial(head_backward, block_rows=QBLK, score_scale=score_scale),
        in_axes=(1, 1, 1, 1, 0, 0, None, 0, 1),
        out_axes=(1, 1, 1, 1, 0, 0),
    )

    def attend_back(unit_items):
        return backward_heads(
            unit_items[0],
            unit_items[1],
            unit_items[2],
            place_rows,
            bias_first,
            bias_second,
            unit_items[3],
            unit_items[4],
            unit_items[5],
        )

    grad_query_h, grad_key_h, grad_value_h, grad_place_h, grad_bias_first, grad_bias_second = (
        lax.map(
            attend_back,
            (
                split_query,
                split_key,
                split_value,
                key_ok,
                log_total,
                grad_heads.reshape(groups, length, head_count, HEAD_DIM),
            ),
        )
    )
    back_query, back_key, back_value = (
        lax.all_to_all(
            grad_query_h.reshape(groups, length, local_width),
            "wide",
            split_axis=1,
            concat_axis=2,
            tiled=True,
        ),
        lax.all_to_all(
            grad_key_h.reshape(groups, length, local_width),
            "wide",
            split_axis=1,
            concat_axis=2,
            tiled=True,
        ),
        lax.all_to_all(
            grad_value_h.reshape(groups, length, local_width),
            "wide",
            split_axis=1,
            concat_axis=2,
            tiled=True,
        ),
    )
    back_query = back_query.reshape(row_count, -1)
    back_key = back_key.reshape(row_count, -1)
    back_value = back_value.reshape(row_count, -1)
    grad_query_w = mult_rows(back_query, attn_low)
    grad_key_w = mult_rows(back_key, attn_low)
    grad_value_w = mult_rows(back_value, attn_low)
    grad_normed = (
        mult_plain(back_query, full_query)
        + mult_plain(back_key, full_key)
        + mult_plain(back_value, full_value)
    )
    grad_attn_in, grad_attn_gain = attn_pull(grad_normed)
    grad1 = grad2 + grad_attn_in
    grad_place_w = jnp.einsum(
        "urc,rd->cd",
        grad_place_h.reshape(groups, 2 * length - 1, local_width),
        rel_table,
        preferred_element_type=jnp.float32,
    )
    grad_content = jnp.sum(grad_bias_first, axis=0).reshape(local_width)
    grad_place_b = jnp.sum(grad_bias_second, axis=0).reshape(local_width)
    back_up_first, back_down_first = gather_ffn(first_up, first_down)
    grad0, grad_first_gain, grad_up_first, grad_down_first = ffn_backward(
        grad1, saved_first, back_up_first, back_down_first
    )
    summed_first = sum_ffn(grad_up_first, grad_down_first)
    mixer_grads = (
        lax.psum_scatter(
            grad_query_w.astype(jnp.bfloat16), "wide", scatter_dimension=0, tiled=True
        ).astype(jnp.float32),
        lax.psum_scatter(
            grad_key_w.astype(jnp.bfloat16), "wide", scatter_dimension=0, tiled=True
        ).astype(jnp.float32),
        lax.psum_scatter(
            grad_value_w.astype(jnp.bfloat16), "wide", scatter_dimension=0, tiled=True
        ).astype(jnp.float32),
        lax.psum_scatter(
            grad_out.astype(jnp.bfloat16), "wide", scatter_dimension=0, tiled=True
        ).astype(jnp.float32),
        lax.psum_scatter(
            grad_glu.astype(jnp.bfloat16), "wide", scatter_dimension=0, tiled=True
        ).astype(jnp.float32),
        lax.psum_scatter(
            grad_point.astype(jnp.bfloat16), "wide", scatter_dimension=0, tiled=True
        ).astype(jnp.float32),
    )
    totals = (
        lax.psum(mixer_grads[0].astype(jnp.bfloat16), "utt").astype(jnp.float32),
        lax.psum(mixer_grads[1].astype(jnp.bfloat16), "utt").astype(jnp.float32),
        lax.psum(mixer_grads[2].astype(jnp.bfloat16), "utt").astype(jnp.float32),
        lax.psum(mixer_grads[3].astype(jnp.bfloat16), "utt").astype(jnp.float32),
        lax.psum(mixer_grads[4].astype(jnp.bfloat16), "utt").astype(jnp.float32),
        lax.psum(mixer_grads[5].astype(jnp.bfloat16), "utt").astype(jnp.float32),
        lax.psum(grad_place_w.astype(jnp.bfloat16), "utt").astype(jnp.float32),
        lax.psum(grad_content.astype(jnp.bfloat16), "utt").astype(jnp.float32),
        lax.psum(grad_place_b.astype(jnp.bfloat16), "utt").astype(jnp.float32),
    )
    small_grads = lax.psum(
        (
            grad_first_gain,
            grad_attn_gain,
            grad_conv_gain,
            grad_middle_gain,
            grad_second_gain,
            grad_final_gain,
            grad_kernel,
        ),
        ("utt", "wide"),
    )
    grad_input = grad0.astype(jnp.bfloat16).reshape(groups, frames_dev, channels)
    return (
        output,
        grad_input,
        small_grads[0],
        summed_first[0],
        summed_first[1],
        small_grads[1],
        totals[0],
        totals[1],
        totals[2],
        totals[3],
        totals[6],
        totals[7],
        totals[8],
        small_grads[2],
        totals[4],
        small_grads[6],
        small_grads[3],
        totals[5],
        small_grads[4],
        summed_second[0],
        summed_second[1],
        small_grads[5],
    )


def solution(mesh):
    in_specs = (
        P("utt", "wide", None),
        P("utt"),
        P("utt", "wide"),
        P("utt", "wide", None),
        P(),
        P(("utt", "wide"), None),
        P(("utt", "wide"), None),
        P(),
        P("wide", None),
        P("wide", None),
        P("wide", None),
        P("wide", None),
        P("wide", None),
        P("wide"),
        P("wide"),
        P(),
        P("wide", None),
        P(),
        P(),
        P("wide", None),
        P(),
        P(("utt", "wide"), None),
        P(("utt", "wide"), None),
        P(),
    )
    out_specs = (
        P("utt", "wide", None),
        P("utt", "wide", None),
        P(),
        P(("utt", "wide"), None),
        P(("utt", "wide"), None),
        P(),
        P("wide", None),
        P("wide", None),
        P("wide", None),
        P("wide", None),
        P("wide", None),
        P("wide"),
        P("wide"),
        P(),
        P("wide", None),
        P(),
        P(),
        P("wide", None),
        P(),
        P(("utt", "wide"), None),
        P(("utt", "wide"), None),
        P(),
    )
    shape = dict(mesh.shape)
    body = per_chip if shape["wide"] == 4 and shape["utt"] % 4 == 0 else per_device
    return jax.shard_map(
        body, mesh=mesh, in_specs=in_specs, out_specs=out_specs, check_vma=False
    )
```

```python
from functools import partial
import math

import jax
import jax.numpy as jnp
from jax import lax
from jax.experimental import pallas as pl
from jax.experimental.pallas import tpu as pltpu
from jax.sharding import PartitionSpec as P

HEAD_DIM = 64
KERNEL = 31
QBLK = 512
RIM = 15
PAIR = 128
ROWS_FWD = 512
ROWS_BWD = 256
VMEM = 56 * 2**20


EPSILON = 1e-05
MASKED_SCORE = -1e30


def with_halo(block, sides, width):
    for axis, dim in sides:
        count = lax.axis_size(axis)
        forward = [(i, i + 1) for i in range(count - 1)]
        backward = [(target, source) for source, target in forward]
        low = lax.ppermute(
            lax.slice_in_dim(block, block.shape[dim] - width, None, axis=dim), axis, forward
        )
        high = lax.ppermute(lax.slice_in_dim(block, 0, width, axis=dim), axis, backward)
        block = jnp.concatenate([low, block, high], axis=dim)
    return block


def norm_rows(values, gain_vec):
    average = jnp.mean(values, axis=-1, keepdims=True)
    centred = values - average
    spread = jnp.mean(centred * centred, axis=-1, keepdims=True)
    return centred * lax.rsqrt(spread + EPSILON) * gain_vec


def silu_slope(before):
    squash = jax.nn.sigmoid(before)
    return squash * (1.0 + before * (1.0 - squash))


def mult_trans(first_mat, second_mat):
    return lax.dot_general(
        first_mat, second_mat, (((1,), (1,)), ((), ())), preferred_element_type=jnp.float32
    )


def mult_plain(first_mat, second_mat):
    return jnp.dot(first_mat, second_mat, preferred_element_type=jnp.float32)


def mult_rows(first_mat, second_mat):
    return lax.dot_general(
        first_mat, second_mat, (((0,), (0,)), ((), ())), preferred_element_type=jnp.float32
    )


def relative_table(length, channels):
    offsets = length - 1 - jnp.arange(2 * length - 1).astype(jnp.float32)
    rates = jnp.exp(
        jnp.arange(channels // 2).astype(jnp.float32) * (-2.0 * math.log(10000.0) / channels)
    )
    angles = offsets[:, None] * rates[None, :]
    return jnp.concatenate([jnp.sin(angles), jnp.cos(angles)], axis=1)


def skew_rows(reversed_scores):
    block_rows, span = reversed_scores.shape
    flat = reversed_scores.reshape(-1)[block_rows - 1 : block_rows - 1 + block_rows * (span - 1)]
    return flat.reshape(block_rows, span - 1)[:, : span - block_rows + 1]


def unskew_rows(grad_scores, span):
    block_rows, length = grad_scores.shape
    padded = jnp.pad(grad_scores, ((0, 0), (0, span - 1 - length)))
    flat = jnp.pad(padded.reshape(-1), (block_rows - 1, 1))
    return flat.reshape(block_rows, span)


def gather_ffn(up_rows, down_rows):
    return (
        lax.all_gather(up_rows, ("utt", "wide"), axis=0, tiled=True),
        lax.all_gather(down_rows, ("utt", "wide"), axis=0, tiled=True),
    )


def sum_ffn(grad_up, grad_down):
    return (
        lax.psum_scatter(grad_up, ("utt", "wide"), scatter_dimension=0, tiled=True),
        lax.psum_scatter(grad_down, ("utt", "wide"), scatter_dimension=0, tiled=True),
    )


def ffn_forward(stream, gain_vec, up_full, down_full):
    normed, norm_pull = jax.vjp(norm_rows, stream, gain_vec)
    normed_low = normed.astype(jnp.bfloat16)
    before = mult_trans(normed_low, up_full)
    active_low = jax.nn.silu(before).astype(jnp.bfloat16)
    return (
        stream + 0.5 * mult_plain(active_low, down_full),
        (norm_pull, normed_low, before, active_low),
    )


def ffn_backward(grad_stream, saved_ffn, up_full, down_full):
    norm_pull, normed_low, before, active_low = saved_ffn
    grad_out = (0.5 * grad_stream).astype(jnp.bfloat16)
    grad_down = mult_rows(active_low, grad_out)
    grad_before = (mult_trans(grad_out, down_full) * silu_slope(before)).astype(jnp.bfloat16)
    grad_up = mult_rows(grad_before, normed_low)
    grad_input, grad_gain = norm_pull(mult_plain(grad_before, up_full))
    return (grad_stream + grad_input, grad_gain, grad_up, grad_down)


def head_forward(
    query_rows,
    key_rows,
    value_rows,
    place_rows,
    bias_first,
    bias_second,
    key_ok,
    block_rows,
    score_scale,
):
    length, head_width = query_rows.shape
    with_u = (query_rows.astype(jnp.float32) + bias_first).astype(jnp.bfloat16)
    with_v = (query_rows.astype(jnp.float32) + bias_second).astype(jnp.bfloat16)

    def one_block(block_index):
        first_row = block_index * block_rows
        block_u = lax.dynamic_slice_in_dim(with_u, first_row, block_rows, 0)
        block_v = lax.dynamic_slice_in_dim(with_v, first_row, block_rows, 0)
        near_rows = lax.dynamic_slice_in_dim(
            place_rows, length - block_rows - first_row, block_rows + length - 1, 0
        )
        scores = (
            mult_trans(block_u, key_rows) + skew_rows(mult_trans(block_v, near_rows))
        ) * score_scale
        scores = jnp.where(key_ok[None, :], scores, MASKED_SCORE)
        highest = jnp.max(scores, axis=1, keepdims=True)
        weights = jnp.exp(scores - highest)
        running = jnp.sum(weights, axis=1, keepdims=True)
        attend_prob = (weights / running).astype(jnp.bfloat16)
        return (
            mult_plain(attend_prob, value_rows).astype(jnp.bfloat16),
            (highest + jnp.log(running))[:, 0],
        )

    attended, log_total = lax.map(one_block, jnp.arange(length // block_rows, dtype=jnp.int32))
    return (attended.reshape(length, head_width), log_total.reshape(length))


def head_backward(
    query_rows,
    key_rows,
    value_rows,
    place_rows,
    bias_first,
    bias_second,
    key_ok,
    log_total,
    grad_mixed,
    block_rows,
    score_scale,
):
    length, head_width = query_rows.shape
    span = block_rows + length - 1
    with_u = (query_rows.astype(jnp.float32) + bias_first).astype(jnp.bfloat16)
    with_v = (query_rows.astype(jnp.float32) + bias_second).astype(jnp.bfloat16)

    def one_block(carried, block_index):
        grad_key, grad_value, grad_place = carried
        first_row = block_index * block_rows
        place_first = length - block_rows - first_row
        block_u = lax.dynamic_slice_in_dim(with_u, first_row, block_rows, 0)
        block_v = lax.dynamic_slice_in_dim(with_v, first_row, block_rows, 0)
        near_rows = lax.dynamic_slice_in_dim(place_rows, place_first, span, 0)
        block_total = lax.dynamic_slice_in_dim(log_total, first_row, block_rows, 0)
        block_grad = lax.dynamic_slice_in_dim(grad_mixed, first_row, block_rows, 0)
        scores = (
            mult_trans(block_u, key_rows) + skew_rows(mult_trans(block_v, near_rows))
        ) * score_scale
        scores = jnp.where(key_ok[None, :], scores, MASKED_SCORE)
        attend_prob = jnp.exp(scores - block_total[:, None])
        grad_prob = mult_trans(block_grad, value_rows)
        inner = jnp.sum(attend_prob * grad_prob, axis=1, keepdims=True)
        grad_score = jnp.where(key_ok[None, :], attend_prob * (grad_prob - inner), 0.0).astype(
            jnp.bfloat16
        )
        grad_value = grad_value + mult_rows(attend_prob.astype(jnp.bfloat16), block_grad)
        grad_with_u = mult_plain(grad_score, key_rows) * score_scale
        grad_key = grad_key + mult_rows(grad_score, block_u) * score_scale
        spread_grad = unskew_rows(grad_score, span)
        grad_with_v = mult_plain(spread_grad, near_rows) * score_scale
        place_part = (
            lax.dynamic_slice_in_dim(grad_place, place_first, span, 0)
            + mult_rows(spread_grad, block_v) * score_scale
        )
        grad_place = lax.dynamic_update_slice_in_dim(grad_place, place_part, place_first, 0)
        return ((grad_key, grad_value, grad_place), (grad_with_u, grad_with_v))

    zero_rows = jnp.zeros((length, head_width), jnp.float32)
    zero_place = jnp.zeros((2 * length - 1, head_width), jnp.float32)
    (grad_key, grad_value, grad_place), (grad_with_u, grad_with_v) = lax.scan(
        one_block,
        (zero_rows, zero_rows, zero_place),
        jnp.arange(length // block_rows, dtype=jnp.int32),
    )
    grad_with_u = grad_with_u.reshape(length, head_width)
    grad_with_v = grad_with_v.reshape(length, head_width)
    grad_query = (grad_with_u + grad_with_v).astype(jnp.bfloat16)
    return (
        grad_query,
        grad_key.astype(jnp.bfloat16),
        grad_value.astype(jnp.bfloat16),
        grad_place.astype(jnp.bfloat16),
        jnp.sum(grad_with_u, axis=0),
        jnp.sum(grad_with_v, axis=0),
    )


def biased(q_ref, bias_ref, scale):
    return ((q_ref[...].astype(jnp.float32) + bias_ref[...].astype(jnp.float32)).astype(jnp.bfloat16).astype(jnp.float32) * scale).astype(jnp.bfloat16)

def attend_fwd_kernel(len_ref, q_ref, k_ref, v_ref, place_ref, cb_ref, pb_ref, out_ref, prob_ref, *, scale):
    rows = q_ref.shape[0]
    length = k_ref.shape[0]
    span = rows + length
    first = pl.multiple_of(length - rows - pl.program_id(1) * rows, rows)
    lanes = lax.broadcasted_iota(jnp.int32, (rows, PAIR), 1)
    with_u = biased(q_ref, cb_ref, scale)
    with_v = biased(q_ref, pb_ref, scale)
    window = place_ref[pl.ds(first, span), :]
    key_ok = lax.broadcasted_iota(jnp.int32, (rows, length), 1) < len_ref[0]
    zero = jnp.zeros_like(with_u)
    mixed = []
    for head in range(2):
        mine = (lanes // HEAD_DIM) == head
        place_part = mult_trans(jnp.where(mine, with_v, zero), window)
        place_part = pltpu.roll(place_part, span - rows + 1, 1, stride=1, stride_axis=0)
        scores = mult_trans(jnp.where(mine, with_u, zero), k_ref[...]) + place_part[:, :length]
        scores = jnp.where(key_ok, scores, MASKED_SCORE)
        weights = jnp.exp(scores - jnp.max(scores, axis=1, keepdims=True))
        total = jnp.sum(weights, axis=1, keepdims=True)
        prob = (weights * (1.0 / total)).astype(jnp.bfloat16)
        prob_ref[head] = prob
        mixed.append(mult_plain(prob, v_ref[...]))
    out_ref[...] = jnp.where(lanes < HEAD_DIM, mixed[0], mixed[1]).astype(jnp.bfloat16)

def attend_fwd(length_arr, q, k, v, place, cb, pb, rows):
    length, width = q.shape
    pairs = width // PAIR
    return pl.pallas_call(
        partial(attend_fwd_kernel, scale=1.0 / math.sqrt(HEAD_DIM)),
        grid=(pairs, length // rows),
        in_specs=[
            pl.BlockSpec(memory_space=pltpu.SMEM),
            pl.BlockSpec((rows, PAIR), lambda p, i: (i, p)),
            pl.BlockSpec((length, PAIR), lambda p, i: (0, p)),
            pl.BlockSpec((length, PAIR), lambda p, i: (0, p)),
            pl.BlockSpec((2 * length, PAIR), lambda p, i: (0, p)),
            pl.BlockSpec((1, PAIR), lambda p, i: (0, p)),
            pl.BlockSpec((1, PAIR), lambda p, i: (0, p)),
        ],
        out_specs=[
            pl.BlockSpec((rows, PAIR), lambda p, i: (i, p)),
            pl.BlockSpec((2, rows, length), lambda p, i: (p, i, 0)),
        ],
        out_shape=[
            jax.ShapeDtypeStruct((length, width), jnp.bfloat16),
            jax.ShapeDtypeStruct((2 * pairs, length, length), jnp.bfloat16),
        ],
        compiler_params=pltpu.CompilerParams(vmem_limit_bytes=VMEM),
        cost_estimate=pl.CostEstimate(flops=40 * 10**9, bytes_accessed=20 * 2**20, transcendentals=pairs * 2 * length * length),
        name="attend_fwd",
    )(length_arr, q, k, v, place, cb, pb)

def attend_bwd_kernel(q_ref, k_ref, v_ref, place_ref, cb_ref, pb_ref, prob_ref, g_ref, gq_ref, gk_ref, gv_ref, gp_ref, gb_ref, gk_s, gv_s, gp_s, *, scale, trans):
    rows = q_ref.shape[0]
    length = k_ref.shape[0]
    span = rows + length
    step = pl.program_id(1)
    first = pl.multiple_of(length - rows - step * rows, rows)
    lanes = lax.broadcasted_iota(jnp.int32, (rows, PAIR), 1)
    flip = (lax.broadcasted_iota(jnp.int32, (rows, rows), 0) + lax.broadcasted_iota(jnp.int32, (rows, rows), 1) == rows - 1).astype(jnp.bfloat16)
    with_u = biased(q_ref, cb_ref, scale)
    with_v = mult_plain(flip, biased(q_ref, pb_ref, scale)).astype(jnp.bfloat16)
    grad = g_ref[...]
    window = place_ref[pl.ds(first, span), :]
    zero = jnp.zeros_like(with_u)

    @pl.when(step == 0)
    def _():
        gk_s[...] = jnp.zeros_like(gk_s)
        gv_s[...] = jnp.zeros_like(gv_s)
        gp_s[...] = jnp.zeros_like(gp_s)
        gb_ref[...] = jnp.zeros_like(gb_ref)

    if trans:
        grad_t, with_u_t, with_v_t = grad.T, with_u.T, with_v.T
    gu = []
    gw = []
    for head in range(2):
        mine = (lanes // HEAD_DIM) == head
        prob = prob_ref[head]
        grad_h = jnp.where(mine, grad, zero)
        grad_prob = mult_trans(grad_h, v_ref[...])
        weighted = prob.astype(jnp.float32) * grad_prob
        inner = jnp.sum(weighted, axis=1, keepdims=True)
        grad_score = (weighted - prob.astype(jnp.float32) * inner).astype(jnp.bfloat16)
        turned = mult_plain(flip, grad_score).astype(jnp.bfloat16)
        turned = jnp.concatenate([turned, jnp.zeros((rows, rows), jnp.bfloat16)], axis=1)
        turned = pltpu.roll(turned, 0, 1, stride=1, stride_axis=0)
        gu.append(mult_plain(grad_score, k_ref[...]))
        gw.append(mult_plain(turned, window))
        if trans:
            band = slice(head * HEAD_DIM, (head + 1) * HEAD_DIM)
            gv_s[band, :] += mult_plain(grad_t[band, :], prob)
            gk_s[band, :] += mult_plain(with_u_t[band, :], grad_score)
            gp_s[band, pl.ds(first, span)] += mult_plain(with_v_t[band, :], turned)
        else:
            gv_s[...] += mult_rows(prob, grad_h)
            gk_s[...] += mult_rows(grad_score, jnp.where(mine, with_u, zero))
            gp_s[pl.ds(first, span), :] += mult_rows(turned, jnp.where(mine, with_v, zero))
    grad_u = jnp.where(lanes < HEAD_DIM, gu[0], gu[1]) * scale
    grad_w = jnp.where(lanes < HEAD_DIM, gw[0], gw[1]) * scale
    gb_ref[0:1, :] += jnp.sum(grad_u, axis=0, keepdims=True)
    gb_ref[1:2, :] += jnp.sum(grad_w, axis=0, keepdims=True)
    high = grad_w.astype(jnp.bfloat16)
    rest = (grad_w - high.astype(jnp.float32)).astype(jnp.bfloat16)
    gq_ref[...] = (grad_u + mult_plain(flip, high) + mult_plain(flip, rest)).astype(jnp.bfloat16)

    @pl.when(step == pl.num_programs(1) - 1)
    def _():
        if trans:
            gk_ref[...] = gk_s[...].T.astype(jnp.bfloat16)
            gv_ref[...] = gv_s[...].T.astype(jnp.bfloat16)
            gp_ref[...] = gp_s[...].T.astype(jnp.bfloat16)
        else:
            gk_ref[...] = gk_s[...].astype(jnp.bfloat16)
            gv_ref[...] = gv_s[...].astype(jnp.bfloat16)
            gp_ref[...] = gp_s[...].astype(jnp.bfloat16)

def attend_bwd(q, k, v, place, cb, pb, prob, grad, rows, trans=True):
    length, width = q.shape
    pairs = width // PAIR
    full = pl.BlockSpec((length, PAIR), lambda p, i: (0, p))
    part = pl.BlockSpec((rows, PAIR), lambda p, i: (i, p))
    vec = pl.BlockSpec((1, PAIR), lambda p, i: (0, p))
    tall = pl.BlockSpec((2 * length, PAIR), lambda p, i: (0, p))
    shape = (lambda n: (PAIR, n)) if trans else (lambda n: (n, PAIR))
    return pl.pallas_call(
        partial(attend_bwd_kernel, scale=1.0 / math.sqrt(HEAD_DIM), trans=trans),
        grid=(pairs, length // rows),
        in_specs=[part, full, full, tall, vec, vec, pl.BlockSpec((2, rows, length), lambda p, i: (p, i, 0)), part],
        out_specs=[part, full, full, tall, pl.BlockSpec((8, PAIR), lambda p, i: (0, p))],
        out_shape=[
            jax.ShapeDtypeStruct((length, width), jnp.bfloat16),
            jax.ShapeDtypeStruct((length, width), jnp.bfloat16),
            jax.ShapeDtypeStruct((length, width), jnp.bfloat16),
            jax.ShapeDtypeStruct((2 * length, width), jnp.bfloat16),
            jax.ShapeDtypeStruct((8, width), jnp.float32),
        ],
        scratch_shapes=[
            pltpu.VMEM(shape(length), jnp.float32),
            pltpu.VMEM(shape(length), jnp.float32),
            pltpu.VMEM(shape(2 * length), jnp.float32),
        ],
        compiler_params=pltpu.CompilerParams(vmem_limit_bytes=VMEM),
        cost_estimate=pl.CostEstimate(flops=80 * 10**9, bytes_accessed=20 * 2**20, transcendentals=0),
        name="attend_bwd",
    )(q, k, v, place, cb, pb, prob, grad)


MESH = pl.DeviceIdType.MESH


def chip_place(layers):
    z, c, y, x = (lax.axis_index(axis) for axis in ("z", "core", "y", "x"))

    def at(dz=0, dc=0, dy=0, dx=0):
        return (
            lax.rem(z + dz, layers),
            lax.rem(c + dc, 2),
            lax.rem(y + dy, 2),
            lax.rem(x + dx, 2),
        )

    return at


def greet(at, layers):
    barrier = pltpu.get_barrier_semaphore()
    peers = [at(dz=k) for k in range(1, layers)] + [at(dc=1), at(dy=1), at(dx=1)]
    for peer in peers:
        pl.semaphore_signal(barrier, inc=1, device_id=peer, device_id_type=MESH)
    pl.semaphore_wait(barrier, len(peers))


def remote(source, target, sems, index, device):
    return pltpu.make_async_remote_copy(
        src_ref=source,
        dst_ref=target,
        send_sem=sems.at[(0, *index)],
        recv_sem=sems.at[(1, *index)],
        device_id=device,
        device_id_type=MESH,
    )


def far_first(layers):
    return sorted(range(1, layers), key=lambda k: -min(k, layers - k)) + [0]


def gather_plan(layers, shards, fulls, z_sem, p_sem, d_sem, c_sem, own_sem):
    at = chip_place(layers)
    arrays = range(len(shards))
    half = shards[0].shape[0] // 2
    items = [(dz, a) for dz in reversed(far_first(layers)) for a in arrays]
    own = [pltpu.make_async_copy(shards[a], fulls[a].at[0, 0, 0, 0], own_sem.at[a]) for a in arrays]
    along, flat, cross, core = {}, {}, {}, {}
    for dz, a in items:
        full = fulls[a].at[0, dz]
        source = full.at[0, 0] if dz else shards[a]
        if dz:
            along[dz, a] = remote(shards[a], full.at[0, 0], z_sem, (a, dz), at(dz=dz))
        flat[dz, a] = (
            remote(source, full.at[0, 1], p_sem, (a, dz, 0), at(dx=1)),
            remote(source, full.at[1, 0], p_sem, (a, dz, 1), at(dy=1)),
        )
        first, second = pl.ds(0, half), pl.ds(half, half)
        cross[dz, a] = (
            remote(full.at[0, 1, second], full.at[1, 1, second], d_sem, (a, dz, 0), at(dy=1)),
            remote(full.at[1, 0, first], full.at[1, 1, first], d_sem, (a, dz, 1), at(dx=1)),
        )
        core[dz, a] = remote(full, fulls[a].at[1, dz], c_sem, (a, dz), at(dc=1))

    def enter():
        greet(at, layers)
        for dz in far_first(layers)[:-1]:
            for a in arrays:
                along[dz, a].start()
        for copy in own:
            copy.start()

    def spread(item):
        if item[0]:
            along[item].wait_recv()
        for copy in flat[item]:
            copy.start()

    def turn(item):
        for got, out in zip(flat[item], cross[item]):
            got.wait_recv()
            out.start()

    def share(item):
        for got in cross[item]:
            got.wait_recv()
        if not item[0]:
            own[item[1]].wait()
        core[item].start()

    steps = []
    for turn_at in range(len(items) + 4):
        for action, lag in ((spread, 0), (turn, 2), (share, 4)):
            if 0 <= turn_at - lag < len(items):
                steps.append(partial(action, items[turn_at - lag]))

    def leave():
        for item in items:
            core[item].wait_recv()
        for item in items:
            if item[0]:
                along[item].wait_send()
            for copy in (*flat[item], *cross[item], core[item]):
                copy.wait_send()

    return enter, steps, leave


def gather_sems(count, layers):
    dma = pltpu.SemaphoreType.DMA
    return [
        dma((2, count, layers)),
        dma((2, count, layers, 2)),
        dma((2, count, layers, 2)),
        dma((2, count, layers)),
        dma((count,)),
    ]


def gather_kernel(layers, count, *refs):
    enter, steps, leave = gather_plan(layers, refs[:count], refs[count : 2 * count], *refs[2 * count :])
    enter()
    for step in steps:
        step()
    leave()


def gather_all(layers, shards, collective_id):
    count = len(shards)
    rows, width = shards[0].shape
    fulls = pl.pallas_call(
        partial(gather_kernel, layers, count),
        in_specs=[pl.BlockSpec(memory_space=pl.ANY)] * count,
        out_specs=[pl.BlockSpec(memory_space=pl.ANY)] * count,
        out_shape=[jax.ShapeDtypeStruct((2, layers, 2, 2, rows, width), jnp.bfloat16)] * count,
        scratch_shapes=gather_sems(count, layers),
        compiler_params=pltpu.CompilerParams(collective_id=collective_id, has_side_effects=True),
        cost_estimate=pl.CostEstimate(flops=0, bytes_accessed=200 * 2**20, transcendentals=0),
        name="gather_all",
    )(*shards)
    return [full.reshape(8 * layers * rows, width) for full in fulls]


def add_rows(target, one, two):
    target[...] = (one[...].astype(jnp.float32) + two[...].astype(jnp.float32)).astype(target.dtype)


def reduce_plan(layers, parts, outs, sums, got_c, got_d, got_p, got_z, load_sem, c_sem, d_sem, p_sem, z_sem):
    at = chip_place(layers)
    arrays = range(len(parts))
    half = parts[0].shape[4] // 2
    items = [(dz, a) for dz in far_first(layers) for a in arrays]
    first, second = pl.ds(0, half), pl.ds(half, half)
    load, core, cross, flat, along = {}, {}, {}, {}, {}
    for dz, a in items:
        total = sums.at[a, dz]
        load[dz, a] = pltpu.make_async_copy(parts[a].at[0, dz], total, load_sem.at[a, dz])
        core[dz, a] = remote(parts[a].at[1, dz], got_c.at[a, dz], c_sem, (a, dz), at(dc=1))
        cross[dz, a] = (
            remote(total.at[1, 1, first], got_d.at[a, dz, 0], d_sem, (a, dz, 0), at(dx=1)),
            remote(total.at[1, 1, second], got_d.at[a, dz, 1], d_sem, (a, dz, 1), at(dy=1)),
        )
        flat[dz, a] = (
            remote(total.at[1, 0], got_p.at[a, dz, 0], p_sem, (a, dz, 0), at(dy=1)),
            remote(total.at[0, 1], got_p.at[a, dz, 1], p_sem, (a, dz, 1), at(dx=1)),
        )
        if dz:
            along[dz, a] = remote(
                total.at[0, 0], got_z.at[a, dz], z_sem, (a, dz), at(dz=layers - dz)
            )

    def enter():
        greet(at, layers)
        for item in items:
            core[item].start()
            load[item].start()

    def join_core(item):
        dz, a = item
        load[item].wait()
        core[item].wait_recv()
        for dy, dx in ((1, 1), (1, 0), (0, 1), (0, 0)):
            here = sums.at[a, dz, dy, dx]
            add_rows(here, here, got_c.at[a, dz, dy, dx])
            if dy and dx:
                for copy in cross[item]:
                    copy.start()

    def join_cross(item):
        dz, a = item
        one, two = sums.at[a, dz, 1, 0, first], sums.at[a, dz, 0, 1, second]
        cross[item][0].wait_recv()
        add_rows(one, one, got_d.at[a, dz, 0])
        flat[item][0].start()
        cross[item][1].wait_recv()
        add_rows(two, two, got_d.at[a, dz, 1])
        flat[item][1].start()

    def join_flat(item):
        dz, a = item
        here = sums.at[a, dz, 0, 0]
        for copy in flat[item]:
            copy.wait_recv()
        here[...] = (
            here[...].astype(jnp.float32)
            + got_p[a, dz, 0].astype(jnp.float32)
            + got_p[a, dz, 1].astype(jnp.float32)
        ).astype(jnp.bfloat16)
        if dz:
            along[item].start()

    steps = []
    lags = ((join_core, 0), (join_cross, 3), (join_flat, 5))
    for turn_at in range(len(items) + 5):
        for action, lag in lags:
            if 0 <= turn_at - lag < len(items):
                steps.append(partial(action, items[turn_at - lag]))

    def leave():
        for a in arrays:
            total = sums[a, 0, 0, 0].astype(jnp.float32)
            for dz in range(1, layers):
                along[dz, a].wait_recv()
                total = total + got_z[a, dz].astype(jnp.float32)
            outs[a][...] = total
        for item in items:
            if item[0]:
                along[item].wait_send()
            for copy in (core[item], *cross[item], *flat[item]):
                copy.wait_send()

    return enter, steps, leave


def reduce_scratch(count, layers, rows, width):
    dma = pltpu.SemaphoreType.DMA
    low = lambda *shape: pltpu.VMEM((count, layers, *shape, width), jnp.bfloat16)
    return [
        low(2, 2, rows),
        low(2, 2, rows),
        low(2, rows // 2),
        low(2, rows),
        low(rows),
        dma((count, layers)),
        dma((2, count, layers)),
        dma((2, count, layers, 2)),
        dma((2, count, layers, 2)),
        dma((2, count, layers)),
    ]


def reduce_kernel(layers, count, *refs):
    enter, steps, leave = reduce_plan(layers, refs[:count], refs[count : 2 * count], *refs[2 * count :])
    enter()
    for step in steps:
        step()
    leave()


def reduce_all(layers, parts, collective_id):
    count = len(parts)
    total, width = parts[0].shape
    rows = total // (8 * layers)
    return pl.pallas_call(
        partial(reduce_kernel, layers, count),
        in_specs=[pl.BlockSpec(memory_space=pl.ANY)] * count,
        out_specs=[pl.BlockSpec(memory_space=pltpu.VMEM)] * count,
        out_shape=[jax.ShapeDtypeStruct((rows, width), jnp.float32)] * count,
        scratch_shapes=reduce_scratch(count, layers, rows, width),
        compiler_params=pltpu.CompilerParams(
            collective_id=collective_id, has_side_effects=True, vmem_limit_bytes=VMEM
        ),
        cost_estimate=pl.CostEstimate(flops=0, bytes_accessed=200 * 2**20, transcendentals=0),
        name="reduce_all",
    )(*(part.reshape(2, layers, 2, 2, rows, width) for part in parts))


class Hops:
    def __init__(self, layers):
        self.layers = layers

    def send(self, block, dz=0, dc=0, dy=0, dx=0):
        pairs = []
        for z in range(self.layers):
            for c in range(2):
                for w in range(4):
                    to = ((z + dz) % self.layers * 2 + (c ^ dc)) * 4 + (w ^ (2 * dy + dx))
                    pairs.append(((z * 2 + c) * 4 + w, to))
        return lax.ppermute(block, ("z", "core", "y", "x"), pairs)

    def turn(self, block, step):
        pairs = []
        for z in range(self.layers):
            for c in range(2):
                for w in range(4):
                    to = (z * 2 + w // 2) * 4 + 2 * c + ((w % 2) ^ step)
                    pairs.append(((z * 2 + c) * 4 + w, to))
        return lax.ppermute(block, ("z", "core", "y", "x"), pairs)


def taps_forward(padded, kernel_f, count):
    total = jnp.zeros((count, padded.shape[1]), jnp.float32)
    for offset in range(KERNEL):
        total = total + padded[offset : offset + count] * kernel_f[offset]
    return total


def with_rim(hops, block, core):
    edge = jnp.where(core == 0, block[-16:], block[:16])
    got = hops.send(edge, dc=1)
    zero = jnp.zeros_like(got)
    low = jnp.where(core == 0, zero, got)[1:]
    high = jnp.where(core == 0, got, zero)[:RIM]
    return jnp.concatenate([low, block, high])


def per_chip(
    frames,
    lengths,
    masked,
    cotangent,
    first_gain,
    first_up,
    first_down,
    attn_gain,
    query_weight,
    key_weight,
    value_weight,
    out_weight,
    place_weight,
    content_bias,
    place_bias,
    conv_gain,
    glu_weight,
    depth_kernel,
    middle_gain,
    point_weight,
    second_gain,
    second_up,
    second_down,
    final_gain,
):
    core, y, x = lax.axis_index("core"), lax.axis_index("y"), lax.axis_index("x")
    wide_at = 2 * y + x
    layers = lax.axis_size("z")
    hops = Hops(layers)
    groups, quarter, channels = frames.shape
    rows = groups * quarter
    length = 2 * rows
    f32 = lambda v: v.astype(jnp.float32)
    low = lambda v: v.astype(jnp.bfloat16)

    def pick(flag, one, two):
        return jnp.where(flag, one, two), jnp.where(flag, two, one)

    def turn_in(block):
        swap = [lax.dynamic_index_in_dim(block, x ^ step, 0, keepdims=False) for step in range(2)]
        got = [hops.turn(swap[step], step) for step in range(2)]
        return jnp.concatenate(pick(x == 0, *got))

    def turn_out(block):
        parts = pick(x == 0, block[:quarter], block[quarter:])
        got = [hops.turn(parts[step], step) for step in range(2)]
        return jnp.stack(pick(x == 0, *got))

    frames_own = turn_in(frames)
    up_first, down_first = gather_all(layers, [first_up, first_down], 1)
    positions = wide_at * quarter + jnp.arange(quarter, dtype=jnp.int32)
    seed_weight = f32(masked) * f32(positions[None, :] < lengths[:, None])
    seed_own_low = low(f32(cotangent) * seed_weight[:, :, None])
    near_lengths = jnp.where(core == y, lengths, hops.send(lengths, dc=1))
    own_length = lax.dynamic_slice_in_dim(near_lengths, x, 1)
    own_rows = core * rows + jnp.arange(rows, dtype=jnp.int32)
    frame_ok = f32(own_rows < own_length[0])[:, None]

    def own_half(weight):
        count = weight.shape[0] // 2
        return lax.dynamic_slice_in_dim(weight, core * count, count)

    band = query_weight.shape[0] // 2
    own_bias = own_half(jnp.stack([content_bias, place_bias], axis=1)).T
    attn_chunk = jnp.concatenate(
        [
            own_half(query_weight),
            own_half(key_weight),
            own_half(value_weight),
            own_half(place_weight),
            jnp.pad(own_bias, ((0, 14), (0, channels - band))),
        ]
    )
    conv_chunk = jnp.concatenate([own_half(out_weight), own_half(point_weight), own_half(glu_weight)])
    attn_all = lax.all_gather(attn_chunk, ("y", "x"), axis=0)
    conv_all = lax.all_gather(conv_chunk, ("y", "x"), axis=0)

    def heads_of(at):
        return attn_all[:, at * band : (at + 1) * band].reshape(4 * band, channels)

    query_own, key_own, value_own, place_own = (heads_of(at) for at in range(4))
    own_biases = attn_all[:, 4 * band : 4 * band + 2, :band].transpose(1, 0, 2).reshape(2, 4 * band)
    conv_other = hops.send(conv_all, dc=1)
    conv_both = jnp.stack(pick(core == 0, conv_all, conv_other), axis=1)
    full_out = jnp.concatenate([conv_all[:, :band], conv_other[:, :band]]).reshape(8 * band, channels)
    full_point = conv_both[:, :, band : 2 * band].reshape(8 * band, channels)
    full_glu = conv_both[:, :, 2 * band :].reshape(16 * band, channels)

    stream0 = f32(frames_own)
    stream1, saved_first = ffn_forward(stream0, f32(first_gain), up_first, down_first)
    normed_attn, attn_pull = jax.vjp(norm_rows, stream1, f32(attn_gain))
    attn_half = low(normed_attn)
    attn_other = hops.send(attn_half, dc=1)
    attn_low = jnp.concatenate(pick(core == 0, attn_half, attn_other))
    rel_table = low(relative_table(length, channels))
    rel_table = jnp.concatenate([rel_table, jnp.zeros((1, channels), jnp.bfloat16)])
    query = low(mult_trans(attn_low, query_own))
    key = low(mult_trans(attn_low, key_own))
    value = low(mult_trans(attn_low, value_own))
    place = low(mult_trans(rel_table, place_own))
    attended, prob = attend_fwd(
        own_length, query, key, value, place, own_biases[:1], own_biases[1:], ROWS_FWD
    )

    def halves(matrix):
        own = lax.dynamic_slice_in_dim(matrix, core * rows, rows)
        other = lax.dynamic_slice_in_dim(matrix, (1 - core) * rows, rows)
        return own, other

    att_own, att_other = halves(attended)
    framed = jnp.concatenate([att_own, hops.send(att_other, dc=1)], axis=1)
    stream2 = stream1 + mult_plain(framed, full_out)
    normed_conv, conv_pull = jax.vjp(norm_rows, stream2, f32(conv_gain))
    conv_low = low(normed_conv)
    glu_in = mult_trans(conv_low, full_glu)
    linear = glu_in[:, :channels]
    gating = jax.nn.sigmoid(glu_in[:, channels:])
    gated = low(linear * gating * frame_ok)
    padded = with_rim(hops, gated, core)
    kernel_f = f32(depth_kernel)
    conv_out = taps_forward(padded, kernel_f, rows)
    middle, middle_pull = jax.vjp(norm_rows, conv_out, f32(middle_gain))
    swished = low(jax.nn.silu(middle))
    stream3 = stream2 + mult_trans(swished, full_point)
    up_second, down_second = gather_all(layers, [second_up, second_down], 1)
    stream4, saved_second = ffn_forward(stream3, f32(second_gain), up_second, down_second)
    final_rows, final_pull = jax.vjp(norm_rows, stream4, f32(final_gain))
    output = turn_out(low(final_rows))

    seed_own = turn_in(seed_own_low)
    grad4, grad_final_gain = final_pull(f32(seed_own))

    def ffn_back(grad_stream, saved_ffn, up_full, down_full):
        norm_pull, normed_low, before, active_low = saved_ffn
        grad_out = low(0.5 * grad_stream)
        grad_down = low(mult_rows(active_low, grad_out))
        grad_before = low(mult_trans(grad_out, down_full) * silu_slope(before))
        grad_up = low(mult_rows(grad_before, normed_low))
        grad_input, grad_gain = norm_pull(mult_plain(grad_before, up_full))
        sum_up, sum_down = reduce_all(layers, [grad_up, grad_down], 2)
        return grad_stream + grad_input, grad_gain, sum_up, sum_down

    grad3, grad_second_gain, sum_up_second, sum_down_second = ffn_back(
        grad4, saved_second, up_second, down_second
    )
    grad_branch = low(grad3)
    grad_point = mult_rows(grad_branch, swished)
    grad_middle = mult_plain(grad_branch, full_point) * silu_slope(middle)
    grad_conv, grad_middle_gain = middle_pull(grad_middle)
    conv_grad_low = low(grad_conv)
    grad_padded = with_rim(hops, conv_grad_low, core)
    grad_gated = taps_forward(grad_padded, kernel_f[::-1], rows)
    grad_kernel = jnp.stack(
        [
            jnp.sum(f32(padded[offset : offset + rows]) * f32(conv_grad_low), axis=0)
            for offset in range(KERNEL)
        ]
    )
    grad_gated = grad_gated * frame_ok
    grad_glu_in = low(
        jnp.concatenate(
            [grad_gated * gating, grad_gated * linear * gating * (1.0 - gating)], axis=1
        )
    )
    grad_glu = mult_rows(grad_glu_in, conv_low)
    grad_conv_in, grad_conv_gain = conv_pull(mult_plain(grad_glu_in, full_glu))
    grad2 = grad3 + grad_conv_in
    grad_attn = low(grad2)
    grad_out = mult_rows(framed, grad_attn)
    grad_framed = low(mult_trans(grad_attn, full_out))
    side = channels // 2
    grad_heads = jnp.concatenate(
        pick(core == 0, grad_framed[:, :side], hops.send(grad_framed[:, side:], dc=1))
    )
    grad_query, grad_key, grad_value, grad_place, grad_biases = attend_bwd(
        query, key, value, place, own_biases[:1], own_biases[1:], prob, grad_heads, ROWS_BWD
    )
    grad_query_w = mult_rows(grad_query, attn_low)
    grad_key_w = mult_rows(grad_key, attn_low)
    grad_value_w = mult_rows(grad_value, attn_low)
    grad_place_w = mult_rows(grad_place, rel_table)
    grad_normed = (
        mult_plain(grad_query, query_own)
        + mult_plain(grad_key, key_own)
        + mult_plain(grad_value, value_own)
    )
    normed_own, normed_other = halves(grad_normed)
    grad_attn_in, grad_attn_gain = attn_pull(normed_own + f32(hops.send(low(normed_other), dc=1)))
    grad1 = grad2 + grad_attn_in
    grad0, grad_first_gain, sum_up_first, sum_down_first = ffn_back(
        grad1, saved_first, up_first, down_first
    )
    grad_input = turn_out(low(grad0))

    def by_wide(matrix):
        return low(matrix).reshape(4, -1, channels)

    def by_core(matrix):
        parts = low(matrix).reshape(4, 2, -1, channels)
        own = lax.dynamic_index_in_dim(parts, core, 1, keepdims=False)
        return own, lax.dynamic_index_in_dim(parts, 1 - core, 1, keepdims=False)

    out_parts = (by_wide(grad_out[: 4 * band]), by_wide(grad_out[4 * band :]))
    kept, sent = (
        jnp.concatenate(parts, axis=1)
        for parts in zip(out_parts, by_core(grad_point), by_core(grad_glu))
    )
    conv_part = low(f32(kept) + f32(hops.send(sent, dc=1)))
    attn_part = jnp.concatenate(
        [by_wide(part) for part in (grad_query_w, grad_key_w, grad_value_w, grad_place_w)], axis=1
    )

    def totals_of(part):
        mine = lax.psum_scatter(part, ("y", "x"), scatter_dimension=0, tiled=False)
        mine = lax.psum(mine, "z")
        return pick(core == 0, mine, hops.send(mine, dc=1))

    conv_totals, attn_totals = totals_of(conv_part), totals_of(attn_part)

    def owned(totals, start, count):
        return f32(jnp.concatenate([part[start : start + count] for part in totals]))

    total_out, total_point = owned(conv_totals, 0, band), owned(conv_totals, band, band)
    total_glu = owned(conv_totals, 2 * band, 2 * band)
    total_query, total_key, total_value, total_place = (
        owned(attn_totals, at * band, band) for at in range(4)
    )

    spread = jnp.zeros((2, 4, 2, band), jnp.float32)
    spread = lax.dynamic_update_slice(
        spread, grad_biases[:2].reshape(2, 4, 1, band), (0, 0, core, 0)
    ).reshape(2, channels)
    small = lax.psum(
        jnp.concatenate(
            [
                grad_first_gain[None],
                grad_attn_gain[None],
                grad_conv_gain[None],
                grad_middle_gain[None],
                grad_second_gain[None],
                grad_final_gain[None],
                spread,
                grad_kernel,
            ]
        ),
        ("z", "core", "y", "x"),
    )
    own_bias_grad = lax.dynamic_slice_in_dim(small[6:8], wide_at * 2 * band, 2 * band, 1)
    return (
        output,
        grad_input,
        small[0],
        sum_up_first,
        sum_down_first,
        small[1],
        total_query,
        total_key,
        total_value,
        total_out,
        total_place,
        own_bias_grad[0],
        own_bias_grad[1],
        small[2],
        total_glu,
        small[8:],
        small[3],
        total_point,
        small[4],
        sum_up_second,
        sum_down_second,
        small[5],
    )


def per_device(
    frames,
    lengths,
    masked,
    cotangent,
    first_gain,
    first_up,
    first_down,
    attn_gain,
    query_weight,
    key_weight,
    value_weight,
    out_weight,
    place_weight,
    content_bias,
    place_bias,
    conv_gain,
    glu_weight,
    depth_kernel,
    middle_gain,
    point_weight,
    second_gain,
    second_up,
    second_down,
    final_gain,
):
    groups, frames_dev, channels = frames.shape
    row_count = groups * frames_dev
    length = frames_dev * lax.axis_size("wide")
    score_scale = 1.0 / math.sqrt(HEAD_DIM)
    positions = lax.axis_index("wide") * frames_dev + jnp.arange(frames_dev, dtype=jnp.int32)
    frame_grid = (positions[None, :] < lengths[:, None]).astype(jnp.float32)
    frame_ok = frame_grid.reshape(row_count, 1)
    key_ok = jnp.arange(length, dtype=jnp.int32)[None, :] < lengths[:, None]
    stream0 = frames.reshape(row_count, channels).astype(jnp.float32)
    up_first, down_first = gather_ffn(first_up, first_down)
    stream1, saved_first = ffn_forward(
        stream0, first_gain.astype(jnp.float32), up_first, down_first
    )
    full_query, full_key, full_value, full_out, full_glu, full_point = (
        lax.all_gather(query_weight, "wide", axis=0, tiled=True),
        lax.all_gather(key_weight, "wide", axis=0, tiled=True),
        lax.all_gather(value_weight, "wide", axis=0, tiled=True),
        lax.all_gather(out_weight, "wide", axis=0, tiled=True),
        lax.all_gather(glu_weight, "wide", axis=0, tiled=True),
        lax.all_gather(point_weight, "wide", axis=0, tiled=True),
    )
    normed_attn, attn_pull = jax.vjp(norm_rows, stream1, attn_gain.astype(jnp.float32))
    attn_low = normed_attn.astype(jnp.bfloat16)
    query_frames = (
        mult_trans(attn_low, full_query).astype(jnp.bfloat16).reshape(groups, frames_dev, -1)
    )
    key_frames = mult_trans(attn_low, full_key).astype(jnp.bfloat16).reshape(groups, frames_dev, -1)
    value_frames = (
        mult_trans(attn_low, full_value).astype(jnp.bfloat16).reshape(groups, frames_dev, -1)
    )
    heads_query, heads_key, heads_value = (
        lax.all_to_all(query_frames, "wide", split_axis=2, concat_axis=1, tiled=True),
        lax.all_to_all(key_frames, "wide", split_axis=2, concat_axis=1, tiled=True),
        lax.all_to_all(value_frames, "wide", split_axis=2, concat_axis=1, tiled=True),
    )
    local_width = heads_query.shape[2]
    head_count = local_width // HEAD_DIM
    rel_table = relative_table(length, channels).astype(jnp.bfloat16)
    place_rows = (
        mult_trans(rel_table, place_weight)
        .astype(jnp.bfloat16)
        .reshape(2 * length - 1, head_count, HEAD_DIM)
    )
    bias_first = content_bias.astype(jnp.float32).reshape(head_count, HEAD_DIM)
    bias_second = place_bias.astype(jnp.float32).reshape(head_count, HEAD_DIM)
    split_query = heads_query.reshape(groups, length, head_count, HEAD_DIM)
    split_key = heads_key.reshape(groups, length, head_count, HEAD_DIM)
    split_value = heads_value.reshape(groups, length, head_count, HEAD_DIM)
    forward_heads = jax.vmap(
        partial(head_forward, block_rows=QBLK, score_scale=score_scale),
        in_axes=(1, 1, 1, 1, 0, 0, None),
        out_axes=(1, 0),
    )

    def attend_utt(unit_items):
        return forward_heads(
            unit_items[0],
            unit_items[1],
            unit_items[2],
            place_rows,
            bias_first,
            bias_second,
            unit_items[3],
        )

    attended, log_total = lax.map(attend_utt, (split_query, split_key, split_value, key_ok))
    framed = lax.all_to_all(
        attended.reshape(groups, length, local_width),
        "wide",
        split_axis=1,
        concat_axis=2,
        tiled=True,
    ).reshape(row_count, -1)
    stream2 = stream1 + mult_plain(framed, full_out)
    normed_conv, conv_pull = jax.vjp(norm_rows, stream2, conv_gain.astype(jnp.float32))
    conv_low = normed_conv.astype(jnp.bfloat16)
    glu_in = mult_trans(conv_low, full_glu)
    linear = glu_in[:, :channels]
    gating = jax.nn.sigmoid(glu_in[:, channels:])
    gated = (linear * gating * frame_ok).astype(jnp.bfloat16).reshape(groups, frames_dev, channels)
    padded = with_halo(gated, (("wide", 1),), RIM)
    kernel_f = depth_kernel.astype(jnp.float32)
    conv_out = jnp.zeros((groups, frames_dev, channels), jnp.float32)
    for offset in range(KERNEL):
        conv_out = conv_out + padded[:, offset : offset + frames_dev, :] * kernel_f[offset]
    conv_out = conv_out.reshape(row_count, channels)
    middle, middle_pull = jax.vjp(norm_rows, conv_out, middle_gain.astype(jnp.float32))
    swished = jax.nn.silu(middle).astype(jnp.bfloat16)
    stream3 = stream2 + mult_trans(swished, full_point)
    up_second, down_second = gather_ffn(second_up, second_down)
    stream4, saved_second = ffn_forward(
        stream3, second_gain.astype(jnp.float32), up_second, down_second
    )
    final_rows, final_pull = jax.vjp(norm_rows, stream4, final_gain.astype(jnp.float32))
    output = final_rows.astype(jnp.bfloat16).reshape(groups, frames_dev, channels)
    seed_weight = (masked.astype(jnp.float32) * frame_grid).reshape(row_count, 1)
    seed_grad = cotangent.reshape(row_count, channels).astype(jnp.float32) * seed_weight
    grad4, grad_final_gain = final_pull(seed_grad)
    back_up_second, back_down_second = gather_ffn(second_up, second_down)
    grad3, grad_second_gain, grad_up_second, grad_down_second = ffn_backward(
        grad4, saved_second, back_up_second, back_down_second
    )
    summed_second = sum_ffn(grad_up_second, grad_down_second)
    grad_branch = grad3.astype(jnp.bfloat16)
    grad_point = mult_rows(grad_branch, swished)
    grad_middle = mult_plain(grad_branch, full_point) * silu_slope(middle)
    grad_conv, grad_middle_gain = middle_pull(grad_middle)
    conv_grad_low = grad_conv.astype(jnp.bfloat16).reshape(groups, frames_dev, channels)
    grad_padded = with_halo(conv_grad_low, (("wide", 1),), RIM)
    grad_gated = jnp.zeros((groups, frames_dev, channels), jnp.float32)
    kernel_rows = []
    for offset in range(KERNEL):
        grad_gated = (
            grad_gated
            + grad_padded[:, 2 * RIM - offset : 2 * RIM - offset + frames_dev, :] * kernel_f[offset]
        )
        kernel_rows.append(
            jnp.einsum(
                "rzn,rzn->n",
                padded[:, offset : offset + frames_dev, :],
                conv_grad_low,
                preferred_element_type=jnp.float32,
            )
        )
    grad_kernel = jnp.stack(kernel_rows)
    grad_gated = grad_gated.reshape(row_count, channels) * frame_ok
    grad_glu_in = jnp.concatenate(
        [grad_gated * gating, grad_gated * linear * gating * (1.0 - gating)], axis=1
    ).astype(jnp.bfloat16)
    grad_glu = mult_rows(grad_glu_in, conv_low)
    grad_conv_in, grad_conv_gain = conv_pull(mult_plain(grad_glu_in, full_glu))
    grad2 = grad3 + grad_conv_in
    grad_attn = grad2.astype(jnp.bfloat16)
    grad_out = mult_rows(framed, grad_attn)
    grad_framed = (
        mult_trans(grad_attn, full_out).astype(jnp.bfloat16).reshape(groups, frames_dev, -1)
    )
    grad_heads = lax.all_to_all(grad_framed, "wide", split_axis=2, concat_axis=1, tiled=True)
    backward_heads = jax.vmap(
        partial(head_backward, block_rows=QBLK, score_scale=score_scale),
        in_axes=(1, 1, 1, 1, 0, 0, None, 0, 1),
        out_axes=(1, 1, 1, 1, 0, 0),
    )

    def attend_back(unit_items):
        return backward_heads(
            unit_items[0],
            unit_items[1],
            unit_items[2],
            place_rows,
            bias_first,
            bias_second,
            unit_items[3],
            unit_items[4],
            unit_items[5],
        )

    grad_query_h, grad_key_h, grad_value_h, grad_place_h, grad_bias_first, grad_bias_second = (
        lax.map(
            attend_back,
            (
                split_query,
                split_key,
                split_value,
                key_ok,
                log_total,
                grad_heads.reshape(groups, length, head_count, HEAD_DIM),
            ),
        )
    )
    back_query, back_key, back_value = (
        lax.all_to_all(
            grad_query_h.reshape(groups, length, local_width),
            "wide",
            split_axis=1,
            concat_axis=2,
            tiled=True,
        ),
        lax.all_to_all(
            grad_key_h.reshape(groups, length, local_width),
            "wide",
            split_axis=1,
            concat_axis=2,
            tiled=True,
        ),
        lax.all_to_all(
            grad_value_h.reshape(groups, length, local_width),
            "wide",
            split_axis=1,
            concat_axis=2,
            tiled=True,
        ),
    )
    back_query = back_query.reshape(row_count, -1)
    back_key = back_key.reshape(row_count, -1)
    back_value = back_value.reshape(row_count, -1)
    grad_query_w = mult_rows(back_query, attn_low)
    grad_key_w = mult_rows(back_key, attn_low)
    grad_value_w = mult_rows(back_value, attn_low)
    grad_normed = (
        mult_plain(back_query, full_query)
        + mult_plain(back_key, full_key)
        + mult_plain(back_value, full_value)
    )
    grad_attn_in, grad_attn_gain = attn_pull(grad_normed)
    grad1 = grad2 + grad_attn_in
    grad_place_w = jnp.einsum(
        "urc,rd->cd",
        grad_place_h.reshape(groups, 2 * length - 1, local_width),
        rel_table,
        preferred_element_type=jnp.float32,
    )
    grad_content = jnp.sum(grad_bias_first, axis=0).reshape(local_width)
    grad_place_b = jnp.sum(grad_bias_second, axis=0).reshape(local_width)
    back_up_first, back_down_first = gather_ffn(first_up, first_down)
    grad0, grad_first_gain, grad_up_first, grad_down_first = ffn_backward(
        grad1, saved_first, back_up_first, back_down_first
    )
    summed_first = sum_ffn(grad_up_first, grad_down_first)
    mixer_grads = (
        lax.psum_scatter(
            grad_query_w.astype(jnp.bfloat16), "wide", scatter_dimension=0, tiled=True
        ).astype(jnp.float32),
        lax.psum_scatter(
            grad_key_w.astype(jnp.bfloat16), "wide", scatter_dimension=0, tiled=True
        ).astype(jnp.float32),
        lax.psum_scatter(
            grad_value_w.astype(jnp.bfloat16), "wide", scatter_dimension=0, tiled=True
        ).astype(jnp.float32),
        lax.psum_scatter(
            grad_out.astype(jnp.bfloat16), "wide", scatter_dimension=0, tiled=True
        ).astype(jnp.float32),
        lax.psum_scatter(
            grad_glu.astype(jnp.bfloat16), "wide", scatter_dimension=0, tiled=True
        ).astype(jnp.float32),
        lax.psum_scatter(
            grad_point.astype(jnp.bfloat16), "wide", scatter_dimension=0, tiled=True
        ).astype(jnp.float32),
    )
    totals = (
        lax.psum(mixer_grads[0].astype(jnp.bfloat16), "utt").astype(jnp.float32),
        lax.psum(mixer_grads[1].astype(jnp.bfloat16), "utt").astype(jnp.float32),
        lax.psum(mixer_grads[2].astype(jnp.bfloat16), "utt").astype(jnp.float32),
        lax.psum(mixer_grads[3].astype(jnp.bfloat16), "utt").astype(jnp.float32),
        lax.psum(mixer_grads[4].astype(jnp.bfloat16), "utt").astype(jnp.float32),
        lax.psum(mixer_grads[5].astype(jnp.bfloat16), "utt").astype(jnp.float32),
        lax.psum(grad_place_w.astype(jnp.bfloat16), "utt").astype(jnp.float32),
        lax.psum(grad_content.astype(jnp.bfloat16), "utt").astype(jnp.float32),
        lax.psum(grad_place_b.astype(jnp.bfloat16), "utt").astype(jnp.float32),
    )
    small_grads = lax.psum(
        (
            grad_first_gain,
            grad_attn_gain,
            grad_conv_gain,
            grad_middle_gain,
            grad_second_gain,
            grad_final_gain,
            grad_kernel,
        ),
        ("utt", "wide"),
    )
    grad_input = grad0.astype(jnp.bfloat16).reshape(groups, frames_dev, channels)
    return (
        output,
        grad_input,
        small_grads[0],
        summed_first[0],
        summed_first[1],
        small_grads[1],
        totals[0],
        totals[1],
        totals[2],
        totals[3],
        totals[6],
        totals[7],
        totals[8],
        small_grads[2],
        totals[4],
        small_grads[6],
        small_grads[3],
        totals[5],
        small_grads[4],
        summed_second[0],
        summed_second[1],
        small_grads[5],
    )


def solution(mesh):
    shape = dict(mesh.shape)
    if shape["wide"] == 4 and shape["utt"] % 4 == 0:
        mesh = jax.sharding.Mesh(
            mesh.devices.reshape(shape["utt"] // 2, 2, 2, 2), ("z", "core", "y", "x")
        )
        utt, wide, body = ("z", "core"), ("y", "x"), per_chip
    else:
        utt, wide, body = "utt", "wide", per_device
    every = (utt, wide) if utt == "utt" else (*utt, *wide)
    in_specs = (
        P(utt, wide, None),
        P(utt),
        P(utt, wide),
        P(utt, wide, None),
        P(),
        P(every, None),
        P(every, None),
        P(),
        P(wide, None),
        P(wide, None),
        P(wide, None),
        P(wide, None),
        P(wide, None),
        P(wide),
        P(wide),
        P(),
        P(wide, None),
        P(),
        P(),
        P(wide, None),
        P(),
        P(every, None),
        P(every, None),
        P(),
    )
    out_specs = (
        P(utt, wide, None),
        P(utt, wide, None),
        P(),
        P(every, None),
        P(every, None),
        P(),
        P(wide, None),
        P(wide, None),
        P(wide, None),
        P(wide, None),
        P(wide, None),
        P(wide),
        P(wide),
        P(),
        P(wide, None),
        P(),
        P(),
        P(wide, None),
        P(),
        P(every, None),
        P(every, None),
        P(),
    )
    return jax.shard_map(
        body, mesh=mesh, in_specs=in_specs, out_specs=out_specs, check_vma=False
    )
```

```python
from functools import partial
import math

import jax
import jax.numpy as jnp
from jax import lax
from jax.experimental import pallas as pl
from jax.experimental.pallas import tpu as pltpu
from jax.sharding import PartitionSpec as P

HEAD_DIM = 64
KERNEL = 31
QBLK = 512
RIM = 15
PAIR = 128
ROWS_FWD = 512
ROWS_BWD = 256
VMEM = 56 * 2**20


EPSILON = 1e-05
MASKED_SCORE = -1e30


def with_halo(block, sides, width):
    for axis, dim in sides:
        count = lax.axis_size(axis)
        forward = [(i, i + 1) for i in range(count - 1)]
        backward = [(target, source) for source, target in forward]
        low = lax.ppermute(
            lax.slice_in_dim(block, block.shape[dim] - width, None, axis=dim), axis, forward
        )
        high = lax.ppermute(lax.slice_in_dim(block, 0, width, axis=dim), axis, backward)
        block = jnp.concatenate([low, block, high], axis=dim)
    return block


def norm_rows(values, gain_vec):
    average = jnp.mean(values, axis=-1, keepdims=True)
    centred = values - average
    spread = jnp.mean(centred * centred, axis=-1, keepdims=True)
    return centred * lax.rsqrt(spread + EPSILON) * gain_vec


def silu_slope(before):
    squash = jax.nn.sigmoid(before)
    return squash * (1.0 + before * (1.0 - squash))


def mult_trans(first_mat, second_mat):
    return lax.dot_general(
        first_mat, second_mat, (((1,), (1,)), ((), ())), preferred_element_type=jnp.float32
    )


def mult_plain(first_mat, second_mat):
    return jnp.dot(first_mat, second_mat, preferred_element_type=jnp.float32)


def mult_rows(first_mat, second_mat):
    return lax.dot_general(
        first_mat, second_mat, (((0,), (0,)), ((), ())), preferred_element_type=jnp.float32
    )


def relative_table(length, channels):
    offsets = length - 1 - jnp.arange(2 * length - 1).astype(jnp.float32)
    rates = jnp.exp(
        jnp.arange(channels // 2).astype(jnp.float32) * (-2.0 * math.log(10000.0) / channels)
    )
    angles = offsets[:, None] * rates[None, :]
    return jnp.concatenate([jnp.sin(angles), jnp.cos(angles)], axis=1)


def skew_rows(reversed_scores):
    block_rows, span = reversed_scores.shape
    flat = reversed_scores.reshape(-1)[block_rows - 1 : block_rows - 1 + block_rows * (span - 1)]
    return flat.reshape(block_rows, span - 1)[:, : span - block_rows + 1]


def unskew_rows(grad_scores, span):
    block_rows, length = grad_scores.shape
    padded = jnp.pad(grad_scores, ((0, 0), (0, span - 1 - length)))
    flat = jnp.pad(padded.reshape(-1), (block_rows - 1, 1))
    return flat.reshape(block_rows, span)


def gather_ffn(up_rows, down_rows):
    return (
        lax.all_gather(up_rows, ("utt", "wide"), axis=0, tiled=True),
        lax.all_gather(down_rows, ("utt", "wide"), axis=0, tiled=True),
    )


def sum_ffn(grad_up, grad_down):
    return (
        lax.psum_scatter(grad_up, ("utt", "wide"), scatter_dimension=0, tiled=True),
        lax.psum_scatter(grad_down, ("utt", "wide"), scatter_dimension=0, tiled=True),
    )


def ffn_forward(stream, gain_vec, up_full, down_full):
    normed, norm_pull = jax.vjp(norm_rows, stream, gain_vec)
    normed_low = normed.astype(jnp.bfloat16)
    before = mult_trans(normed_low, up_full)
    active_low = jax.nn.silu(before).astype(jnp.bfloat16)
    return (
        stream + 0.5 * mult_plain(active_low, down_full),
        (norm_pull, normed_low, before, active_low),
    )


def ffn_backward(grad_stream, saved_ffn, up_full, down_full):
    norm_pull, normed_low, before, active_low = saved_ffn
    grad_out = (0.5 * grad_stream).astype(jnp.bfloat16)
    grad_down = mult_rows(active_low, grad_out)
    grad_before = (mult_trans(grad_out, down_full) * silu_slope(before)).astype(jnp.bfloat16)
    grad_up = mult_rows(grad_before, normed_low)
    grad_input, grad_gain = norm_pull(mult_plain(grad_before, up_full))
    return (grad_stream + grad_input, grad_gain, grad_up, grad_down)


def head_forward(
    query_rows,
    key_rows,
    value_rows,
    place_rows,
    bias_first,
    bias_second,
    key_ok,
    block_rows,
    score_scale,
):
    length, head_width = query_rows.shape
    with_u = (query_rows.astype(jnp.float32) + bias_first).astype(jnp.bfloat16)
    with_v = (query_rows.astype(jnp.float32) + bias_second).astype(jnp.bfloat16)

    def one_block(block_index):
        first_row = block_index * block_rows
        block_u = lax.dynamic_slice_in_dim(with_u, first_row, block_rows, 0)
        block_v = lax.dynamic_slice_in_dim(with_v, first_row, block_rows, 0)
        near_rows = lax.dynamic_slice_in_dim(
            place_rows, length - block_rows - first_row, block_rows + length - 1, 0
        )
        scores = (
            mult_trans(block_u, key_rows) + skew_rows(mult_trans(block_v, near_rows))
        ) * score_scale
        scores = jnp.where(key_ok[None, :], scores, MASKED_SCORE)
        highest = jnp.max(scores, axis=1, keepdims=True)
        weights = jnp.exp(scores - highest)
        running = jnp.sum(weights, axis=1, keepdims=True)
        attend_prob = (weights / running).astype(jnp.bfloat16)
        return (
            mult_plain(attend_prob, value_rows).astype(jnp.bfloat16),
            (highest + jnp.log(running))[:, 0],
        )

    attended, log_total = lax.map(one_block, jnp.arange(length // block_rows, dtype=jnp.int32))
    return (attended.reshape(length, head_width), log_total.reshape(length))


def head_backward(
    query_rows,
    key_rows,
    value_rows,
    place_rows,
    bias_first,
    bias_second,
    key_ok,
    log_total,
    grad_mixed,
    block_rows,
    score_scale,
):
    length, head_width = query_rows.shape
    span = block_rows + length - 1
    with_u = (query_rows.astype(jnp.float32) + bias_first).astype(jnp.bfloat16)
    with_v = (query_rows.astype(jnp.float32) + bias_second).astype(jnp.bfloat16)

    def one_block(carried, block_index):
        grad_key, grad_value, grad_place = carried
        first_row = block_index * block_rows
        place_first = length - block_rows - first_row
        block_u = lax.dynamic_slice_in_dim(with_u, first_row, block_rows, 0)
        block_v = lax.dynamic_slice_in_dim(with_v, first_row, block_rows, 0)
        near_rows = lax.dynamic_slice_in_dim(place_rows, place_first, span, 0)
        block_total = lax.dynamic_slice_in_dim(log_total, first_row, block_rows, 0)
        block_grad = lax.dynamic_slice_in_dim(grad_mixed, first_row, block_rows, 0)
        scores = (
            mult_trans(block_u, key_rows) + skew_rows(mult_trans(block_v, near_rows))
        ) * score_scale
        scores = jnp.where(key_ok[None, :], scores, MASKED_SCORE)
        attend_prob = jnp.exp(scores - block_total[:, None])
        grad_prob = mult_trans(block_grad, value_rows)
        inner = jnp.sum(attend_prob * grad_prob, axis=1, keepdims=True)
        grad_score = jnp.where(key_ok[None, :], attend_prob * (grad_prob - inner), 0.0).astype(
            jnp.bfloat16
        )
        grad_value = grad_value + mult_rows(attend_prob.astype(jnp.bfloat16), block_grad)
        grad_with_u = mult_plain(grad_score, key_rows) * score_scale
        grad_key = grad_key + mult_rows(grad_score, block_u) * score_scale
        spread_grad = unskew_rows(grad_score, span)
        grad_with_v = mult_plain(spread_grad, near_rows) * score_scale
        place_part = (
            lax.dynamic_slice_in_dim(grad_place, place_first, span, 0)
            + mult_rows(spread_grad, block_v) * score_scale
        )
        grad_place = lax.dynamic_update_slice_in_dim(grad_place, place_part, place_first, 0)
        return ((grad_key, grad_value, grad_place), (grad_with_u, grad_with_v))

    zero_rows = jnp.zeros((length, head_width), jnp.float32)
    zero_place = jnp.zeros((2 * length - 1, head_width), jnp.float32)
    (grad_key, grad_value, grad_place), (grad_with_u, grad_with_v) = lax.scan(
        one_block,
        (zero_rows, zero_rows, zero_place),
        jnp.arange(length // block_rows, dtype=jnp.int32),
    )
    grad_with_u = grad_with_u.reshape(length, head_width)
    grad_with_v = grad_with_v.reshape(length, head_width)
    grad_query = (grad_with_u + grad_with_v).astype(jnp.bfloat16)
    return (
        grad_query,
        grad_key.astype(jnp.bfloat16),
        grad_value.astype(jnp.bfloat16),
        grad_place.astype(jnp.bfloat16),
        jnp.sum(grad_with_u, axis=0),
        jnp.sum(grad_with_v, axis=0),
    )


def biased(q_ref, bias_ref, scale):
    return ((q_ref[...].astype(jnp.float32) + bias_ref[...].astype(jnp.float32)).astype(jnp.bfloat16).astype(jnp.float32) * scale).astype(jnp.bfloat16)

def attend_fwd_kernel(len_ref, q_ref, k_ref, v_ref, place_ref, cb_ref, pb_ref, out_ref, prob_ref, *, scale):
    rows = q_ref.shape[0]
    length = k_ref.shape[0]
    span = rows + length
    first = pl.multiple_of(length - rows - pl.program_id(1) * rows, rows)
    lanes = lax.broadcasted_iota(jnp.int32, (rows, PAIR), 1)
    with_u = biased(q_ref, cb_ref, scale)
    with_v = biased(q_ref, pb_ref, scale)
    window = place_ref[pl.ds(first, span), :]
    key_ok = lax.broadcasted_iota(jnp.int32, (rows, length), 1) < len_ref[0]
    zero = jnp.zeros_like(with_u)
    mixed = []
    for head in range(2):
        mine = (lanes // HEAD_DIM) == head
        place_part = mult_trans(jnp.where(mine, with_v, zero), window)
        place_part = pltpu.roll(place_part, span - rows + 1, 1, stride=1, stride_axis=0)
        scores = mult_trans(jnp.where(mine, with_u, zero), k_ref[...]) + place_part[:, :length]
        scores = jnp.where(key_ok, scores, MASKED_SCORE)
        weights = jnp.exp(scores - jnp.max(scores, axis=1, keepdims=True))
        total = jnp.sum(weights, axis=1, keepdims=True)
        prob = (weights * (1.0 / total)).astype(jnp.bfloat16)
        prob_ref[head] = prob
        mixed.append(mult_plain(prob, v_ref[...]))
    out_ref[...] = jnp.where(lanes < HEAD_DIM, mixed[0], mixed[1]).astype(jnp.bfloat16)

def attend_fwd(length_arr, q, k, v, place, cb, pb, rows):
    length, width = q.shape
    pairs = width // PAIR
    return pl.pallas_call(
        partial(attend_fwd_kernel, scale=1.0 / math.sqrt(HEAD_DIM)),
        grid=(pairs, length // rows),
        in_specs=[
            pl.BlockSpec(memory_space=pltpu.SMEM),
            pl.BlockSpec((rows, PAIR), lambda p, i: (i, p)),
            pl.BlockSpec((length, PAIR), lambda p, i: (0, p)),
            pl.BlockSpec((length, PAIR), lambda p, i: (0, p)),
            pl.BlockSpec((2 * length, PAIR), lambda p, i: (0, p)),
            pl.BlockSpec((1, PAIR), lambda p, i: (0, p)),
            pl.BlockSpec((1, PAIR), lambda p, i: (0, p)),
        ],
        out_specs=[
            pl.BlockSpec((rows, PAIR), lambda p, i: (i, p)),
            pl.BlockSpec((2, rows, length), lambda p, i: (p, i, 0)),
        ],
        out_shape=[
            jax.ShapeDtypeStruct((length, width), jnp.bfloat16),
            jax.ShapeDtypeStruct((2 * pairs, length, length), jnp.bfloat16),
        ],
        compiler_params=pltpu.CompilerParams(vmem_limit_bytes=VMEM),
        cost_estimate=pl.CostEstimate(flops=40 * 10**9, bytes_accessed=20 * 2**20, transcendentals=pairs * 2 * length * length),
        name="attend_fwd",
    )(length_arr, q, k, v, place, cb, pb)

def attend_bwd_kernel(q_ref, k_ref, v_ref, place_ref, cb_ref, pb_ref, prob_ref, g_ref, gq_ref, gk_ref, gv_ref, gp_ref, gb_ref, gk_s, gv_s, gp_s, *, scale):
    rows = q_ref.shape[0]
    length = k_ref.shape[0]
    span = rows + length
    step = pl.program_id(1)
    first = pl.multiple_of(length - rows - step * rows, rows)
    lanes = lax.broadcasted_iota(jnp.int32, (rows, PAIR), 1)
    flip = (lax.broadcasted_iota(jnp.int32, (rows, rows), 0) + lax.broadcasted_iota(jnp.int32, (rows, rows), 1) == rows - 1).astype(jnp.bfloat16)
    with_u = biased(q_ref, cb_ref, scale)
    with_v = mult_plain(flip, biased(q_ref, pb_ref, scale)).astype(jnp.bfloat16)
    grad = g_ref[...]
    window = place_ref[pl.ds(first, span), :]
    zero = jnp.zeros_like(with_u)

    @pl.when(step == 0)
    def _():
        gk_s[...] = jnp.zeros_like(gk_s)
        gv_s[...] = jnp.zeros_like(gv_s)
        gp_s[...] = jnp.zeros_like(gp_s)
        gb_ref[...] = jnp.zeros_like(gb_ref)

    grad_t, with_u_t, with_v_t = grad.T, with_u.T, with_v.T
    gu = []
    gw = []
    for head in range(2):
        mine = (lanes // HEAD_DIM) == head
        prob = prob_ref[head]
        grad_h = jnp.where(mine, grad, zero)
        grad_prob = mult_trans(grad_h, v_ref[...])
        weighted = prob.astype(jnp.float32) * grad_prob
        inner = jnp.sum(weighted, axis=1, keepdims=True)
        grad_score = (weighted - prob.astype(jnp.float32) * inner).astype(jnp.bfloat16)
        turned = mult_plain(flip, grad_score).astype(jnp.bfloat16)
        turned = jnp.concatenate([turned, jnp.zeros((rows, rows), jnp.bfloat16)], axis=1)
        turned = pltpu.roll(turned, 0, 1, stride=1, stride_axis=0)
        gu.append(mult_plain(grad_score, k_ref[...]))
        gw.append(mult_plain(turned, window))
        band = slice(head * HEAD_DIM, (head + 1) * HEAD_DIM)
        gv_s[band, :] += mult_plain(grad_t[band, :], prob)
        gk_s[band, :] += mult_plain(with_u_t[band, :], grad_score)
        gp_s[band, pl.ds(first, span)] += mult_plain(with_v_t[band, :], turned)
    grad_u = jnp.where(lanes < HEAD_DIM, gu[0], gu[1]) * scale
    grad_w = jnp.where(lanes < HEAD_DIM, gw[0], gw[1]) * scale
    gb_ref[0:1, :] += jnp.sum(grad_u, axis=0, keepdims=True)
    gb_ref[1:2, :] += jnp.sum(grad_w, axis=0, keepdims=True)
    high = grad_w.astype(jnp.bfloat16)
    rest = (grad_w - high.astype(jnp.float32)).astype(jnp.bfloat16)
    gq_ref[...] = (grad_u + mult_plain(flip, high) + mult_plain(flip, rest)).astype(jnp.bfloat16)

    @pl.when(step == pl.num_programs(1) - 1)
    def _():
        gk_ref[...] = gk_s[...].T.astype(jnp.bfloat16)
        gv_ref[...] = gv_s[...].T.astype(jnp.bfloat16)
        gp_ref[...] = gp_s[...].T.astype(jnp.bfloat16)


def attend_bwd_sum_kernel(layers, shared, count, *refs, scale):
    ins, parts = refs[:8], refs[8 : 8 + count]
    refs = refs[8 + count :]
    outs, sums, scratch, own = refs[:5], refs[5 : 5 + count], refs[5 + count : 8 + count], refs[8 + count :]
    at = pl.program_id(0) * pl.num_programs(1) + pl.program_id(1)
    enter, step, turns, leave = reduce_plan(layers, shared, parts, sums, None, own)
    blocks = pl.num_programs(0) * pl.num_programs(1)
    pl.when(at == 0)(enter)
    for turn_at in range(min(turns, blocks)):
        pl.when(at == turn_at)(partial(step, turn_at))
    attend_bwd_kernel(*ins, *outs, *scratch, scale=scale)

    @pl.when(at == blocks - 1)
    def _():
        for turn_at in range(blocks, turns):
            step(turn_at)
        leave()


def attend_bwd(q, k, v, place, cb, pb, prob, grad, rows, layers, shared, parts, collective_id):
    length, width = q.shape
    pairs = width // PAIR
    count = len(parts)
    blocks, shapes = reduce_shapes(layers, shared, parts)
    shard, channels = shapes[shared].shape[2:]
    still = lambda shape: pl.BlockSpec(shape, lambda p, i: (0,) * len(shape))
    full = pl.BlockSpec((length, PAIR), lambda p, i: (0, p))
    part = pl.BlockSpec((rows, PAIR), lambda p, i: (i, p))
    vec = pl.BlockSpec((1, PAIR), lambda p, i: (0, p))
    tall = pl.BlockSpec((2 * length, PAIR), lambda p, i: (0, p))
    return pl.pallas_call(
        partial(attend_bwd_sum_kernel, layers, shared, count, scale=1.0 / math.sqrt(HEAD_DIM)),
        grid=(pairs, length // rows),
        in_specs=[
            part,
            full,
            full,
            tall,
            vec,
            vec,
            pl.BlockSpec((2, rows, length), lambda p, i: (p, i, 0)),
            part,
        ]
        + [pl.BlockSpec(memory_space=pl.ANY)] * count,
        out_specs=[part, full, full, tall, pl.BlockSpec((8, PAIR), lambda p, i: (0, p))]
        + [still(shape.shape) for shape in shapes],
        out_shape=[
            jax.ShapeDtypeStruct((length, width), jnp.bfloat16),
            jax.ShapeDtypeStruct((length, width), jnp.bfloat16),
            jax.ShapeDtypeStruct((length, width), jnp.bfloat16),
            jax.ShapeDtypeStruct((2 * length, width), jnp.bfloat16),
            jax.ShapeDtypeStruct((8, width), jnp.float32),
        ]
        + shapes,
        scratch_shapes=[
            pltpu.VMEM((PAIR, length), jnp.float32),
            pltpu.VMEM((PAIR, length), jnp.float32),
            pltpu.VMEM((PAIR, 2 * length), jnp.float32),
        ]
        + reduce_scratch(count, layers, shard, channels),
        compiler_params=pltpu.CompilerParams(
            vmem_limit_bytes=VMEM, collective_id=collective_id, has_side_effects=True
        ),
        cost_estimate=pl.CostEstimate(
            flops=100 * 10**9, bytes_accessed=40 * 2**20, transcendentals=0
        ),
        name="attend_bwd",
    )(
        q,
        k,
        v,
        place,
        cb,
        pb,
        prob,
        grad,
        *blocks,
    )


MESH = pl.DeviceIdType.MESH


def chip_place(layers):
    z, c, y, x = (lax.axis_index(axis) for axis in ("z", "core", "y", "x"))

    def at(dz=0, dc=0, dy=0, dx=0):
        return (
            lax.rem(z + dz, layers),
            lax.rem(c + dc, 2),
            lax.rem(y + dy, 2),
            lax.rem(x + dx, 2),
        )

    def spot(dz=0, dc=0, dy=0, dx=0):
        return at(layers - dz, dc, dy, dx)

    return at, spot


def greet(at, layers):
    barrier = pltpu.get_barrier_semaphore()
    peers = [at(dz=k) for k in range(1, layers)] + [at(dc=1), at(dy=1), at(dx=1)]
    for peer in peers:
        pl.semaphore_signal(barrier, inc=1, device_id=peer, device_id_type=MESH)
    pl.semaphore_wait(barrier, len(peers))


def remote(source, target, sems, index, device):
    return pltpu.make_async_remote_copy(
        src_ref=source,
        dst_ref=target,
        send_sem=sems.at[(0, *index)],
        recv_sem=sems.at[(1, *index)],
        device_id=device,
        device_id_type=MESH,
    )


def far_first(layers):
    return sorted(range(1, layers), key=lambda k: -min(k, layers - k)) + [0]


def gather_plan(layers, shards, fulls, z_sem, p_sem, d_sem, c_sem, own_sem):
    at, spot = chip_place(layers)
    arrays = range(len(shards))
    half = shards[0].shape[0] // 2
    items = [(dz, a) for dz in reversed(far_first(layers)) for a in arrays]
    own = [pltpu.make_async_copy(shards[a], fulls[a].at[spot()], own_sem.at[a]) for a in arrays]
    along, flat, cross, core = {}, {}, {}, {}
    for dz, a in items:
        full = fulls[a]
        source = full.at[spot(dz)] if dz else shards[a]
        if dz:
            along[dz, a] = remote(shards[a], full.at[spot()], z_sem, (a, dz), at(dz=dz))
        flat[dz, a] = (
            remote(source, full.at[spot(dz)], p_sem, (a, dz, 0), at(dx=1)),
            remote(source, full.at[spot(dz)], p_sem, (a, dz, 1), at(dy=1)),
        )
        from_x = full.at[(*spot(dz, dx=1), pl.ds(half, half))]
        from_y = full.at[(*spot(dz, dy=1), pl.ds(0, half))]
        cross[dz, a] = (
            remote(from_x, from_x, d_sem, (a, dz, 0), at(dy=1)),
            remote(from_y, from_y, d_sem, (a, dz, 1), at(dx=1)),
        )
        plane = full.at[spot(dz)[:2]]
        core[dz, a] = remote(plane, plane, c_sem, (a, dz), at(dc=1))

    def enter():
        greet(at, layers)
        for dz in far_first(layers)[:-1]:
            for a in arrays:
                along[dz, a].start()
        for copy in own:
            copy.start()

    def spread(item):
        if item[0]:
            along[item].wait_recv()
        for copy in flat[item]:
            copy.start()

    def turn(item):
        for got, out in zip(flat[item], cross[item]):
            got.wait_recv()
            out.start()

    def share(item):
        for got in cross[item]:
            got.wait_recv()
        if not item[0]:
            own[item[1]].wait()
        core[item].start()

    steps = []
    for turn_at in range(len(items) + 4):
        for action, lag in ((spread, 0), (turn, 2), (share, 4)):
            if 0 <= turn_at - lag < len(items):
                steps.append(partial(action, items[turn_at - lag]))

    def leave():
        for item in items:
            core[item].wait_recv()
        for item in items:
            if item[0]:
                along[item].wait_send()
            for copy in (*flat[item], *cross[item], core[item]):
                copy.wait_send()

    return enter, steps, leave


def gather_sems(count, layers):
    dma = pltpu.SemaphoreType.DMA
    return [
        dma((2, count, layers)),
        dma((2, count, layers, 2)),
        dma((2, count, layers, 2)),
        dma((2, count, layers)),
        dma((count,)),
    ]


def gather_kernel(layers, count, *refs):
    enter, steps, leave = gather_plan(layers, refs[:count], refs[count : 2 * count], *refs[2 * count :])
    enter()
    for step in steps:
        step()
    leave()


def gather_all(layers, shards, collective_id):
    count = len(shards)
    rows, width = shards[0].shape
    fulls = pl.pallas_call(
        partial(gather_kernel, layers, count),
        in_specs=[pl.BlockSpec(memory_space=pl.ANY)] * count,
        out_specs=[pl.BlockSpec(memory_space=pl.ANY)] * count,
        out_shape=[jax.ShapeDtypeStruct((layers, 2, 2, 2, rows, width), jnp.bfloat16)] * count,
        scratch_shapes=gather_sems(count, layers),
        compiler_params=pltpu.CompilerParams(collective_id=collective_id, has_side_effects=True),
        cost_estimate=pl.CostEstimate(flops=0, bytes_accessed=200 * 2**20, transcendentals=0),
        name="gather_all",
    )(*shards)
    return [full.reshape(8 * layers * rows, width) for full in fulls]


def add_rows(target, one, two):
    target[...] = (one[...].astype(jnp.float32) + two[...].astype(jnp.float32)).astype(target.dtype)


def reduce_plan(layers, shared, parts, outs, small, scratch):
    at, spot = chip_place(layers)
    sums, got_c, got_d, got_p, got_z, got_s, load_sem, c_sem, d_sem, p_sem, z_sem, s_sem, *tiny = scratch
    arrays = range(len(parts))
    rows = sums.shape[4]
    half = rows // 2
    order = far_first(layers)
    items = [(dz, shared) for dz in order]
    items += [(dz, a) for dz in order for a in arrays if a != shared]
    first, second = pl.ds(0, half), pl.ds(half, half)
    here, by_y, by_x, far = (spot(0, 0, dy, dx)[2:] for dy, dx in ((0, 0), (1, 0), (0, 1), (1, 1)))
    whole = [len(part.shape) == 6 for part in parts]
    core_at = spot()[1]
    load, core, cross, flat, along = {}, {}, {}, {}, {}
    for dz, a in items:
        total = sums.at[a, dz]
        source = parts[a].at[spot(dz)[:2]] if whole[a] else parts[a].at[spot(dz)[0]]
        load[dz, a] = pltpu.make_async_copy(source, total, load_sem.at[a, dz])
        if whole[a]:
            core[dz, a] = remote(
                parts[a].at[spot(dz, dc=1)[:2]], got_c.at[a, dz], c_sem, (a, dz), at(dc=1)
            )
        cross[dz, a] = (
            remote(total.at[(*far, first)], got_d.at[a, dz, 0], d_sem, (a, dz, 0), at(dx=1)),
            remote(total.at[(*far, second)], got_d.at[a, dz, 1], d_sem, (a, dz, 1), at(dy=1)),
        )
        flat[dz, a] = (
            remote(total.at[by_y], got_p.at[a, dz, 0], p_sem, (a, dz, 0), at(dy=1)),
            remote(total.at[by_x], got_p.at[a, dz, 1], p_sem, (a, dz, 1), at(dx=1)),
        )
        if dz:
            along[dz, a] = remote(
                total.at[here], got_z.at[a, dz], z_sem, (a, dz), at(dz=layers - dz)
            )
    own = got_s.at[(core_at, spot()[0])]
    handed = {k: remote(own, own, s_sem, (k,), at(dz=k)) for k in range(1, layers)}
    swapped = remote(got_s.at[core_at], got_s.at[core_at], s_sem, (0,), at(dc=1))
    hops = []
    if small:
        level, got_t, t_sem = tiny
        hops = [
            remote(level.at[i], got_t.at[i], t_sem, (i,), device)
            for i, device in enumerate((at(dc=1), at(dx=1), at(dy=1)))
        ]
        hops += [
            remote(level.at[3], got_t.at[2 + k], t_sem, (2 + k,), at(dz=k)) for k in range(1, layers)
        ]

    def enter():
        greet(at, layers)
        if small:
            level[0] = small[0][...]
            hops[0].start()
        for item in items:
            if item in core:
                core[item].start()
            load[item].start()

    def join_core(item):
        dz, a = item
        load[item].wait()
        if whole[a]:
            core[item].wait_recv()
        for place in (far, by_y, by_x, here):
            target = sums.at[(a, dz, *place)]
            if whole[a]:
                add_rows(target, target, got_c.at[(a, dz, *place)])
            if place is far:
                for copy in cross[item]:
                    copy.start()

    def join_cross(item):
        dz, a = item
        one, two = sums.at[(a, dz, *by_y, first)], sums.at[(a, dz, *by_x, second)]
        cross[item][0].wait_recv()
        add_rows(one, one, got_d.at[a, dz, 0])
        flat[item][0].start()
        cross[item][1].wait_recv()
        add_rows(two, two, got_d.at[a, dz, 1])
        flat[item][1].start()

    def join_flat(item):
        dz, a = item
        target = sums.at[(a, dz, *here)]
        for copy in flat[item]:
            copy.wait_recv()
        target[...] = (
            target[...].astype(jnp.float32)
            + got_p[a, dz, 0].astype(jnp.float32)
            + got_p[a, dz, 1].astype(jnp.float32)
        ).astype(jnp.bfloat16)
        if dz:
            along[item].start()

    def total_of(a):
        total = sums[(a, 0, *here)].astype(jnp.float32)
        for dz in range(1, layers):
            along[dz, a].wait_recv()
            total = total + got_z[a, dz].astype(jnp.float32)
        return total

    def join_small(turn_at):
        if turn_at < 3:
            hops[turn_at].wait_recv()
            level[turn_at + 1] = level[turn_at] + got_t[turn_at]
            for hop in hops[turn_at + 1 : turn_at + 2] if turn_at < 2 else hops[3:]:
                hop.start()
        else:
            total = level[3]
            for k in range(1, layers):
                hops[2 + k].wait_recv()
                total = total + got_t[2 + k]
            small[1][...] = total

    def hand_on():
        own[...] = total_of(shared).astype(jnp.bfloat16)
        for copy in handed.values():
            copy.start()

    def swap():
        for copy in handed.values():
            copy.wait_recv()
        swapped.start()

    handed_at = layers - 1 + 5 + 2
    turns = max(len(items) + 5, handed_at + 4)

    def step(turn_at):
        for action, lag in ((join_core, 0), (join_cross, 3), (join_flat, 5)):
            if 0 <= turn_at - lag < len(items):
                action(items[turn_at - lag])
        if small and 1 <= turn_at <= 4:
            join_small(turn_at - 1)
        if turn_at == handed_at:
            hand_on()
        if turn_at == handed_at + 3:
            swap()

    def leave():
        for a in arrays:
            if a != shared:
                outs[a][...] = total_of(a)
        swapped.wait_recv()
        outs[shared][...] = got_s[...]
        for item in items:
            if item[0]:
                along[item].wait_send()
            for copy in (*cross[item], *flat[item]):
                copy.wait_send()
            if item in core:
                core[item].wait_send()
        for copy in (*handed.values(), swapped, *hops):
            copy.wait_send()

    return enter, step, turns, leave


def reduce_scratch(count, layers, rows, width, small=None):
    dma = pltpu.SemaphoreType.DMA
    low = lambda *shape: pltpu.VMEM((count, layers, *shape, width), jnp.bfloat16)
    scratch = [
        low(2, 2, rows),
        low(2, 2, rows),
        low(2, rows // 2),
        low(2, rows),
        low(rows),
        pltpu.VMEM((2, layers, rows, width), jnp.bfloat16),
        dma((count, layers)),
        dma((2, count, layers)),
        dma((2, count, layers, 2)),
        dma((2, count, layers, 2)),
        dma((2, count, layers)),
        dma((2, layers)),
    ]
    if small is not None:
        scratch += [
            pltpu.VMEM((4, *small.shape), jnp.float32),
            pltpu.VMEM((2 + layers, *small.shape), jnp.float32),
            dma((2, 2 + layers)),
        ]
    return scratch


def reduce_shapes(layers, shared, parts):
    blocks, shapes = [], []
    for a, (part, count) in enumerate(parts):
        width = part.shape[-1]
        rows = part.size // width // (4 * count * layers)
        blocks.append(part.reshape(layers, *((2,) if count == 2 else ()), 2, 2, rows, width))
        if a == shared:
            shapes.append(jax.ShapeDtypeStruct((2, layers, rows, width), jnp.bfloat16))
        else:
            shapes.append(jax.ShapeDtypeStruct((rows, width), jnp.float32))
    return blocks, shapes


def reduce_kernel(layers, shared, count, *refs):
    parts, small, outs, total = refs[:count], refs[count], refs[count + 1 : 2 * count + 1], refs[2 * count + 1]
    enter, step, turns, leave = reduce_plan(
        layers, shared, parts, outs, (small, total), refs[2 * count + 2 :]
    )
    enter()
    for turn_at in range(turns):
        step(turn_at)
    leave()


def reduce_all(layers, shared, parts, small, collective_id):
    count = len(parts)
    blocks, shapes = reduce_shapes(layers, shared, parts)
    rows, width = shapes[shared].shape[2:]
    near = pl.BlockSpec(memory_space=pltpu.VMEM)
    return pl.pallas_call(
        partial(reduce_kernel, layers, shared, count),
        in_specs=[pl.BlockSpec(memory_space=pl.ANY)] * count + [near],
        out_specs=[near] * (count + 1),
        out_shape=shapes + [jax.ShapeDtypeStruct(small.shape, jnp.float32)],
        scratch_shapes=reduce_scratch(count, layers, rows, width, small),
        compiler_params=pltpu.CompilerParams(
            collective_id=collective_id, has_side_effects=True, vmem_limit_bytes=VMEM
        ),
        cost_estimate=pl.CostEstimate(flops=0, bytes_accessed=300 * 2**20, transcendentals=0),
        name="reduce_all",
    )(*blocks, small)


class Hops:
    def __init__(self, layers):
        self.layers = layers

    def send(self, block, dz=0, dc=0, dy=0, dx=0):
        pairs = []
        for z in range(self.layers):
            for c in range(2):
                for w in range(4):
                    to = ((z + dz) % self.layers * 2 + (c ^ dc)) * 4 + (w ^ (2 * dy + dx))
                    pairs.append(((z * 2 + c) * 4 + w, to))
        return lax.ppermute(block, ("z", "core", "y", "x"), pairs)

    def turn(self, block, step):
        pairs = []
        for z in range(self.layers):
            for c in range(2):
                for w in range(4):
                    to = (z * 2 + w // 2) * 4 + 2 * c + ((w % 2) ^ step)
                    pairs.append(((z * 2 + c) * 4 + w, to))
        return lax.ppermute(block, ("z", "core", "y", "x"), pairs)


def relative_waves(length, channels):
    step = 32
    rates = jnp.exp(
        jnp.arange(channels // 2).astype(jnp.float32) * (-2.0 * math.log(10000.0) / channels)
    )
    coarse = (length - 1 - step * jnp.arange(2 * length // step)).astype(jnp.float32)
    fine = jnp.arange(step).astype(jnp.float32)
    coarse, fine = coarse[:, None, None] * rates, fine[None, :, None] * rates
    sin_c, cos_c, sin_f, cos_f = jnp.sin(coarse), jnp.cos(coarse), jnp.sin(fine), jnp.cos(fine)
    return jnp.concatenate(
        [sin_c * cos_f - cos_c * sin_f, cos_c * cos_f + sin_c * sin_f], axis=2
    ).reshape(2 * length, channels)


def taps_forward(padded, kernel_f, count):
    total = jnp.zeros((count, padded.shape[1]), jnp.float32)
    for offset in range(KERNEL):
        total = total + padded[offset : offset + count] * kernel_f[offset]
    return total


def with_rim(hops, block, core):
    edge = jnp.where(core == 0, block[-16:], block[:16])
    got = hops.send(edge, dc=1)
    zero = jnp.zeros_like(got)
    low = jnp.where(core == 0, zero, got)[1:]
    high = jnp.where(core == 0, got, zero)[:RIM]
    return jnp.concatenate([low, block, high])


def per_chip(
    frames,
    lengths,
    masked,
    cotangent,
    first_gain,
    first_up,
    first_down,
    attn_gain,
    query_weight,
    key_weight,
    value_weight,
    out_weight,
    place_weight,
    content_bias,
    place_bias,
    conv_gain,
    glu_weight,
    depth_kernel,
    middle_gain,
    point_weight,
    second_gain,
    second_up,
    second_down,
    final_gain,
):
    core, y, x = lax.axis_index("core"), lax.axis_index("y"), lax.axis_index("x")
    wide_at = 2 * y + x
    layers = lax.axis_size("z")
    hops = Hops(layers)
    groups, quarter, channels = frames.shape
    rows = groups * quarter
    length = 2 * rows
    f32 = lambda v: v.astype(jnp.float32)
    low = lambda v: v.astype(jnp.bfloat16)

    def pick(flag, one, two):
        return jnp.where(flag, one, two), jnp.where(flag, two, one)

    def turn_in(block):
        swap = [lax.dynamic_index_in_dim(block, x ^ step, 0, keepdims=False) for step in range(2)]
        got = [hops.turn(swap[step], step) for step in range(2)]
        return jnp.concatenate(pick(x == 0, *got))

    def turn_out(block):
        parts = pick(x == 0, block[:quarter], block[quarter:])
        got = [hops.turn(parts[step], step) for step in range(2)]
        return jnp.stack(pick(x == 0, *got))

    frames_own = turn_in(frames)
    up_first, down_first = gather_all(layers, [first_up, first_down], 1)
    positions = wide_at * quarter + jnp.arange(quarter, dtype=jnp.int32)
    seed_weight = f32(masked) * f32(positions[None, :] < lengths[:, None])
    seed_own_low = low(f32(cotangent) * seed_weight[:, :, None])
    near_lengths = jnp.where(core == y, lengths, hops.send(lengths, dc=1))
    own_length = lax.dynamic_slice_in_dim(near_lengths, x, 1)
    own_rows = core * rows + jnp.arange(rows, dtype=jnp.int32)
    frame_ok = f32(own_rows < own_length[0])[:, None]

    def own_half(weight):
        count = weight.shape[0] // 2
        return lax.dynamic_slice_in_dim(weight, core * count, count)

    band = query_weight.shape[0] // 2
    own_bias = own_half(jnp.stack([content_bias, place_bias], axis=1)).T
    attn_chunk = jnp.concatenate(
        [
            own_half(query_weight),
            own_half(key_weight),
            own_half(value_weight),
            own_half(place_weight),
            jnp.pad(own_bias, ((0, 14), (0, channels - band))),
        ]
    )
    conv_chunk = jnp.concatenate([own_half(out_weight), own_half(point_weight), own_half(glu_weight)])
    attn_all = lax.all_gather(attn_chunk, ("y", "x"), axis=0)
    conv_all = lax.all_gather(conv_chunk, ("y", "x"), axis=0)
    up_second, down_second = (
        lax.all_gather(shard, ("z", "core", "y", "x"), axis=0, tiled=True)
        for shard in (second_up, second_down)
    )

    def heads_of(at):
        return attn_all[:, at * band : (at + 1) * band].reshape(4 * band, channels)

    query_own, key_own, value_own, place_own = (heads_of(at) for at in range(4))
    own_biases = attn_all[:, 4 * band : 4 * band + 2, :band].transpose(1, 0, 2).reshape(2, 4 * band)
    conv_other = hops.send(conv_all, dc=1)
    conv_both = jnp.stack(pick(core == 0, conv_all, conv_other), axis=1)
    full_out = conv_both[:, :, :band].reshape(8 * band, channels)
    full_point = conv_both[:, :, band : 2 * band].reshape(8 * band, channels)
    full_glu = conv_both[:, :, 2 * band :].reshape(16 * band, channels)

    stream0 = f32(frames_own)
    stream1, saved_first = ffn_forward(stream0, f32(first_gain), up_first, down_first)
    normed_attn, attn_pull = jax.vjp(norm_rows, stream1, f32(attn_gain))
    attn_half = low(normed_attn)
    attn_other = hops.send(attn_half, dc=1)
    attn_low = jnp.concatenate(pick(core == 0, attn_half, attn_other))
    rel_table = low(relative_waves(length, channels))
    query = low(mult_trans(attn_low, query_own))
    key = low(mult_trans(attn_low, key_own))
    value = low(mult_trans(attn_low, value_own))
    place = low(mult_trans(rel_table, place_own))
    attended, prob = attend_fwd(
        own_length, query, key, value, place, own_biases[:1], own_biases[1:], ROWS_FWD
    )

    def halves(matrix):
        own = lax.dynamic_slice_in_dim(matrix, core * rows, rows)
        other = lax.dynamic_slice_in_dim(matrix, (1 - core) * rows, rows)
        return own, other

    att_own, att_other = halves(attended)
    att_parts = pick(core == 0, att_own, hops.send(att_other, dc=1))
    framed = jnp.stack([part.reshape(rows, 4, band) for part in att_parts], axis=2)
    framed = framed.reshape(rows, 8 * band)
    stream2 = stream1 + mult_plain(framed, full_out)
    normed_conv, conv_pull = jax.vjp(norm_rows, stream2, f32(conv_gain))
    conv_low = low(normed_conv)
    glu_in = mult_trans(conv_low, full_glu)
    linear = glu_in[:, :channels]
    gating = jax.nn.sigmoid(glu_in[:, channels:])
    gated = low(linear * gating * frame_ok)
    padded = with_rim(hops, gated, core)
    kernel_f = f32(depth_kernel)
    conv_out = taps_forward(padded, kernel_f, rows)
    middle, middle_pull = jax.vjp(norm_rows, conv_out, f32(middle_gain))
    swished = low(jax.nn.silu(middle))
    stream3 = stream2 + mult_trans(swished, full_point)
    stream4, saved_second = ffn_forward(stream3, f32(second_gain), up_second, down_second)
    final_rows, final_pull = jax.vjp(norm_rows, stream4, f32(final_gain))
    output = turn_out(low(final_rows))

    seed_own = turn_in(seed_own_low)
    grad4, grad_final_gain = final_pull(f32(seed_own))

    def ffn_back(grad_stream, saved_ffn, up_full, down_full):
        norm_pull, normed_low, before, active_low = saved_ffn
        grad_out = low(0.5 * grad_stream)
        grad_down = low(mult_rows(active_low, grad_out))
        grad_before = low(mult_trans(grad_out, down_full) * silu_slope(before))
        grad_up = low(mult_rows(grad_before, normed_low))
        grad_input, grad_gain = norm_pull(mult_plain(grad_before, up_full))
        return grad_stream + grad_input, grad_gain, grad_up, grad_down

    grad3, grad_second_gain, grad_up_second, grad_down_second = ffn_back(
        grad4, saved_second, up_second, down_second
    )
    grad_branch = low(grad3)
    grad_point = mult_rows(grad_branch, swished)
    grad_middle = mult_plain(grad_branch, full_point) * silu_slope(middle)
    grad_conv, grad_middle_gain = middle_pull(grad_middle)
    conv_grad_low = low(grad_conv)
    grad_padded = with_rim(hops, conv_grad_low, core)
    grad_gated = taps_forward(grad_padded, kernel_f[::-1], rows)
    grad_kernel = jnp.stack(
        [
            jnp.sum(f32(padded[offset : offset + rows]) * f32(conv_grad_low), axis=0)
            for offset in range(KERNEL)
        ]
    )
    grad_gated = grad_gated * frame_ok
    grad_glu_in = low(
        jnp.concatenate(
            [grad_gated * gating, grad_gated * linear * gating * (1.0 - gating)], axis=1
        )
    )
    grad_glu = mult_rows(grad_glu_in, conv_low)
    grad_conv_in, grad_conv_gain = conv_pull(mult_plain(grad_glu_in, full_glu))
    grad2 = grad3 + grad_conv_in
    grad_attn = low(grad2)
    grad_out = mult_rows(framed, grad_attn)
    grad_framed = low(mult_trans(grad_attn, full_out))
    grad_parts = grad_framed.reshape(rows, 4, 2, band)
    grad_parts = [grad_parts[:, :, at].reshape(rows, 4 * band) for at in range(2)]
    grad_kept, grad_sent = pick(core == 0, *grad_parts)
    grad_heads = jnp.concatenate(pick(core == 0, grad_kept, hops.send(grad_sent, dc=1)))

    def by_place(matrix, cores):
        blocks = low(matrix).reshape(4, cores, layers, -1, channels)
        return blocks.transpose(2, 1, 0, 3, 4)

    conv_part = jnp.concatenate(
        [by_place(part, 2) for part in (grad_out, grad_point, grad_glu)], axis=3
    )
    *attn_grads, sum_up_second, sum_down_second, conv_sums = attend_bwd(
        query,
        key,
        value,
        place,
        own_biases[:1],
        own_biases[1:],
        prob,
        grad_heads,
        ROWS_BWD,
        layers,
        2,
        [(grad_up_second, 2), (grad_down_second, 2), (conv_part, 2)],
        3,
    )
    grad_query, grad_key, grad_value, grad_place, grad_biases = attn_grads
    grad_query_w = mult_rows(grad_query, attn_low)
    grad_key_w = mult_rows(grad_key, attn_low)
    grad_value_w = mult_rows(grad_value, attn_low)
    grad_place_w = mult_rows(grad_place, rel_table)
    grad_normed = (
        mult_plain(grad_query, query_own)
        + mult_plain(grad_key, key_own)
        + mult_plain(grad_value, value_own)
    )
    normed_own, normed_other = halves(grad_normed)
    grad_attn_in, grad_attn_gain = attn_pull(normed_own + f32(hops.send(low(normed_other), dc=1)))
    grad1 = grad2 + grad_attn_in
    grad0, grad_first_gain, grad_up_first, grad_down_first = ffn_back(
        grad1, saved_first, up_first, down_first
    )
    grad_input = turn_out(low(grad0))

    attn_part = jnp.concatenate(
        [by_place(part, 1) for part in (grad_query_w, grad_key_w, grad_value_w, grad_place_w)],
        axis=3,
    )
    spread = jnp.zeros((2, 4, 2, band), jnp.float32)
    spread = lax.dynamic_update_slice(
        spread, grad_biases[:2].reshape(2, 4, 1, band), (0, 0, core, 0)
    ).reshape(2, channels)
    gains = (
        grad_conv_gain,
        grad_middle_gain,
        grad_second_gain,
        grad_final_gain,
        grad_first_gain,
        grad_attn_gain,
    )
    small = jnp.concatenate([jnp.stack(gains), spread, grad_kernel])
    small = jnp.pad(small, ((0, -small.shape[0] % 8), (0, 0)))
    sum_up_first, sum_down_first, attn_sums, small = reduce_all(
        layers, 2, [(grad_up_first, 2), (grad_down_first, 2), (attn_part, 1)], small, 2
    )

    def owned(sums, start, count):
        return f32(sums[:, :, start : start + count]).reshape(-1, channels)

    step = band // layers
    total_out, total_point = owned(conv_sums, 0, step), owned(conv_sums, step, step)
    total_glu = owned(conv_sums, 2 * step, 2 * step)
    total_query, total_key, total_value, total_place = (
        owned(attn_sums, at * step, step) for at in range(4)
    )
    own_bias_grad = lax.dynamic_slice_in_dim(small[6:8], wide_at * 2 * band, 2 * band, 1)
    return (
        output,
        grad_input,
        small[4],
        sum_up_first,
        sum_down_first,
        small[5],
        total_query,
        total_key,
        total_value,
        total_out,
        total_place,
        own_bias_grad[0],
        own_bias_grad[1],
        small[0],
        total_glu,
        small[8 : 8 + KERNEL],
        small[1],
        total_point,
        small[2],
        sum_up_second,
        sum_down_second,
        small[3],
    )


def per_device(
    frames,
    lengths,
    masked,
    cotangent,
    first_gain,
    first_up,
    first_down,
    attn_gain,
    query_weight,
    key_weight,
    value_weight,
    out_weight,
    place_weight,
    content_bias,
    place_bias,
    conv_gain,
    glu_weight,
    depth_kernel,
    middle_gain,
    point_weight,
    second_gain,
    second_up,
    second_down,
    final_gain,
):
    groups, frames_dev, channels = frames.shape
    row_count = groups * frames_dev
    length = frames_dev * lax.axis_size("wide")
    score_scale = 1.0 / math.sqrt(HEAD_DIM)
    positions = lax.axis_index("wide") * frames_dev + jnp.arange(frames_dev, dtype=jnp.int32)
    frame_grid = (positions[None, :] < lengths[:, None]).astype(jnp.float32)
    frame_ok = frame_grid.reshape(row_count, 1)
    key_ok = jnp.arange(length, dtype=jnp.int32)[None, :] < lengths[:, None]
    stream0 = frames.reshape(row_count, channels).astype(jnp.float32)
    up_first, down_first = gather_ffn(first_up, first_down)
    stream1, saved_first = ffn_forward(
        stream0, first_gain.astype(jnp.float32), up_first, down_first
    )
    full_query, full_key, full_value, full_out, full_glu, full_point = (
        lax.all_gather(query_weight, "wide", axis=0, tiled=True),
        lax.all_gather(key_weight, "wide", axis=0, tiled=True),
        lax.all_gather(value_weight, "wide", axis=0, tiled=True),
        lax.all_gather(out_weight, "wide", axis=0, tiled=True),
        lax.all_gather(glu_weight, "wide", axis=0, tiled=True),
        lax.all_gather(point_weight, "wide", axis=0, tiled=True),
    )
    normed_attn, attn_pull = jax.vjp(norm_rows, stream1, attn_gain.astype(jnp.float32))
    attn_low = normed_attn.astype(jnp.bfloat16)
    query_frames = (
        mult_trans(attn_low, full_query).astype(jnp.bfloat16).reshape(groups, frames_dev, -1)
    )
    key_frames = mult_trans(attn_low, full_key).astype(jnp.bfloat16).reshape(groups, frames_dev, -1)
    value_frames = (
        mult_trans(attn_low, full_value).astype(jnp.bfloat16).reshape(groups, frames_dev, -1)
    )
    heads_query, heads_key, heads_value = (
        lax.all_to_all(query_frames, "wide", split_axis=2, concat_axis=1, tiled=True),
        lax.all_to_all(key_frames, "wide", split_axis=2, concat_axis=1, tiled=True),
        lax.all_to_all(value_frames, "wide", split_axis=2, concat_axis=1, tiled=True),
    )
    local_width = heads_query.shape[2]
    head_count = local_width // HEAD_DIM
    rel_table = relative_table(length, channels).astype(jnp.bfloat16)
    place_rows = (
        mult_trans(rel_table, place_weight)
        .astype(jnp.bfloat16)
        .reshape(2 * length - 1, head_count, HEAD_DIM)
    )
    bias_first = content_bias.astype(jnp.float32).reshape(head_count, HEAD_DIM)
    bias_second = place_bias.astype(jnp.float32).reshape(head_count, HEAD_DIM)
    split_query = heads_query.reshape(groups, length, head_count, HEAD_DIM)
    split_key = heads_key.reshape(groups, length, head_count, HEAD_DIM)
    split_value = heads_value.reshape(groups, length, head_count, HEAD_DIM)
    forward_heads = jax.vmap(
        partial(head_forward, block_rows=QBLK, score_scale=score_scale),
        in_axes=(1, 1, 1, 1, 0, 0, None),
        out_axes=(1, 0),
    )

    def attend_utt(unit_items):
        return forward_heads(
            unit_items[0],
            unit_items[1],
            unit_items[2],
            place_rows,
            bias_first,
            bias_second,
            unit_items[3],
        )

    attended, log_total = lax.map(attend_utt, (split_query, split_key, split_value, key_ok))
    framed = lax.all_to_all(
        attended.reshape(groups, length, local_width),
        "wide",
        split_axis=1,
        concat_axis=2,
        tiled=True,
    ).reshape(row_count, -1)
    stream2 = stream1 + mult_plain(framed, full_out)
    normed_conv, conv_pull = jax.vjp(norm_rows, stream2, conv_gain.astype(jnp.float32))
    conv_low = normed_conv.astype(jnp.bfloat16)
    glu_in = mult_trans(conv_low, full_glu)
    linear = glu_in[:, :channels]
    gating = jax.nn.sigmoid(glu_in[:, channels:])
    gated = (linear * gating * frame_ok).astype(jnp.bfloat16).reshape(groups, frames_dev, channels)
    padded = with_halo(gated, (("wide", 1),), RIM)
    kernel_f = depth_kernel.astype(jnp.float32)
    conv_out = jnp.zeros((groups, frames_dev, channels), jnp.float32)
    for offset in range(KERNEL):
        conv_out = conv_out + padded[:, offset : offset + frames_dev, :] * kernel_f[offset]
    conv_out = conv_out.reshape(row_count, channels)
    middle, middle_pull = jax.vjp(norm_rows, conv_out, middle_gain.astype(jnp.float32))
    swished = jax.nn.silu(middle).astype(jnp.bfloat16)
    stream3 = stream2 + mult_trans(swished, full_point)
    up_second, down_second = gather_ffn(second_up, second_down)
    stream4, saved_second = ffn_forward(
        stream3, second_gain.astype(jnp.float32), up_second, down_second
    )
    final_rows, final_pull = jax.vjp(norm_rows, stream4, final_gain.astype(jnp.float32))
    output = final_rows.astype(jnp.bfloat16).reshape(groups, frames_dev, channels)
    seed_weight = (masked.astype(jnp.float32) * frame_grid).reshape(row_count, 1)
    seed_grad = cotangent.reshape(row_count, channels).astype(jnp.float32) * seed_weight
    grad4, grad_final_gain = final_pull(seed_grad)
    back_up_second, back_down_second = gather_ffn(second_up, second_down)
    grad3, grad_second_gain, grad_up_second, grad_down_second = ffn_backward(
        grad4, saved_second, back_up_second, back_down_second
    )
    summed_second = sum_ffn(grad_up_second, grad_down_second)
    grad_branch = grad3.astype(jnp.bfloat16)
    grad_point = mult_rows(grad_branch, swished)
    grad_middle = mult_plain(grad_branch, full_point) * silu_slope(middle)
    grad_conv, grad_middle_gain = middle_pull(grad_middle)
    conv_grad_low = grad_conv.astype(jnp.bfloat16).reshape(groups, frames_dev, channels)
    grad_padded = with_halo(conv_grad_low, (("wide", 1),), RIM)
    grad_gated = jnp.zeros((groups, frames_dev, channels), jnp.float32)
    kernel_rows = []
    for offset in range(KERNEL):
        grad_gated = (
            grad_gated
            + grad_padded[:, 2 * RIM - offset : 2 * RIM - offset + frames_dev, :] * kernel_f[offset]
        )
        kernel_rows.append(
            jnp.einsum(
                "rzn,rzn->n",
                padded[:, offset : offset + frames_dev, :],
                conv_grad_low,
                preferred_element_type=jnp.float32,
            )
        )
    grad_kernel = jnp.stack(kernel_rows)
    grad_gated = grad_gated.reshape(row_count, channels) * frame_ok
    grad_glu_in = jnp.concatenate(
        [grad_gated * gating, grad_gated * linear * gating * (1.0 - gating)], axis=1
    ).astype(jnp.bfloat16)
    grad_glu = mult_rows(grad_glu_in, conv_low)
    grad_conv_in, grad_conv_gain = conv_pull(mult_plain(grad_glu_in, full_glu))
    grad2 = grad3 + grad_conv_in
    grad_attn = grad2.astype(jnp.bfloat16)
    grad_out = mult_rows(framed, grad_attn)
    grad_framed = (
        mult_trans(grad_attn, full_out).astype(jnp.bfloat16).reshape(groups, frames_dev, -1)
    )
    grad_heads = lax.all_to_all(grad_framed, "wide", split_axis=2, concat_axis=1, tiled=True)
    backward_heads = jax.vmap(
        partial(head_backward, block_rows=QBLK, score_scale=score_scale),
        in_axes=(1, 1, 1, 1, 0, 0, None, 0, 1),
        out_axes=(1, 1, 1, 1, 0, 0),
    )

    def attend_back(unit_items):
        return backward_heads(
            unit_items[0],
            unit_items[1],
            unit_items[2],
            place_rows,
            bias_first,
            bias_second,
            unit_items[3],
            unit_items[4],
            unit_items[5],
        )

    grad_query_h, grad_key_h, grad_value_h, grad_place_h, grad_bias_first, grad_bias_second = (
        lax.map(
            attend_back,
            (
                split_query,
                split_key,
                split_value,
                key_ok,
                log_total,
                grad_heads.reshape(groups, length, head_count, HEAD_DIM),
            ),
        )
    )
    back_query, back_key, back_value = (
        lax.all_to_all(
            grad_query_h.reshape(groups, length, local_width),
            "wide",
            split_axis=1,
            concat_axis=2,
            tiled=True,
        ),
        lax.all_to_all(
            grad_key_h.reshape(groups, length, local_width),
            "wide",
            split_axis=1,
            concat_axis=2,
            tiled=True,
        ),
        lax.all_to_all(
            grad_value_h.reshape(groups, length, local_width),
            "wide",
            split_axis=1,
            concat_axis=2,
            tiled=True,
        ),
    )
    back_query = back_query.reshape(row_count, -1)
    back_key = back_key.reshape(row_count, -1)
    back_value = back_value.reshape(row_count, -1)
    grad_query_w = mult_rows(back_query, attn_low)
    grad_key_w = mult_rows(back_key, attn_low)
    grad_value_w = mult_rows(back_value, attn_low)
    grad_normed = (
        mult_plain(back_query, full_query)
        + mult_plain(back_key, full_key)
        + mult_plain(back_value, full_value)
    )
    grad_attn_in, grad_attn_gain = attn_pull(grad_normed)
    grad1 = grad2 + grad_attn_in
    grad_place_w = jnp.einsum(
        "urc,rd->cd",
        grad_place_h.reshape(groups, 2 * length - 1, local_width),
        rel_table,
        preferred_element_type=jnp.float32,
    )
    grad_content = jnp.sum(grad_bias_first, axis=0).reshape(local_width)
    grad_place_b = jnp.sum(grad_bias_second, axis=0).reshape(local_width)
    back_up_first, back_down_first = gather_ffn(first_up, first_down)
    grad0, grad_first_gain, grad_up_first, grad_down_first = ffn_backward(
        grad1, saved_first, back_up_first, back_down_first
    )
    summed_first = sum_ffn(grad_up_first, grad_down_first)
    mixer_grads = (
        lax.psum_scatter(
            grad_query_w.astype(jnp.bfloat16), "wide", scatter_dimension=0, tiled=True
        ).astype(jnp.float32),
        lax.psum_scatter(
            grad_key_w.astype(jnp.bfloat16), "wide", scatter_dimension=0, tiled=True
        ).astype(jnp.float32),
        lax.psum_scatter(
            grad_value_w.astype(jnp.bfloat16), "wide", scatter_dimension=0, tiled=True
        ).astype(jnp.float32),
        lax.psum_scatter(
            grad_out.astype(jnp.bfloat16), "wide", scatter_dimension=0, tiled=True
        ).astype(jnp.float32),
        lax.psum_scatter(
            grad_glu.astype(jnp.bfloat16), "wide", scatter_dimension=0, tiled=True
        ).astype(jnp.float32),
        lax.psum_scatter(
            grad_point.astype(jnp.bfloat16), "wide", scatter_dimension=0, tiled=True
        ).astype(jnp.float32),
    )
    totals = (
        lax.psum(mixer_grads[0].astype(jnp.bfloat16), "utt").astype(jnp.float32),
        lax.psum(mixer_grads[1].astype(jnp.bfloat16), "utt").astype(jnp.float32),
        lax.psum(mixer_grads[2].astype(jnp.bfloat16), "utt").astype(jnp.float32),
        lax.psum(mixer_grads[3].astype(jnp.bfloat16), "utt").astype(jnp.float32),
        lax.psum(mixer_grads[4].astype(jnp.bfloat16), "utt").astype(jnp.float32),
        lax.psum(mixer_grads[5].astype(jnp.bfloat16), "utt").astype(jnp.float32),
        lax.psum(grad_place_w.astype(jnp.bfloat16), "utt").astype(jnp.float32),
        lax.psum(grad_content.astype(jnp.bfloat16), "utt").astype(jnp.float32),
        lax.psum(grad_place_b.astype(jnp.bfloat16), "utt").astype(jnp.float32),
    )
    small_grads = lax.psum(
        (
            grad_first_gain,
            grad_attn_gain,
            grad_conv_gain,
            grad_middle_gain,
            grad_second_gain,
            grad_final_gain,
            grad_kernel,
        ),
        ("utt", "wide"),
    )
    grad_input = grad0.astype(jnp.bfloat16).reshape(groups, frames_dev, channels)
    return (
        output,
        grad_input,
        small_grads[0],
        summed_first[0],
        summed_first[1],
        small_grads[1],
        totals[0],
        totals[1],
        totals[2],
        totals[3],
        totals[6],
        totals[7],
        totals[8],
        small_grads[2],
        totals[4],
        small_grads[6],
        small_grads[3],
        totals[5],
        small_grads[4],
        summed_second[0],
        summed_second[1],
        small_grads[5],
    )


def solution(mesh):
    shape = dict(mesh.shape)
    if shape["wide"] == 4 and shape["utt"] % 4 == 0:
        mesh = jax.sharding.Mesh(
            mesh.devices.reshape(shape["utt"] // 2, 2, 2, 2), ("z", "core", "y", "x")
        )
        utt, wide, body = ("z", "core"), ("y", "x"), per_chip
    else:
        utt, wide, body = "utt", "wide", per_device
    every = (utt, wide) if utt == "utt" else (*utt, *wide)
    in_specs = (
        P(utt, wide, None),
        P(utt),
        P(utt, wide),
        P(utt, wide, None),
        P(),
        P(every, None),
        P(every, None),
        P(),
        P(wide, None),
        P(wide, None),
        P(wide, None),
        P(wide, None),
        P(wide, None),
        P(wide),
        P(wide),
        P(),
        P(wide, None),
        P(),
        P(),
        P(wide, None),
        P(),
        P(every, None),
        P(every, None),
        P(),
    )
    out_specs = (
        P(utt, wide, None),
        P(utt, wide, None),
        P(),
        P(every, None),
        P(every, None),
        P(),
        P(wide, None),
        P(wide, None),
        P(wide, None),
        P(wide, None),
        P(wide, None),
        P(wide),
        P(wide),
        P(),
        P(wide, None),
        P(),
        P(),
        P(wide, None),
        P(),
        P(every, None),
        P(every, None),
        P(),
    )
    return jax.shard_map(
        body, mesh=mesh, in_specs=in_specs, out_specs=out_specs, check_vma=False
    )
```

```python
from functools import partial
import math

import jax
import jax.numpy as jnp
from jax import lax
from jax.experimental import pallas as pl
from jax.experimental.pallas import tpu as pltpu
from jax.sharding import PartitionSpec as P

HEAD_DIM = 64
KERNEL = 31
QBLK = 512
RIM = 15
PAIR = 128
ROWS_FWD = 256
ROWS_BWD = 256
FF_BLOCK = 512
VMEM = 58 * 2**20


EPSILON = 1e-05
MASKED_SCORE = -1e30


def with_halo(block, sides, width):
    for axis, dim in sides:
        count = lax.axis_size(axis)
        forward = [(i, i + 1) for i in range(count - 1)]
        backward = [(target, source) for source, target in forward]
        low = lax.ppermute(
            lax.slice_in_dim(block, block.shape[dim] - width, None, axis=dim), axis, forward
        )
        high = lax.ppermute(lax.slice_in_dim(block, 0, width, axis=dim), axis, backward)
        block = jnp.concatenate([low, block, high], axis=dim)
    return block


def norm_rows(values, gain_vec):
    average = jnp.mean(values, axis=-1, keepdims=True)
    centred = values - average
    spread = jnp.mean(centred * centred, axis=-1, keepdims=True)
    return centred * lax.rsqrt(spread + EPSILON) * gain_vec


def silu_slope(before):
    squash = jax.nn.sigmoid(before)
    return squash * (1.0 + before * (1.0 - squash))


def mult_trans(first_mat, second_mat):
    return lax.dot_general(
        first_mat, second_mat, (((1,), (1,)), ((), ())), preferred_element_type=jnp.float32
    )


def mult_plain(first_mat, second_mat):
    return jnp.dot(first_mat, second_mat, preferred_element_type=jnp.float32)


def mult_rows(first_mat, second_mat):
    return lax.dot_general(
        first_mat, second_mat, (((0,), (0,)), ((), ())), preferred_element_type=jnp.float32
    )


def relative_table(length, channels):
    offsets = length - 1 - jnp.arange(2 * length - 1).astype(jnp.float32)
    rates = jnp.exp(
        jnp.arange(channels // 2).astype(jnp.float32) * (-2.0 * math.log(10000.0) / channels)
    )
    angles = offsets[:, None] * rates[None, :]
    return jnp.concatenate([jnp.sin(angles), jnp.cos(angles)], axis=1)


def skew_rows(reversed_scores):
    block_rows, span = reversed_scores.shape
    flat = reversed_scores.reshape(-1)[block_rows - 1 : block_rows - 1 + block_rows * (span - 1)]
    return flat.reshape(block_rows, span - 1)[:, : span - block_rows + 1]


def unskew_rows(grad_scores, span):
    block_rows, length = grad_scores.shape
    padded = jnp.pad(grad_scores, ((0, 0), (0, span - 1 - length)))
    flat = jnp.pad(padded.reshape(-1), (block_rows - 1, 1))
    return flat.reshape(block_rows, span)


def gather_ffn(up_rows, down_rows):
    return (
        lax.all_gather(up_rows, ("utt", "wide"), axis=0, tiled=True),
        lax.all_gather(down_rows, ("utt", "wide"), axis=0, tiled=True),
    )


def sum_ffn(grad_up, grad_down):
    return (
        lax.psum_scatter(grad_up, ("utt", "wide"), scatter_dimension=0, tiled=True),
        lax.psum_scatter(grad_down, ("utt", "wide"), scatter_dimension=0, tiled=True),
    )


def ffn_forward(stream, gain_vec, up_full, down_full):
    normed, norm_pull = jax.vjp(norm_rows, stream, gain_vec)
    normed_low = normed.astype(jnp.bfloat16)
    before = mult_trans(normed_low, up_full)
    active_low = jax.nn.silu(before).astype(jnp.bfloat16)
    return (
        stream + 0.5 * mult_plain(active_low, down_full),
        (norm_pull, normed_low, before, active_low),
    )


def ffn_backward(grad_stream, saved_ffn, up_full, down_full):
    norm_pull, normed_low, before, active_low = saved_ffn
    grad_out = (0.5 * grad_stream).astype(jnp.bfloat16)
    grad_down = mult_rows(active_low, grad_out)
    grad_before = (mult_trans(grad_out, down_full) * silu_slope(before)).astype(jnp.bfloat16)
    grad_up = mult_rows(grad_before, normed_low)
    grad_input, grad_gain = norm_pull(mult_plain(grad_before, up_full))
    return (grad_stream + grad_input, grad_gain, grad_up, grad_down)


def head_forward(
    query_rows,
    key_rows,
    value_rows,
    place_rows,
    bias_first,
    bias_second,
    key_ok,
    block_rows,
    score_scale,
):
    length, head_width = query_rows.shape
    with_u = (query_rows.astype(jnp.float32) + bias_first).astype(jnp.bfloat16)
    with_v = (query_rows.astype(jnp.float32) + bias_second).astype(jnp.bfloat16)

    def one_block(block_index):
        first_row = block_index * block_rows
        block_u = lax.dynamic_slice_in_dim(with_u, first_row, block_rows, 0)
        block_v = lax.dynamic_slice_in_dim(with_v, first_row, block_rows, 0)
        near_rows = lax.dynamic_slice_in_dim(
            place_rows, length - block_rows - first_row, block_rows + length - 1, 0
        )
        scores = (
            mult_trans(block_u, key_rows) + skew_rows(mult_trans(block_v, near_rows))
        ) * score_scale
        scores = jnp.where(key_ok[None, :], scores, MASKED_SCORE)
        highest = jnp.max(scores, axis=1, keepdims=True)
        weights = jnp.exp(scores - highest)
        running = jnp.sum(weights, axis=1, keepdims=True)
        attend_prob = (weights / running).astype(jnp.bfloat16)
        return (
            mult_plain(attend_prob, value_rows).astype(jnp.bfloat16),
            (highest + jnp.log(running))[:, 0],
        )

    attended, log_total = lax.map(one_block, jnp.arange(length // block_rows, dtype=jnp.int32))
    return (attended.reshape(length, head_width), log_total.reshape(length))


def head_backward(
    query_rows,
    key_rows,
    value_rows,
    place_rows,
    bias_first,
    bias_second,
    key_ok,
    log_total,
    grad_mixed,
    block_rows,
    score_scale,
):
    length, head_width = query_rows.shape
    span = block_rows + length - 1
    with_u = (query_rows.astype(jnp.float32) + bias_first).astype(jnp.bfloat16)
    with_v = (query_rows.astype(jnp.float32) + bias_second).astype(jnp.bfloat16)

    def one_block(carried, block_index):
        grad_key, grad_value, grad_place = carried
        first_row = block_index * block_rows
        place_first = length - block_rows - first_row
        block_u = lax.dynamic_slice_in_dim(with_u, first_row, block_rows, 0)
        block_v = lax.dynamic_slice_in_dim(with_v, first_row, block_rows, 0)
        near_rows = lax.dynamic_slice_in_dim(place_rows, place_first, span, 0)
        block_total = lax.dynamic_slice_in_dim(log_total, first_row, block_rows, 0)
        block_grad = lax.dynamic_slice_in_dim(grad_mixed, first_row, block_rows, 0)
        scores = (
            mult_trans(block_u, key_rows) + skew_rows(mult_trans(block_v, near_rows))
        ) * score_scale
        scores = jnp.where(key_ok[None, :], scores, MASKED_SCORE)
        attend_prob = jnp.exp(scores - block_total[:, None])
        grad_prob = mult_trans(block_grad, value_rows)
        inner = jnp.sum(attend_prob * grad_prob, axis=1, keepdims=True)
        grad_score = jnp.where(key_ok[None, :], attend_prob * (grad_prob - inner), 0.0).astype(
            jnp.bfloat16
        )
        grad_value = grad_value + mult_rows(attend_prob.astype(jnp.bfloat16), block_grad)
        grad_with_u = mult_plain(grad_score, key_rows) * score_scale
        grad_key = grad_key + mult_rows(grad_score, block_u) * score_scale
        spread_grad = unskew_rows(grad_score, span)
        grad_with_v = mult_plain(spread_grad, near_rows) * score_scale
        place_part = (
            lax.dynamic_slice_in_dim(grad_place, place_first, span, 0)
            + mult_rows(spread_grad, block_v) * score_scale
        )
        grad_place = lax.dynamic_update_slice_in_dim(grad_place, place_part, place_first, 0)
        return ((grad_key, grad_value, grad_place), (grad_with_u, grad_with_v))

    zero_rows = jnp.zeros((length, head_width), jnp.float32)
    zero_place = jnp.zeros((2 * length - 1, head_width), jnp.float32)
    (grad_key, grad_value, grad_place), (grad_with_u, grad_with_v) = lax.scan(
        one_block,
        (zero_rows, zero_rows, zero_place),
        jnp.arange(length // block_rows, dtype=jnp.int32),
    )
    grad_with_u = grad_with_u.reshape(length, head_width)
    grad_with_v = grad_with_v.reshape(length, head_width)
    grad_query = (grad_with_u + grad_with_v).astype(jnp.bfloat16)
    return (
        grad_query,
        grad_key.astype(jnp.bfloat16),
        grad_value.astype(jnp.bfloat16),
        grad_place.astype(jnp.bfloat16),
        jnp.sum(grad_with_u, axis=0),
        jnp.sum(grad_with_v, axis=0),
    )


def biased(q_ref, bias_ref, scale):
    return ((q_ref[...].astype(jnp.float32) + bias_ref[...].astype(jnp.float32)).astype(jnp.bfloat16).astype(jnp.float32) * scale).astype(jnp.bfloat16)

def attend_fwd_kernel(len_ref, q_ref, k_ref, v_ref, place_ref, cb_ref, pb_ref, out_ref, prob_ref, *, scale):
    rows = q_ref.shape[0]
    length = k_ref.shape[0]
    span = rows + length
    first = pl.multiple_of(length - rows - pl.program_id(1) * rows, rows)
    lanes = lax.broadcasted_iota(jnp.int32, (rows, PAIR), 1)
    with_u = biased(q_ref, cb_ref, scale)
    with_v = biased(q_ref, pb_ref, scale)
    window = place_ref[pl.ds(first, span), :]
    key_ok = lax.broadcasted_iota(jnp.int32, (rows, length), 1) < len_ref[0]
    zero = jnp.zeros_like(with_u)
    mixed = []
    for head in range(2):
        mine = (lanes // HEAD_DIM) == head
        place_part = mult_trans(jnp.where(mine, with_v, zero), window)
        place_part = pltpu.roll(place_part, span - rows + 1, 1, stride=1, stride_axis=0)
        scores = mult_trans(jnp.where(mine, with_u, zero), k_ref[...]) + place_part[:, :length]
        scores = jnp.where(key_ok, scores, MASKED_SCORE)
        weights = jnp.exp(scores - jnp.max(scores, axis=1, keepdims=True))
        total = jnp.sum(weights, axis=1, keepdims=True)
        prob = (weights * (1.0 / total)).astype(jnp.bfloat16)
        prob_ref[head] = prob
        mixed.append(mult_plain(prob, v_ref[...]))
    out_ref[...] = jnp.where(lanes < HEAD_DIM, mixed[0], mixed[1]).astype(jnp.bfloat16)

def attend_fwd_gather_kernel(layers, count, blocks, *refs, scale):
    ins, shards, refs = refs[:7], refs[7 : 7 + count], refs[7 + count :]
    outs, fulls, sems = refs[:2], refs[2 : 2 + count], refs[2 + count :]
    at = pl.program_id(0) * pl.num_programs(1) + pl.program_id(1)
    plan = gather_plan(layers, shards, fulls, (), *sems)
    run_between(*plan, at, blocks, partial(attend_fwd_kernel, *ins, *outs, scale=scale))


def attend_fwd(length_arr, q, k, v, place, cb, pb, rows, layers, shards, collective_id):
    length, width = q.shape
    pairs = width // PAIR
    count = len(shards)
    shard = shards[0].shape
    part = pl.BlockSpec((rows, PAIR), lambda p, i: (i, p))
    full = pl.BlockSpec((length, PAIR), lambda p, i: (0, p))
    tall = pl.BlockSpec((2 * length, PAIR), lambda p, i: (0, p))
    vec = pl.BlockSpec((1, PAIR), lambda p, i: (0, p))
    far = [pl.BlockSpec(memory_space=pl.ANY)] * count
    blocks = pairs * (length // rows)
    attended, prob, *fulls = pl.pallas_call(
        partial(attend_fwd_gather_kernel, layers, count, blocks, scale=1.0 / math.sqrt(HEAD_DIM)),
        grid=(pairs, length // rows),
        in_specs=[pl.BlockSpec(memory_space=pltpu.SMEM), part, full, full, tall, vec, vec] + far,
        out_specs=[part, pl.BlockSpec((2, rows, length), lambda p, i: (p, i, 0))] + far,
        out_shape=[
            jax.ShapeDtypeStruct((length, width), jnp.bfloat16),
            jax.ShapeDtypeStruct((2 * pairs, length, length), jnp.bfloat16),
        ]
        + [jax.ShapeDtypeStruct((layers, 2, 2, 2, *shard), jnp.bfloat16)] * count,
        scratch_shapes=gather_sems(count, layers),
        compiler_params=pltpu.CompilerParams(
            vmem_limit_bytes=VMEM, collective_id=collective_id, has_side_effects=True
        ),
        cost_estimate=pl.CostEstimate(
            flops=40 * 10**9, bytes_accessed=20 * 2**20, transcendentals=2 * pairs * length * length
        ),
        name="attend_fwd",
    )(length_arr, q, k, v, place, cb, pb, *shards)
    return attended, prob, [full.reshape(-1, shard[1]) for full in fulls]


def attend_bwd_kernel(q_ref, k_ref, v_ref, place_ref, cb_ref, pb_ref, prob_ref, g_ref, gq_ref, gk_ref, gv_ref, gp_ref, gb_ref, gk_s, gv_s, gp_s, *, scale):
    rows = q_ref.shape[0]
    length = k_ref.shape[0]
    span = rows + length
    step = pl.program_id(1)
    first = pl.multiple_of(length - rows - step * rows, rows)
    lanes = lax.broadcasted_iota(jnp.int32, (rows, PAIR), 1)
    flip = (lax.broadcasted_iota(jnp.int32, (rows, rows), 0) + lax.broadcasted_iota(jnp.int32, (rows, rows), 1) == rows - 1).astype(jnp.bfloat16)
    with_u = biased(q_ref, cb_ref, scale)
    with_v = mult_plain(flip, biased(q_ref, pb_ref, scale)).astype(jnp.bfloat16)
    grad = g_ref[...]
    window = place_ref[pl.ds(first, span), :]
    zero = jnp.zeros_like(with_u)

    @pl.when(step == 0)
    def _():
        gk_s[...] = jnp.zeros_like(gk_s)
        gv_s[...] = jnp.zeros_like(gv_s)
        gp_s[...] = jnp.zeros_like(gp_s)
        gb_ref[...] = jnp.zeros_like(gb_ref)

    grad_t, with_u_t, with_v_t = grad.T, with_u.T, with_v.T
    gu = []
    gw = []
    for head in range(2):
        mine = (lanes // HEAD_DIM) == head
        prob = prob_ref[head]
        grad_h = jnp.where(mine, grad, zero)
        grad_prob = mult_trans(grad_h, v_ref[...])
        weighted = prob.astype(jnp.float32) * grad_prob
        inner = jnp.sum(weighted, axis=1, keepdims=True)
        grad_score = (weighted - prob.astype(jnp.float32) * inner).astype(jnp.bfloat16)
        turned = mult_plain(flip, grad_score).astype(jnp.bfloat16)
        turned = jnp.concatenate([turned, jnp.zeros((rows, rows), jnp.bfloat16)], axis=1)
        turned = pltpu.roll(turned, 0, 1, stride=1, stride_axis=0)
        gu.append(mult_plain(grad_score, k_ref[...]))
        gw.append(mult_plain(turned, window))
        band = slice(head * HEAD_DIM, (head + 1) * HEAD_DIM)
        gv_s[band, :] += mult_plain(grad_t[band, :], prob)
        gk_s[band, :] += mult_plain(with_u_t[band, :], grad_score)
        gp_s[band, pl.ds(first, span)] += mult_plain(with_v_t[band, :], turned)
    grad_u = jnp.where(lanes < HEAD_DIM, gu[0], gu[1]) * scale
    grad_w = jnp.where(lanes < HEAD_DIM, gw[0], gw[1]) * scale
    gb_ref[0:1, :] += jnp.sum(grad_u, axis=0, keepdims=True)
    gb_ref[1:2, :] += jnp.sum(grad_w, axis=0, keepdims=True)
    high = grad_w.astype(jnp.bfloat16)
    rest = (grad_w - high.astype(jnp.float32)).astype(jnp.bfloat16)
    gq_ref[...] = (grad_u + mult_plain(flip, high) + mult_plain(flip, rest)).astype(jnp.bfloat16)

    @pl.when(step == pl.num_programs(1) - 1)
    def _():
        gk_ref[...] = gk_s[...].T.astype(jnp.bfloat16)
        gv_ref[...] = gv_s[...].T.astype(jnp.bfloat16)
        gp_ref[...] = gp_s[...].T.astype(jnp.bfloat16)


def attend_bwd_sum_kernel(layers, shared, count, blocks, *refs, scale):
    ins, parts = refs[:8], refs[8 : 8 + count]
    refs = refs[8 + count :]
    outs, sums, scratch, own = refs[:5], refs[5 : 5 + count], refs[5 + count : 8 + count], refs[8 + count :]
    at = pl.program_id(0) * pl.num_programs(1) + pl.program_id(1)
    plan = reduce_plan(layers, shared, parts, sums, None, own)
    body = partial(attend_bwd_kernel, *ins, *outs, *scratch, scale=scale)
    run_between(*plan, at, blocks, body)


def attend_bwd(q, k, v, place, cb, pb, prob, grad, rows, layers, shared, parts, collective_id):
    length, width = q.shape
    pairs = width // PAIR
    count = len(parts)
    inputs, shapes = reduce_shapes(layers, shared, parts)
    shard, channels = shapes[shared].shape[2:]
    still = lambda shape: pl.BlockSpec(shape, lambda p, i: (0,) * len(shape))
    full = pl.BlockSpec((length, PAIR), lambda p, i: (0, p))
    part = pl.BlockSpec((rows, PAIR), lambda p, i: (i, p))
    vec = pl.BlockSpec((1, PAIR), lambda p, i: (0, p))
    tall = pl.BlockSpec((2 * length, PAIR), lambda p, i: (0, p))
    return pl.pallas_call(
        partial(attend_bwd_sum_kernel, layers, shared, count, pairs * (length // rows), scale=1.0 / math.sqrt(HEAD_DIM)),
        grid=(pairs, length // rows),
        in_specs=[
            part,
            full,
            full,
            tall,
            vec,
            vec,
            pl.BlockSpec((2, rows, length), lambda p, i: (p, i, 0)),
            part,
        ]
        + [pl.BlockSpec(memory_space=pl.ANY)] * count,
        out_specs=[part, full, full, tall, pl.BlockSpec((8, PAIR), lambda p, i: (0, p))]
        + [still(shape.shape) for shape in shapes],
        out_shape=[
            jax.ShapeDtypeStruct((length, width), jnp.bfloat16),
            jax.ShapeDtypeStruct((length, width), jnp.bfloat16),
            jax.ShapeDtypeStruct((length, width), jnp.bfloat16),
            jax.ShapeDtypeStruct((2 * length, width), jnp.bfloat16),
            jax.ShapeDtypeStruct((8, width), jnp.float32),
        ]
        + shapes,
        scratch_shapes=[
            pltpu.VMEM((PAIR, length), jnp.float32),
            pltpu.VMEM((PAIR, length), jnp.float32),
            pltpu.VMEM((PAIR, 2 * length), jnp.float32),
        ]
        + reduce_scratch(count, layers, shard, channels),
        compiler_params=pltpu.CompilerParams(
            vmem_limit_bytes=VMEM, collective_id=collective_id, has_side_effects=True
        ),
        cost_estimate=pl.CostEstimate(
            flops=100 * 10**9, bytes_accessed=40 * 2**20, transcendentals=0
        ),
        name="attend_bwd",
    )(
        q,
        k,
        v,
        place,
        cb,
        pb,
        prob,
        grad,
        *inputs,
    )


MESH = pl.DeviceIdType.MESH


def chip_place(layers):
    z, c, y, x = (lax.axis_index(axis) for axis in ("z", "core", "y", "x"))

    def at(dz=0, dc=0, dy=0, dx=0):
        return (
            lax.rem(z + dz, layers),
            lax.rem(c + dc, 2),
            lax.rem(y + dy, 2),
            lax.rem(x + dx, 2),
        )

    def spot(dz=0, dc=0, dy=0, dx=0):
        return at(layers - dz, dc, dy, dx)

    return at, spot


def greet(at, layers):
    barrier = pltpu.get_barrier_semaphore()
    peers = [at(dz=k) for k in range(1, layers)] + [at(dc=1), at(dy=1), at(dx=1)]
    for peer in peers:
        pl.semaphore_signal(barrier, inc=1, device_id=peer, device_id_type=MESH)
    pl.semaphore_wait(barrier, len(peers))


def remote(source, target, sems, index, device):
    return pltpu.make_async_remote_copy(
        src_ref=source,
        dst_ref=target,
        send_sem=sems.at[(0, *index)],
        recv_sem=sems.at[(1, *index)],
        device_id=device,
        device_id_type=MESH,
    )


def far_first(layers):
    return sorted(range(1, layers), key=lambda k: -min(k, layers - k)) + [0]


def gather_plan(layers, shards, fulls, flat_only, z_sem, p_sem, d_sem, c_sem, own_sem):
    at, spot = chip_place(layers)
    arrays = range(len(shards))
    z, _, _, _ = spot()
    odd = lax.rem(z, 2)
    pair = at(dz=1 + odd * (layers - 2))
    items = [(0, a) for a in flat_only]
    items += [(dz, a) for dz in reversed(far_first(layers)) for a in arrays if a not in flat_only]
    own, along, flat, cross, last = {}, {}, {}, {}, {}
    for dz, a in items:
        full = fulls[a]
        flat_at = a in flat_only
        place = (lambda *_, **by: (odd, *spot(**by)[2:])) if flat_at else (lambda **by: spot(dz, **by))
        half = shards[a].shape[0] // 32 * 16
        source = full.at[place()] if dz else shards[a]
        if dz:
            along[dz, a] = remote(shards[a], full.at[spot()], z_sem, (a, dz), at(dz=dz))
        else:
            own[dz, a] = pltpu.make_async_copy(shards[a], full.at[place()], own_sem.at[a])
        flat[dz, a] = (
            remote(source, full.at[place()], p_sem, (a, dz, 0), at(dx=1)),
            remote(source, full.at[place()], p_sem, (a, dz, 1), at(dy=1)),
        )
        from_x = full.at[(*place(dx=1), pl.ds(half, shards[a].shape[0] - half))]
        from_y = full.at[(*place(dy=1), pl.ds(0, half))]
        cross[dz, a] = (
            remote(from_x, from_x, d_sem, (a, dz, 0), at(dy=1)),
            remote(from_y, from_y, d_sem, (a, dz, 1), at(dx=1)),
        )
        plane = full.at[place()[:-2]]
        last[dz, a] = remote(plane, plane, c_sem, (a, dz), pair if flat_at else at(dc=1))

    def enter():
        greet(at, layers)
        for item in items:
            if item[0]:
                along[item].start()
        for copy in own.values():
            copy.start()

    def spread(item):
        if item in along:
            along[item].wait_recv()
        for copy in flat[item]:
            copy.start()

    def turn(item):
        for got, out in zip(flat[item], cross[item]):
            got.wait_recv()
            out.start()

    def share(item):
        for got in cross[item]:
            got.wait_recv()
        if item in own:
            own[item].wait()
        last[item].start()

    def step(turn_at):
        for action, lag in ((spread, 0), (turn, 2), (share, 4)):
            if 0 <= turn_at - lag < len(items):
                action(items[turn_at - lag])

    def leave():
        for item in items:
            last[item].wait_recv()
        for item in items:
            if item in along:
                along[item].wait_send()
            for copy in (*flat[item], *cross[item], last[item]):
                copy.wait_send()

    return enter, step, len(items) + 4, leave


def gather_sems(count, layers):
    dma = pltpu.SemaphoreType.DMA
    return [
        dma((2, count, layers)),
        dma((2, count, layers, 2)),
        dma((2, count, layers, 2)),
        dma((2, count, layers)),
        dma((count,)),
    ]


def gather_kernel(layers, count, *refs):
    enter, step, turns, leave = gather_plan(
        layers, refs[:count], refs[count : 2 * count], (count - 1,), *refs[2 * count :]
    )
    enter()
    for turn_at in range(turns):
        step(turn_at)
    leave()


def gather_all(layers, shards, flat_shard, collective_id):
    ins = [*shards, flat_shard]
    count = len(ins)
    width = flat_shard.shape[1]
    shapes = [(layers, 2, 2, 2, *shard.shape) for shard in shards] + [(2, 2, 2, *flat_shard.shape)]
    *fulls, flat_full = pl.pallas_call(
        partial(gather_kernel, layers, count),
        in_specs=[pl.BlockSpec(memory_space=pl.ANY)] * count,
        out_specs=[pl.BlockSpec(memory_space=pl.ANY)] * count,
        out_shape=[jax.ShapeDtypeStruct(shape, jnp.bfloat16) for shape in shapes],
        scratch_shapes=gather_sems(count, layers),
        compiler_params=pltpu.CompilerParams(collective_id=collective_id, has_side_effects=True),
        cost_estimate=pl.CostEstimate(flops=0, bytes_accessed=300 * 2**20, transcendentals=0),
        name="gather_all",
    )(*ins)
    return [full.reshape(-1, width) for full in fulls], flat_full


def add_rows(target, one, two):
    target[...] = (one[...].astype(jnp.float32) + two[...].astype(jnp.float32)).astype(target.dtype)


def reduce_plan(layers, shared, parts, outs, small, scratch, made=None, summed=None):
    at, spot = chip_place(layers)
    sums, got_c, got_d, got_p, got_z, got_s, load_sem, c_sem, d_sem, p_sem, z_sem, s_sem, *tiny = scratch
    arrays = range(len(parts))
    rows = sums.shape[4]
    half = rows // 2
    order = far_first(layers)
    items = [(dz, shared) for dz in order if summed is None]
    items += [(dz, a) for dz in order for a in arrays if a != shared]
    first, second = pl.ds(0, half), pl.ds(half, half)
    here, by_y, by_x, far = (spot(0, 0, dy, dx)[2:] for dy, dx in ((0, 0), (1, 0), (0, 1), (1, 1)))
    made = made or {}
    whole = [a in made or len(parts[a].shape) == 6 for a in arrays]
    core_at = spot()[1]
    load, core, cross, flat, along = {}, {}, {}, {}, {}
    for dz, a in items:
        total = sums.at[a, dz]
        if a not in made:
            source = parts[a].at[spot(dz)[:2]] if whole[a] else parts[a].at[spot(dz)[0]]
            load[dz, a] = pltpu.make_async_copy(source, total, load_sem.at[a, dz])
        if whole[a]:
            slot = order.index(dz) % 2
            source = parts[a].at[slot] if a in made else parts[a].at[spot(dz, dc=1)[:2]]
            core[dz, a] = remote(source, got_c.at[a, dz], c_sem, (a, dz), at(dc=1))
        cross[dz, a] = (
            remote(total.at[(*far, first)], got_d.at[a, dz, 0], d_sem, (a, dz, 0), at(dx=1)),
            remote(total.at[(*far, second)], got_d.at[a, dz, 1], d_sem, (a, dz, 1), at(dy=1)),
        )
        flat[dz, a] = (
            remote(total.at[by_y], got_p.at[a, dz, 0], p_sem, (a, dz, 0), at(dy=1)),
            remote(total.at[by_x], got_p.at[a, dz, 1], p_sem, (a, dz, 1), at(dx=1)),
        )
        if dz:
            along[dz, a] = remote(
                total.at[here], got_z.at[a, dz], z_sem, (a, dz), at(dz=layers - dz)
            )
    own = got_s.at[(core_at, spot()[0])]
    handed = {k: remote(own, own, s_sem, (k,), at(dz=k)) for k in range(1, layers)}
    swapped = remote(got_s.at[core_at], got_s.at[core_at], s_sem, (0,), at(dc=1))
    sent = {}
    if summed:
        got_m, m_sem = tiny[3:]
        sent = {
            k: remote(summed[0].at[spot(k)[0]], got_m.at[k], m_sem, (k,), at(dz=layers - k))
            for k in range(1, layers)
        }
    hops = []
    if small:
        level, got_t, t_sem = tiny[:3]
        hops = [
            remote(level.at[i], got_t.at[i], t_sem, (i,), device)
            for i, device in enumerate((at(dc=1), at(dx=1), at(dy=1)))
        ]
        hops += [
            remote(level.at[3], got_t.at[2 + k], t_sem, (2 + k,), at(dz=k)) for k in range(1, layers)
        ]

    def enter():
        greet(at, layers)
        if small:
            level[0] = small[0][...]
            hops[0].start()
        for copy in sent.values():
            copy.start()
        for item in items:
            if item in load:
                load[item].start()
                if item in core:
                    core[item].start()

    def make(item):
        dz, a = item
        if a not in made:
            return
        left, right = made[a]
        size = 4 * rows
        turn_of = order.index(dz)
        if turn_of >= 2:
            core[order[turn_of - 2], a].wait_send()
        for dc, target in ((1, parts[a].at[turn_of % 2]), (0, sums.at[a, dz])):
            z_at, c_at = spot(dz, dc)[:2]
            columns = pl.ds(pl.multiple_of((2 * z_at + c_at) * size, size), size)
            block = mult_rows(left[:, columns], right[...]).astype(jnp.bfloat16)
            for at_y in range(2):
                for at_x in range(2):
                    row = (2 * at_y + at_x) * rows
                    target[at_y, at_x] = block[row : row + rows]
            if dc:
                core[item].start()

    def join_core(item):
        dz, a = item
        if item in load:
            load[item].wait()
        if whole[a]:
            core[item].wait_recv()
        for place in (far, by_y, by_x, here):
            target = sums.at[(a, dz, *place)]
            if whole[a]:
                add_rows(target, target, got_c.at[(a, dz, *place)])
            if place is far:
                for copy in cross[item]:
                    copy.start()

    def join_cross(item):
        dz, a = item
        one, two = sums.at[(a, dz, *by_y, first)], sums.at[(a, dz, *by_x, second)]
        cross[item][0].wait_recv()
        add_rows(one, one, got_d.at[a, dz, 0])
        flat[item][0].start()
        cross[item][1].wait_recv()
        add_rows(two, two, got_d.at[a, dz, 1])
        flat[item][1].start()

    def join_flat(item):
        dz, a = item
        target = sums.at[(a, dz, *here)]
        for copy in flat[item]:
            copy.wait_recv()
        target[...] = (
            target[...].astype(jnp.float32)
            + got_p[a, dz, 0].astype(jnp.float32)
            + got_p[a, dz, 1].astype(jnp.float32)
        ).astype(jnp.bfloat16)
        if dz:
            along[item].start()

    def total_of(a):
        total = sums[(a, 0, *here)].astype(jnp.float32)
        for dz in range(1, layers):
            along[dz, a].wait_recv()
            total = total + got_z[a, dz].astype(jnp.float32)
        return total

    def join_small(turn_at):
        if turn_at < 3:
            hops[turn_at].wait_recv()
            level[turn_at + 1] = level[turn_at] + got_t[turn_at]
            for hop in hops[turn_at + 1 : turn_at + 2] if turn_at < 2 else hops[3:]:
                hop.start()
        else:
            total = level[3]
            for k in range(1, layers):
                hops[2 + k].wait_recv()
                total = total + got_t[2 + k]
            small[1][...] = total

    def hand_on():
        if summed:
            total = summed[0][spot()[0]].astype(jnp.float32)
            for k, copy in sent.items():
                copy.wait_recv()
                total = total + got_m[k].astype(jnp.float32)
        else:
            total = total_of(shared)
        own[...] = total.astype(jnp.bfloat16)
        for copy in handed.values():
            copy.start()

    def swap():
        for copy in handed.values():
            copy.wait_recv()
        swapped.start()

    lead = 2 if made else 0
    handed_at = 5 if summed else layers - 1 + 5 + 2 + lead
    turns = max(len(items) + 5 + lead, handed_at + 4)

    def step(turn_at):
        actions = ((make, 0), (join_core, lead), (join_cross, lead + 3), (join_flat, lead + 5))
        for action, lag in actions:
            if 0 <= turn_at - lag < len(items):
                action(items[turn_at - lag])
        if small and 1 <= turn_at <= 4:
            join_small(turn_at - 1)
        if turn_at == handed_at:
            hand_on()
        if turn_at == handed_at + 3:
            swap()

    def leave():
        for a in arrays:
            if a != shared:
                outs[a][...] = total_of(a)
        swapped.wait_recv()
        (summed[1] if summed else outs[shared])[...] = got_s[...]
        for item in items:
            if item[0]:
                along[item].wait_send()
            for copy in (*cross[item], *flat[item]):
                copy.wait_send()
            if item in core and not (item[1] in made and item[0] in order[:-2]):
                core[item].wait_send()
        for copy in (*handed.values(), *sent.values(), swapped, *hops):
            copy.wait_send()

    return enter, step, turns, leave


def reduce_scratch(count, layers, rows, width, small=None):
    dma = pltpu.SemaphoreType.DMA
    low = lambda *shape: pltpu.VMEM((count, layers, *shape, width), jnp.bfloat16)
    scratch = [
        low(2, 2, rows),
        low(2, 2, rows),
        low(2, rows // 2),
        low(2, rows),
        low(rows),
        pltpu.VMEM((2, layers, rows, width), jnp.bfloat16),
        dma((count, layers)),
        dma((2, count, layers)),
        dma((2, count, layers, 2)),
        dma((2, count, layers, 2)),
        dma((2, count, layers)),
        dma((2, layers)),
    ]
    if small is not None:
        scratch += [
            pltpu.VMEM((4, *small.shape), jnp.float32),
            pltpu.VMEM((2 + layers, *small.shape), jnp.float32),
            dma((2, 2 + layers)),
            pltpu.VMEM((layers, rows, width), jnp.bfloat16),
            dma((2, layers)),
        ]
    return scratch


def reduce_shapes(layers, shared, parts):
    blocks, shapes = [], []
    for a, (part, count) in enumerate(parts):
        width = part.shape[-1]
        rows = part.size // width // (4 * count * layers)
        blocks.append(part.reshape(layers, *((2,) if count == 2 else ()), 2, 2, rows, width))
        if a == shared:
            shapes.append(jax.ShapeDtypeStruct((2, layers, rows, width), jnp.bfloat16))
        else:
            shapes.append(jax.ShapeDtypeStruct((rows, width), jnp.float32))
    return blocks, shapes


def reduce_kernel(layers, part, left_a, right_a, left_b, right_b, small, sum_a, sum_b, handed, total, ring_a, ring_b, *scratch):
    enter, step, turns, leave = reduce_plan(
        layers,
        None,
        (ring_a, ring_b),
        (sum_a, sum_b),
        (small, total),
        scratch,
        {0: (left_a, right_a), 1: (left_b, right_b)},
        (part, handed),
    )
    enter()
    for turn_at in range(turns):
        step(turn_at)
    leave()


def reduce_all(layers, part, products, small, collective_id):
    rows, width = part.shape[1:]
    near = pl.BlockSpec(memory_space=pltpu.VMEM)
    ring = pltpu.VMEM((2, 2, 2, rows, width), jnp.bfloat16)
    return pl.pallas_call(
        partial(reduce_kernel, layers),
        in_specs=[near] * 6,
        out_specs=[near] * 4,
        out_shape=[
            jax.ShapeDtypeStruct((rows, width), jnp.float32),
            jax.ShapeDtypeStruct((rows, width), jnp.float32),
            jax.ShapeDtypeStruct((2, layers, rows, width), jnp.bfloat16),
            jax.ShapeDtypeStruct(small.shape, jnp.float32),
        ],
        scratch_shapes=[ring, ring] + reduce_scratch(2, layers, rows, width, small),
        compiler_params=pltpu.CompilerParams(
            collective_id=collective_id, has_side_effects=True, vmem_limit_bytes=VMEM
        ),
        cost_estimate=pl.CostEstimate(
            flops=8 * 10**9, bytes_accessed=300 * 2**20, transcendentals=0
        ),
        name="reduce_all",
    )(part, *(matrix for product in products for matrix in product), small)


def run_between(enter, step, turns, leave, at, blocks, body):
    pl.when(at == 0)(enter)
    for turn_at in range(min(turns, blocks)):
        pl.when(at == turn_at)(partial(step, turn_at))
    body()

    @pl.when(at == blocks - 1)
    def _():
        for turn_at in range(blocks, turns):
            step(turn_at)
        leave()


def norm_stats(values):
    centred = values - jnp.mean(values, axis=-1, keepdims=True)
    inverse = lax.rsqrt(jnp.mean(centred * centred, axis=-1, keepdims=True) + EPSILON)
    return centred * inverse, inverse


def norm_back(normal, inverse, gain_vec, upstream):
    grad = upstream * gain_vec
    grad_mean = jnp.mean(grad, axis=-1, keepdims=True)
    grad_along = jnp.mean(grad * normal, axis=-1, keepdims=True)
    return (
        (grad - grad_mean - normal * grad_along) * inverse,
        jnp.sum(upstream * normal, axis=0, keepdims=True),
    )


def ffn_fwd_kernel(x_ref, gain_ref, up_ref, down_ref, y_ref, h_ref, act_ref, slope_ref):
    @pl.when(pl.program_id(0) == 0)
    def _():
        values = x_ref[...].astype(jnp.float32)
        normal, _ = norm_stats(values)
        h_ref[...] = (normal * gain_ref[...].astype(jnp.float32)).astype(jnp.bfloat16)
        y_ref[...] = values

    before = mult_trans(h_ref[...], up_ref[...])
    squash = 1.0 / (1.0 + jnp.exp(-before))
    active = before * squash
    slope_ref[...] = (squash + active * (1.0 - squash)).astype(jnp.bfloat16)
    active_low = active.astype(jnp.bfloat16)
    act_ref[...] = active_low
    y_ref[...] += 0.5 * mult_plain(active_low, down_ref[...])


def ffn_blocks(rows, width, block):
    still = pl.BlockSpec((rows, width), lambda j: (0, 0))
    vec = pl.BlockSpec((1, width), lambda j: (0, 0))
    weight = pl.BlockSpec((block, width), lambda j: (j, 0))
    hidden = pl.BlockSpec((rows, block), lambda j: (0, j))
    return still, vec, weight, hidden


def ffn_fwd(x, gain_vec, up, down):
    rows, width = x.shape
    total = up.shape[0]
    still, vec, weight, hidden = ffn_blocks(rows, width, FF_BLOCK)
    return pl.pallas_call(
        ffn_fwd_kernel,
        grid=(total // FF_BLOCK,),
        in_specs=[still, vec, weight, weight],
        out_specs=[still, still, hidden, hidden],
        out_shape=[
            jax.ShapeDtypeStruct((rows, width), jnp.float32),
            jax.ShapeDtypeStruct((rows, width), jnp.bfloat16),
            jax.ShapeDtypeStruct((rows, total), jnp.bfloat16),
            jax.ShapeDtypeStruct((rows, total), jnp.bfloat16),
        ],
        compiler_params=pltpu.CompilerParams(vmem_limit_bytes=VMEM),
        cost_estimate=pl.CostEstimate(
            flops=4 * rows * width * total,
            bytes_accessed=4 * width * total + 4 * rows * total,
            transcendentals=rows * total,
        ),
        name="ffn_fwd",
    )(x, gain_vec, up, down)


def ffn_bwd_kernel(x_ref, gain_ref, g_ref, slope_ref, up_ref, down_ref, gx_ref, gf_ref, gp_ref, gain_out, sum_s):
    step = pl.program_id(0)

    @pl.when(step == 0)
    def _():
        gf_ref[...] = (0.5 * g_ref[...]).astype(jnp.bfloat16)
        sum_s[...] = jnp.zeros_like(sum_s)

    grad_act = mult_trans(gf_ref[...], down_ref[...])
    grad_before = (grad_act * slope_ref[...].astype(jnp.float32)).astype(jnp.bfloat16)
    gp_ref[...] = grad_before
    sum_s[...] += mult_plain(grad_before, up_ref[...])

    @pl.when(step == pl.num_programs(0) - 1)
    def _():
        normal, inverse = norm_stats(x_ref[...].astype(jnp.float32))
        grad, gain_grad = norm_back(normal, inverse, gain_ref[...].astype(jnp.float32), sum_s[...])
        gx_ref[...] = (g_ref[...] + grad).astype(gx_ref.dtype)
        gain_out[...] = gain_grad


def ffn_bwd(x, gain_vec, grad, slope, up, down, out_type):
    rows, width = x.shape
    total = up.shape[0]
    still, vec, weight, hidden = ffn_blocks(rows, width, FF_BLOCK)
    return pl.pallas_call(
        ffn_bwd_kernel,
        grid=(total // FF_BLOCK,),
        in_specs=[still, vec, still, hidden, weight, weight],
        out_specs=[still, still, hidden, vec],
        out_shape=[
            jax.ShapeDtypeStruct((rows, width), out_type),
            jax.ShapeDtypeStruct((rows, width), jnp.bfloat16),
            jax.ShapeDtypeStruct((rows, total), jnp.bfloat16),
            jax.ShapeDtypeStruct((1, width), jnp.float32),
        ],
        scratch_shapes=[pltpu.VMEM((rows, width), jnp.float32)],
        compiler_params=pltpu.CompilerParams(vmem_limit_bytes=VMEM),
        cost_estimate=pl.CostEstimate(
            flops=4 * rows * width * total,
            bytes_accessed=4 * width * total + 4 * rows * total,
            transcendentals=0,
        ),
        name="ffn_bwd",
    )(x, gain_vec, grad, slope, up, down)


class Hops:
    def __init__(self, layers):
        self.layers = layers

    def send(self, block, dz=0, dc=0, dy=0, dx=0):
        pairs = []
        for z in range(self.layers):
            for c in range(2):
                for w in range(4):
                    to = ((z + dz) % self.layers * 2 + (c ^ dc)) * 4 + (w ^ (2 * dy + dx))
                    pairs.append(((z * 2 + c) * 4 + w, to))
        return lax.ppermute(block, ("z", "core", "y", "x"), pairs)

    def turn(self, block, step):
        pairs = []
        for z in range(self.layers):
            for c in range(2):
                for w in range(4):
                    to = (z * 2 + w // 2) * 4 + 2 * c + ((w % 2) ^ step)
                    pairs.append(((z * 2 + c) * 4 + w, to))
        return lax.ppermute(block, ("z", "core", "y", "x"), pairs)


def relative_waves(length, channels):
    step = 32
    rates = jnp.exp(
        jnp.arange(channels // 2).astype(jnp.float32) * (-2.0 * math.log(10000.0) / channels)
    )
    coarse = (length - 1 - step * jnp.arange(2 * length // step)).astype(jnp.float32)
    fine = jnp.arange(step).astype(jnp.float32)
    coarse, fine = coarse[:, None, None] * rates, fine[None, :, None] * rates
    sin_c, cos_c, sin_f, cos_f = jnp.sin(coarse), jnp.cos(coarse), jnp.sin(fine), jnp.cos(fine)
    return jnp.concatenate(
        [sin_c * cos_f - cos_c * sin_f, cos_c * cos_f + sin_c * sin_f], axis=2
    ).reshape(2 * length, channels)


def taps_forward(padded, kernel_f, count):
    total = jnp.zeros((count, padded.shape[1]), jnp.float32)
    for offset in range(KERNEL):
        total = total + padded[offset : offset + count] * kernel_f[offset]
    return total


def with_rim(hops, block, core):
    edge = jnp.where(core == 0, block[-16:], block[:16])
    got = hops.send(edge, dc=1)
    zero = jnp.zeros_like(got)
    low = jnp.where(core == 0, zero, got)[1:]
    high = jnp.where(core == 0, got, zero)[:RIM]
    return jnp.concatenate([low, block, high])


def per_chip(
    frames,
    lengths,
    masked,
    cotangent,
    first_gain,
    first_up,
    first_down,
    attn_gain,
    query_weight,
    key_weight,
    value_weight,
    out_weight,
    place_weight,
    content_bias,
    place_bias,
    conv_gain,
    glu_weight,
    depth_kernel,
    middle_gain,
    point_weight,
    second_gain,
    second_up,
    second_down,
    final_gain,
):
    core, y, x = lax.axis_index("core"), lax.axis_index("y"), lax.axis_index("x")
    wide_at = 2 * y + x
    layers = lax.axis_size("z")
    hops = Hops(layers)
    groups, quarter, channels = frames.shape
    rows = groups * quarter
    length = 2 * rows
    f32 = lambda v: v.astype(jnp.float32)
    low = lambda v: v.astype(jnp.bfloat16)

    def pick(flag, one, two):
        return jnp.where(flag, one, two), jnp.where(flag, two, one)

    def turn_in(block):
        swap = [lax.dynamic_index_in_dim(block, x ^ step, 0, keepdims=False) for step in range(2)]
        got = [hops.turn(swap[step], step) for step in range(2)]
        return jnp.concatenate(pick(x == 0, *got))

    def turn_out(block):
        parts = pick(x == 0, block[:quarter], block[quarter:])
        got = [hops.turn(parts[step], step) for step in range(2)]
        return jnp.stack(pick(x == 0, *got))

    frames_own = turn_in(frames)
    positions = wide_at * quarter + jnp.arange(quarter, dtype=jnp.int32)
    seed_weight = f32(masked) * f32(positions[None, :] < lengths[:, None])
    seed_own_low = low(f32(cotangent) * seed_weight[:, :, None])
    near_lengths = jnp.where(core == y, lengths, hops.send(lengths, dc=1))
    own_length = lax.dynamic_slice_in_dim(near_lengths, x, 1)
    own_rows = core * rows + jnp.arange(rows, dtype=jnp.int32)
    frame_ok = f32(own_rows < own_length[0])[:, None]

    def own_half(weight):
        count = weight.shape[0] // 2
        return lax.dynamic_slice_in_dim(weight, core * count, count)

    band = query_weight.shape[0] // 2
    odd = lax.rem(lax.axis_index("z"), 2)
    piece = band // 2

    def own_quarter(weight):
        return lax.dynamic_slice_in_dim(weight, core * band + odd * piece, piece)

    own_bias = own_half(jnp.stack([content_bias, place_bias], axis=1)).T
    attn_chunk = jnp.concatenate(
        [own_quarter(weight) for weight in (query_weight, key_weight, value_weight, place_weight)]
        + [jnp.pad(own_bias, ((0, 14), (0, channels - band)))]
    )
    (up_first, down_first), attn_all = gather_all(layers, [first_up, first_down], attn_chunk, 1)
    conv_chunk = jnp.concatenate([own_half(out_weight), own_half(point_weight), own_half(glu_weight)])
    conv_chunk, attn_all = lax.optimization_barrier((conv_chunk, attn_all))
    conv_all = lax.all_gather(conv_chunk, ("y", "x"), axis=0)
    attn_all = attn_all.reshape(2, 4, -1, channels)

    def heads_of(at):
        rows_of = attn_all[:, :, at * piece : (at + 1) * piece]
        return rows_of.transpose(1, 0, 2, 3).reshape(4 * band, channels)

    query_own, key_own, value_own, place_own = (heads_of(at) for at in range(4))
    own_biases = attn_all[0, :, 4 * piece : 4 * piece + 2, :band].transpose(1, 0, 2).reshape(2, 4 * band)
    conv_other = hops.send(conv_all, dc=1)
    conv_both = jnp.stack(pick(core == 0, conv_all, conv_other), axis=1)
    full_out = conv_both[:, :, :band].reshape(8 * band, channels)
    full_point = conv_both[:, :, band : 2 * band].reshape(8 * band, channels)
    full_glu = conv_both[:, :, 2 * band :].reshape(16 * band, channels)

    stream1, first_low, first_act, first_slope = ffn_fwd(
        frames_own, first_gain[None], up_first, down_first
    )
    stream1, seed_own_low = lax.optimization_barrier((stream1, seed_own_low))
    normed_attn, attn_pull = jax.vjp(norm_rows, stream1, f32(attn_gain))
    attn_half = low(normed_attn)
    attn_other = hops.send(attn_half, dc=1)
    attn_low = jnp.concatenate(pick(core == 0, attn_half, attn_other))
    rel_table = low(relative_waves(length, channels))
    query = low(mult_trans(attn_low, query_own))
    key = low(mult_trans(attn_low, key_own))
    value = low(mult_trans(attn_low, value_own))
    place = low(mult_trans(rel_table, place_own))
    attended, prob, (up_second, down_second) = attend_fwd(
        own_length,
        query,
        key,
        value,
        place,
        own_biases[:1],
        own_biases[1:],
        ROWS_FWD,
        layers,
        [second_up, second_down],
        4,
    )

    def halves(matrix):
        own = lax.dynamic_slice_in_dim(matrix, core * rows, rows)
        other = lax.dynamic_slice_in_dim(matrix, (1 - core) * rows, rows)
        return own, other

    att_own, att_other = halves(attended)
    att_parts = pick(core == 0, att_own, hops.send(att_other, dc=1))
    framed = jnp.stack([part.reshape(rows, 4, band) for part in att_parts], axis=2)
    framed = framed.reshape(rows, 8 * band)
    stream2 = stream1 + mult_plain(framed, full_out)
    normed_conv, conv_pull = jax.vjp(norm_rows, stream2, f32(conv_gain))
    conv_low = low(normed_conv)
    glu_in = mult_trans(conv_low, full_glu)
    linear = glu_in[:, :channels]
    gating = jax.nn.sigmoid(glu_in[:, channels:])
    gated = low(linear * gating * frame_ok)
    padded = with_rim(hops, gated, core)
    kernel_f = f32(depth_kernel)
    conv_out = taps_forward(padded, kernel_f, rows)
    middle, middle_pull = jax.vjp(norm_rows, conv_out, f32(middle_gain))
    swished = low(jax.nn.silu(middle))
    stream3 = stream2 + mult_trans(swished, full_point)
    stream4, second_low, second_act, second_slope = ffn_fwd(
        stream3, second_gain[None], up_second, down_second
    )
    final_rows, final_pull = jax.vjp(norm_rows, stream4, f32(final_gain))
    output = turn_out(low(final_rows))

    seed_own = turn_in(seed_own_low)
    grad4, grad_final_gain = final_pull(f32(seed_own))

    grad3, grad_out2, grad_before2, grad_second_gain = ffn_bwd(
        stream3, second_gain[None], grad4, second_slope, up_second, down_second, jnp.float32
    )
    grad_down_second = low(mult_rows(second_act, grad_out2))
    grad_up_second = low(mult_rows(grad_before2, second_low))
    grad_branch = low(grad3)
    grad_point = mult_rows(grad_branch, swished)
    grad_middle = mult_plain(grad_branch, full_point) * silu_slope(middle)
    grad_conv, grad_middle_gain = middle_pull(grad_middle)
    conv_grad_low = low(grad_conv)
    grad_padded = with_rim(hops, conv_grad_low, core)
    grad_gated = taps_forward(grad_padded, kernel_f[::-1], rows)
    grad_kernel = jnp.stack(
        [
            jnp.sum(f32(padded[offset : offset + rows]) * f32(conv_grad_low), axis=0)
            for offset in range(KERNEL)
        ]
    )
    grad_gated = grad_gated * frame_ok
    grad_glu_in = low(
        jnp.concatenate(
            [grad_gated * gating, grad_gated * linear * gating * (1.0 - gating)], axis=1
        )
    )
    grad_glu = mult_rows(grad_glu_in, conv_low)
    grad_conv_in, grad_conv_gain = conv_pull(mult_plain(grad_glu_in, full_glu))
    grad2 = grad3 + grad_conv_in
    grad_attn = low(grad2)
    grad_out = mult_rows(framed, grad_attn)
    grad_framed = low(mult_trans(grad_attn, full_out))
    grad_parts = grad_framed.reshape(rows, 4, 2, band)
    grad_parts = [grad_parts[:, :, at].reshape(rows, 4 * band) for at in range(2)]
    grad_kept, grad_sent = pick(core == 0, *grad_parts)
    grad_heads = jnp.concatenate(pick(core == 0, grad_kept, hops.send(grad_sent, dc=1)))

    def by_place(matrix, cores):
        blocks = low(matrix).reshape(4, cores, layers, -1, channels)
        return blocks.transpose(2, 1, 0, 3, 4)

    conv_part = jnp.concatenate(
        [by_place(part, 2) for part in (grad_out, grad_point, grad_glu)], axis=3
    )
    *attn_grads, sum_up_second, sum_down_second, conv_sums = attend_bwd(
        query,
        key,
        value,
        place,
        own_biases[:1],
        own_biases[1:],
        prob,
        grad_heads,
        ROWS_BWD,
        layers,
        2,
        [(grad_up_second, 2), (grad_down_second, 2), (conv_part, 2)],
        3,
    )
    grad_query, grad_key, grad_value, grad_place, grad_biases = attn_grads
    grad_query_w = mult_rows(grad_query, attn_low)
    grad_key_w = mult_rows(grad_key, attn_low)
    grad_value_w = mult_rows(grad_value, attn_low)
    grad_place_w = mult_rows(grad_place, rel_table)
    attn_part = jnp.concatenate(
        [
            low(part).reshape(4, layers, -1, channels)
            for part in (grad_query_w, grad_key_w, grad_value_w, grad_place_w)
        ],
        axis=2,
    )
    attn_part, grad_query = lax.optimization_barrier((attn_part, grad_query))
    attn_part = lax.psum_scatter(attn_part, ("y", "x"), scatter_dimension=0, tiled=False)
    grad_normed = (
        mult_plain(grad_query, query_own)
        + mult_plain(grad_key, key_own)
        + mult_plain(grad_value, value_own)
    )
    normed_own, normed_other = halves(grad_normed)
    grad_attn_in, grad_attn_gain = attn_pull(normed_own + f32(hops.send(low(normed_other), dc=1)))
    grad1 = grad2 + grad_attn_in
    grad0, grad_out1, grad_before1, grad_first_gain = ffn_bwd(
        frames_own, first_gain[None], grad1, first_slope, up_first, down_first, jnp.bfloat16
    )
    grad_input = turn_out(grad0)

    spread = jnp.zeros((2, 4, 2, band), jnp.float32)
    spread = lax.dynamic_update_slice(
        spread, grad_biases[:2].reshape(2, 4, 1, band), (0, 0, core, 0)
    ).reshape(2, channels)
    gains = (
        grad_conv_gain,
        grad_middle_gain,
        grad_second_gain[0],
        grad_final_gain,
        grad_first_gain[0],
        grad_attn_gain,
    )
    small = jnp.concatenate([jnp.stack(gains), spread, grad_kernel])
    small = jnp.pad(small, ((0, -small.shape[0] % 8), (0, 0)))
    sum_up_first, sum_down_first, attn_sums, small = reduce_all(
        layers,
        attn_part,
        [(grad_before1, first_low), (first_act, grad_out1)],
        small,
        2,
    )

    def owned(sums, start, count):
        return f32(sums[:, :, start : start + count]).reshape(-1, channels)

    step = band // layers
    total_out, total_point = owned(conv_sums, 0, step), owned(conv_sums, step, step)
    total_glu = owned(conv_sums, 2 * step, 2 * step)
    total_query, total_key, total_value, total_place = (
        owned(attn_sums, at * step, step) for at in range(4)
    )
    own_bias_grad = lax.dynamic_slice_in_dim(small[6:8], wide_at * 2 * band, 2 * band, 1)
    return (
        output,
        grad_input,
        small[4],
        sum_up_first,
        sum_down_first,
        small[5],
        total_query,
        total_key,
        total_value,
        total_out,
        total_place,
        own_bias_grad[0],
        own_bias_grad[1],
        small[0],
        total_glu,
        small[8 : 8 + KERNEL],
        small[1],
        total_point,
        small[2],
        sum_up_second,
        sum_down_second,
        small[3],
    )


def per_device(
    frames,
    lengths,
    masked,
    cotangent,
    first_gain,
    first_up,
    first_down,
    attn_gain,
    query_weight,
    key_weight,
    value_weight,
    out_weight,
    place_weight,
    content_bias,
    place_bias,
    conv_gain,
    glu_weight,
    depth_kernel,
    middle_gain,
    point_weight,
    second_gain,
    second_up,
    second_down,
    final_gain,
):
    groups, frames_dev, channels = frames.shape
    row_count = groups * frames_dev
    length = frames_dev * lax.axis_size("wide")
    score_scale = 1.0 / math.sqrt(HEAD_DIM)
    positions = lax.axis_index("wide") * frames_dev + jnp.arange(frames_dev, dtype=jnp.int32)
    frame_grid = (positions[None, :] < lengths[:, None]).astype(jnp.float32)
    frame_ok = frame_grid.reshape(row_count, 1)
    key_ok = jnp.arange(length, dtype=jnp.int32)[None, :] < lengths[:, None]
    stream0 = frames.reshape(row_count, channels).astype(jnp.float32)
    up_first, down_first = gather_ffn(first_up, first_down)
    stream1, saved_first = ffn_forward(
        stream0, first_gain.astype(jnp.float32), up_first, down_first
    )
    full_query, full_key, full_value, full_out, full_glu, full_point = (
        lax.all_gather(query_weight, "wide", axis=0, tiled=True),
        lax.all_gather(key_weight, "wide", axis=0, tiled=True),
        lax.all_gather(value_weight, "wide", axis=0, tiled=True),
        lax.all_gather(out_weight, "wide", axis=0, tiled=True),
        lax.all_gather(glu_weight, "wide", axis=0, tiled=True),
        lax.all_gather(point_weight, "wide", axis=0, tiled=True),
    )
    normed_attn, attn_pull = jax.vjp(norm_rows, stream1, attn_gain.astype(jnp.float32))
    attn_low = normed_attn.astype(jnp.bfloat16)
    query_frames = (
        mult_trans(attn_low, full_query).astype(jnp.bfloat16).reshape(groups, frames_dev, -1)
    )
    key_frames = mult_trans(attn_low, full_key).astype(jnp.bfloat16).reshape(groups, frames_dev, -1)
    value_frames = (
        mult_trans(attn_low, full_value).astype(jnp.bfloat16).reshape(groups, frames_dev, -1)
    )
    heads_query, heads_key, heads_value = (
        lax.all_to_all(query_frames, "wide", split_axis=2, concat_axis=1, tiled=True),
        lax.all_to_all(key_frames, "wide", split_axis=2, concat_axis=1, tiled=True),
        lax.all_to_all(value_frames, "wide", split_axis=2, concat_axis=1, tiled=True),
    )
    local_width = heads_query.shape[2]
    head_count = local_width // HEAD_DIM
    rel_table = relative_table(length, channels).astype(jnp.bfloat16)
    place_rows = (
        mult_trans(rel_table, place_weight)
        .astype(jnp.bfloat16)
        .reshape(2 * length - 1, head_count, HEAD_DIM)
    )
    bias_first = content_bias.astype(jnp.float32).reshape(head_count, HEAD_DIM)
    bias_second = place_bias.astype(jnp.float32).reshape(head_count, HEAD_DIM)
    split_query = heads_query.reshape(groups, length, head_count, HEAD_DIM)
    split_key = heads_key.reshape(groups, length, head_count, HEAD_DIM)
    split_value = heads_value.reshape(groups, length, head_count, HEAD_DIM)
    forward_heads = jax.vmap(
        partial(head_forward, block_rows=QBLK, score_scale=score_scale),
        in_axes=(1, 1, 1, 1, 0, 0, None),
        out_axes=(1, 0),
    )

    def attend_utt(unit_items):
        return forward_heads(
            unit_items[0],
            unit_items[1],
            unit_items[2],
            place_rows,
            bias_first,
            bias_second,
            unit_items[3],
        )

    attended, log_total = lax.map(attend_utt, (split_query, split_key, split_value, key_ok))
    framed = lax.all_to_all(
        attended.reshape(groups, length, local_width),
        "wide",
        split_axis=1,
        concat_axis=2,
        tiled=True,
    ).reshape(row_count, -1)
    stream2 = stream1 + mult_plain(framed, full_out)
    normed_conv, conv_pull = jax.vjp(norm_rows, stream2, conv_gain.astype(jnp.float32))
    conv_low = normed_conv.astype(jnp.bfloat16)
    glu_in = mult_trans(conv_low, full_glu)
    linear = glu_in[:, :channels]
    gating = jax.nn.sigmoid(glu_in[:, channels:])
    gated = (linear * gating * frame_ok).astype(jnp.bfloat16).reshape(groups, frames_dev, channels)
    padded = with_halo(gated, (("wide", 1),), RIM)
    kernel_f = depth_kernel.astype(jnp.float32)
    conv_out = jnp.zeros((groups, frames_dev, channels), jnp.float32)
    for offset in range(KERNEL):
        conv_out = conv_out + padded[:, offset : offset + frames_dev, :] * kernel_f[offset]
    conv_out = conv_out.reshape(row_count, channels)
    middle, middle_pull = jax.vjp(norm_rows, conv_out, middle_gain.astype(jnp.float32))
    swished = jax.nn.silu(middle).astype(jnp.bfloat16)
    stream3 = stream2 + mult_trans(swished, full_point)
    up_second, down_second = gather_ffn(second_up, second_down)
    stream4, saved_second = ffn_forward(
        stream3, second_gain.astype(jnp.float32), up_second, down_second
    )
    final_rows, final_pull = jax.vjp(norm_rows, stream4, final_gain.astype(jnp.float32))
    output = final_rows.astype(jnp.bfloat16).reshape(groups, frames_dev, channels)
    seed_weight = (masked.astype(jnp.float32) * frame_grid).reshape(row_count, 1)
    seed_grad = cotangent.reshape(row_count, channels).astype(jnp.float32) * seed_weight
    grad4, grad_final_gain = final_pull(seed_grad)
    back_up_second, back_down_second = gather_ffn(second_up, second_down)
    grad3, grad_second_gain, grad_up_second, grad_down_second = ffn_backward(
        grad4, saved_second, back_up_second, back_down_second
    )
    summed_second = sum_ffn(grad_up_second, grad_down_second)
    grad_branch = grad3.astype(jnp.bfloat16)
    grad_point = mult_rows(grad_branch, swished)
    grad_middle = mult_plain(grad_branch, full_point) * silu_slope(middle)
    grad_conv, grad_middle_gain = middle_pull(grad_middle)
    conv_grad_low = grad_conv.astype(jnp.bfloat16).reshape(groups, frames_dev, channels)
    grad_padded = with_halo(conv_grad_low, (("wide", 1),), RIM)
    grad_gated = jnp.zeros((groups, frames_dev, channels), jnp.float32)
    kernel_rows = []
    for offset in range(KERNEL):
        grad_gated = (
            grad_gated
            + grad_padded[:, 2 * RIM - offset : 2 * RIM - offset + frames_dev, :] * kernel_f[offset]
        )
        kernel_rows.append(
            jnp.einsum(
                "rzn,rzn->n",
                padded[:, offset : offset + frames_dev, :],
                conv_grad_low,
                preferred_element_type=jnp.float32,
            )
        )
    grad_kernel = jnp.stack(kernel_rows)
    grad_gated = grad_gated.reshape(row_count, channels) * frame_ok
    grad_glu_in = jnp.concatenate(
        [grad_gated * gating, grad_gated * linear * gating * (1.0 - gating)], axis=1
    ).astype(jnp.bfloat16)
    grad_glu = mult_rows(grad_glu_in, conv_low)
    grad_conv_in, grad_conv_gain = conv_pull(mult_plain(grad_glu_in, full_glu))
    grad2 = grad3 + grad_conv_in
    grad_attn = grad2.astype(jnp.bfloat16)
    grad_out = mult_rows(framed, grad_attn)
    grad_framed = (
        mult_trans(grad_attn, full_out).astype(jnp.bfloat16).reshape(groups, frames_dev, -1)
    )
    grad_heads = lax.all_to_all(grad_framed, "wide", split_axis=2, concat_axis=1, tiled=True)
    backward_heads = jax.vmap(
        partial(head_backward, block_rows=QBLK, score_scale=score_scale),
        in_axes=(1, 1, 1, 1, 0, 0, None, 0, 1),
        out_axes=(1, 1, 1, 1, 0, 0),
    )

    def attend_back(unit_items):
        return backward_heads(
            unit_items[0],
            unit_items[1],
            unit_items[2],
            place_rows,
            bias_first,
            bias_second,
            unit_items[3],
            unit_items[4],
            unit_items[5],
        )

    grad_query_h, grad_key_h, grad_value_h, grad_place_h, grad_bias_first, grad_bias_second = (
        lax.map(
            attend_back,
            (
                split_query,
                split_key,
                split_value,
                key_ok,
                log_total,
                grad_heads.reshape(groups, length, head_count, HEAD_DIM),
            ),
        )
    )
    back_query, back_key, back_value = (
        lax.all_to_all(
            grad_query_h.reshape(groups, length, local_width),
            "wide",
            split_axis=1,
            concat_axis=2,
            tiled=True,
        ),
        lax.all_to_all(
            grad_key_h.reshape(groups, length, local_width),
            "wide",
            split_axis=1,
            concat_axis=2,
            tiled=True,
        ),
        lax.all_to_all(
            grad_value_h.reshape(groups, length, local_width),
            "wide",
            split_axis=1,
            concat_axis=2,
            tiled=True,
        ),
    )
    back_query = back_query.reshape(row_count, -1)
    back_key = back_key.reshape(row_count, -1)
    back_value = back_value.reshape(row_count, -1)
    grad_query_w = mult_rows(back_query, attn_low)
    grad_key_w = mult_rows(back_key, attn_low)
    grad_value_w = mult_rows(back_value, attn_low)
    grad_normed = (
        mult_plain(back_query, full_query)
        + mult_plain(back_key, full_key)
        + mult_plain(back_value, full_value)
    )
    grad_attn_in, grad_attn_gain = attn_pull(grad_normed)
    grad1 = grad2 + grad_attn_in
    grad_place_w = jnp.einsum(
        "urc,rd->cd",
        grad_place_h.reshape(groups, 2 * length - 1, local_width),
        rel_table,
        preferred_element_type=jnp.float32,
    )
    grad_content = jnp.sum(grad_bias_first, axis=0).reshape(local_width)
    grad_place_b = jnp.sum(grad_bias_second, axis=0).reshape(local_width)
    back_up_first, back_down_first = gather_ffn(first_up, first_down)
    grad0, grad_first_gain, grad_up_first, grad_down_first = ffn_backward(
        grad1, saved_first, back_up_first, back_down_first
    )
    summed_first = sum_ffn(grad_up_first, grad_down_first)
    mixer_grads = (
        lax.psum_scatter(
            grad_query_w.astype(jnp.bfloat16), "wide", scatter_dimension=0, tiled=True
        ).astype(jnp.float32),
        lax.psum_scatter(
            grad_key_w.astype(jnp.bfloat16), "wide", scatter_dimension=0, tiled=True
        ).astype(jnp.float32),
        lax.psum_scatter(
            grad_value_w.astype(jnp.bfloat16), "wide", scatter_dimension=0, tiled=True
        ).astype(jnp.float32),
        lax.psum_scatter(
            grad_out.astype(jnp.bfloat16), "wide", scatter_dimension=0, tiled=True
        ).astype(jnp.float32),
        lax.psum_scatter(
            grad_glu.astype(jnp.bfloat16), "wide", scatter_dimension=0, tiled=True
        ).astype(jnp.float32),
        lax.psum_scatter(
            grad_point.astype(jnp.bfloat16), "wide", scatter_dimension=0, tiled=True
        ).astype(jnp.float32),
    )
    totals = (
        lax.psum(mixer_grads[0].astype(jnp.bfloat16), "utt").astype(jnp.float32),
        lax.psum(mixer_grads[1].astype(jnp.bfloat16), "utt").astype(jnp.float32),
        lax.psum(mixer_grads[2].astype(jnp.bfloat16), "utt").astype(jnp.float32),
        lax.psum(mixer_grads[3].astype(jnp.bfloat16), "utt").astype(jnp.float32),
        lax.psum(mixer_grads[4].astype(jnp.bfloat16), "utt").astype(jnp.float32),
        lax.psum(mixer_grads[5].astype(jnp.bfloat16), "utt").astype(jnp.float32),
        lax.psum(grad_place_w.astype(jnp.bfloat16), "utt").astype(jnp.float32),
        lax.psum(grad_content.astype(jnp.bfloat16), "utt").astype(jnp.float32),
        lax.psum(grad_place_b.astype(jnp.bfloat16), "utt").astype(jnp.float32),
    )
    small_grads = lax.psum(
        (
            grad_first_gain,
            grad_attn_gain,
            grad_conv_gain,
            grad_middle_gain,
            grad_second_gain,
            grad_final_gain,
            grad_kernel,
        ),
        ("utt", "wide"),
    )
    grad_input = grad0.astype(jnp.bfloat16).reshape(groups, frames_dev, channels)
    return (
        output,
        grad_input,
        small_grads[0],
        summed_first[0],
        summed_first[1],
        small_grads[1],
        totals[0],
        totals[1],
        totals[2],
        totals[3],
        totals[6],
        totals[7],
        totals[8],
        small_grads[2],
        totals[4],
        small_grads[6],
        small_grads[3],
        totals[5],
        small_grads[4],
        summed_second[0],
        summed_second[1],
        small_grads[5],
    )


def solution(mesh):
    shape = dict(mesh.shape)
    if shape["wide"] == 4 and shape["utt"] % 4 == 0:
        mesh = jax.sharding.Mesh(
            mesh.devices.reshape(shape["utt"] // 2, 2, 2, 2), ("z", "core", "y", "x")
        )
        utt, wide, body = ("z", "core"), ("y", "x"), per_chip
    else:
        utt, wide, body = "utt", "wide", per_device
    every = (utt, wide) if utt == "utt" else (*utt, *wide)
    in_specs = (
        P(utt, wide, None),
        P(utt),
        P(utt, wide),
        P(utt, wide, None),
        P(),
        P(every, None),
        P(every, None),
        P(),
        P(wide, None),
        P(wide, None),
        P(wide, None),
        P(wide, None),
        P(wide, None),
        P(wide),
        P(wide),
        P(),
        P(wide, None),
        P(),
        P(),
        P(wide, None),
        P(),
        P(every, None),
        P(every, None),
        P(),
    )
    out_specs = (
        P(utt, wide, None),
        P(utt, wide, None),
        P(),
        P(every, None),
        P(every, None),
        P(),
        P(wide, None),
        P(wide, None),
        P(wide, None),
        P(wide, None),
        P(wide, None),
        P(wide),
        P(wide),
        P(),
        P(wide, None),
        P(),
        P(),
        P(wide, None),
        P(),
        P(every, None),
        P(every, None),
        P(),
    )
    return jax.shard_map(
        body, mesh=mesh, in_specs=in_specs, out_specs=out_specs, check_vma=False
    )
```

```python
from functools import partial
import math

import jax
import jax.numpy as jnp
from jax import lax
from jax.experimental import pallas as pl
from jax.experimental.pallas import tpu as pltpu
from jax.sharding import PartitionSpec as P

HEAD_DIM = 64
KERNEL = 31
QBLK = 512
RIM = 15
PAIR = 128
ROWS_FWD = 256
ROWS_BWD = 256
FF_BLOCK = 512
VMEM = 58 * 2**20


EPSILON = 1e-05
MASKED_SCORE = -1e30


def with_halo(block, sides, width):
    for axis, dim in sides:
        count = lax.axis_size(axis)
        forward = [(i, i + 1) for i in range(count - 1)]
        backward = [(target, source) for source, target in forward]
        low = lax.ppermute(
            lax.slice_in_dim(block, block.shape[dim] - width, None, axis=dim), axis, forward
        )
        high = lax.ppermute(lax.slice_in_dim(block, 0, width, axis=dim), axis, backward)
        block = jnp.concatenate([low, block, high], axis=dim)
    return block


def norm_rows(values, gain_vec):
    average = jnp.mean(values, axis=-1, keepdims=True)
    centred = values - average
    spread = jnp.mean(centred * centred, axis=-1, keepdims=True)
    return centred * lax.rsqrt(spread + EPSILON) * gain_vec


def silu_slope(before):
    squash = jax.nn.sigmoid(before)
    return squash * (1.0 + before * (1.0 - squash))


def mult_trans(first_mat, second_mat):
    return lax.dot_general(
        first_mat, second_mat, (((1,), (1,)), ((), ())), preferred_element_type=jnp.float32
    )


def mult_plain(first_mat, second_mat):
    return jnp.dot(first_mat, second_mat, preferred_element_type=jnp.float32)


def mult_rows(first_mat, second_mat):
    return lax.dot_general(
        first_mat, second_mat, (((0,), (0,)), ((), ())), preferred_element_type=jnp.float32
    )


def relative_table(length, channels):
    offsets = length - 1 - jnp.arange(2 * length - 1).astype(jnp.float32)
    rates = jnp.exp(
        jnp.arange(channels // 2).astype(jnp.float32) * (-2.0 * math.log(10000.0) / channels)
    )
    angles = offsets[:, None] * rates[None, :]
    return jnp.concatenate([jnp.sin(angles), jnp.cos(angles)], axis=1)


def skew_rows(reversed_scores):
    block_rows, span = reversed_scores.shape
    flat = reversed_scores.reshape(-1)[block_rows - 1 : block_rows - 1 + block_rows * (span - 1)]
    return flat.reshape(block_rows, span - 1)[:, : span - block_rows + 1]


def unskew_rows(grad_scores, span):
    block_rows, length = grad_scores.shape
    padded = jnp.pad(grad_scores, ((0, 0), (0, span - 1 - length)))
    flat = jnp.pad(padded.reshape(-1), (block_rows - 1, 1))
    return flat.reshape(block_rows, span)


def gather_ffn(up_rows, down_rows):
    return (
        lax.all_gather(up_rows, ("utt", "wide"), axis=0, tiled=True),
        lax.all_gather(down_rows, ("utt", "wide"), axis=0, tiled=True),
    )


def sum_ffn(grad_up, grad_down):
    return (
        lax.psum_scatter(grad_up, ("utt", "wide"), scatter_dimension=0, tiled=True),
        lax.psum_scatter(grad_down, ("utt", "wide"), scatter_dimension=0, tiled=True),
    )


def ffn_forward(stream, gain_vec, up_full, down_full):
    normed, norm_pull = jax.vjp(norm_rows, stream, gain_vec)
    normed_low = normed.astype(jnp.bfloat16)
    before = mult_trans(normed_low, up_full)
    active_low = jax.nn.silu(before).astype(jnp.bfloat16)
    return (
        stream + 0.5 * mult_plain(active_low, down_full),
        (norm_pull, normed_low, before, active_low),
    )


def ffn_backward(grad_stream, saved_ffn, up_full, down_full):
    norm_pull, normed_low, before, active_low = saved_ffn
    grad_out = (0.5 * grad_stream).astype(jnp.bfloat16)
    grad_down = mult_rows(active_low, grad_out)
    grad_before = (mult_trans(grad_out, down_full) * silu_slope(before)).astype(jnp.bfloat16)
    grad_up = mult_rows(grad_before, normed_low)
    grad_input, grad_gain = norm_pull(mult_plain(grad_before, up_full))
    return (grad_stream + grad_input, grad_gain, grad_up, grad_down)


def head_forward(
    query_rows,
    key_rows,
    value_rows,
    place_rows,
    bias_first,
    bias_second,
    key_ok,
    block_rows,
    score_scale,
):
    length, head_width = query_rows.shape
    with_u = (query_rows.astype(jnp.float32) + bias_first).astype(jnp.bfloat16)
    with_v = (query_rows.astype(jnp.float32) + bias_second).astype(jnp.bfloat16)

    def one_block(block_index):
        first_row = block_index * block_rows
        block_u = lax.dynamic_slice_in_dim(with_u, first_row, block_rows, 0)
        block_v = lax.dynamic_slice_in_dim(with_v, first_row, block_rows, 0)
        near_rows = lax.dynamic_slice_in_dim(
            place_rows, length - block_rows - first_row, block_rows + length - 1, 0
        )
        scores = (
            mult_trans(block_u, key_rows) + skew_rows(mult_trans(block_v, near_rows))
        ) * score_scale
        scores = jnp.where(key_ok[None, :], scores, MASKED_SCORE)
        highest = jnp.max(scores, axis=1, keepdims=True)
        weights = jnp.exp(scores - highest)
        running = jnp.sum(weights, axis=1, keepdims=True)
        attend_prob = (weights / running).astype(jnp.bfloat16)
        return (
            mult_plain(attend_prob, value_rows).astype(jnp.bfloat16),
            (highest + jnp.log(running))[:, 0],
        )

    attended, log_total = lax.map(one_block, jnp.arange(length // block_rows, dtype=jnp.int32))
    return (attended.reshape(length, head_width), log_total.reshape(length))


def head_backward(
    query_rows,
    key_rows,
    value_rows,
    place_rows,
    bias_first,
    bias_second,
    key_ok,
    log_total,
    grad_mixed,
    block_rows,
    score_scale,
):
    length, head_width = query_rows.shape
    span = block_rows + length - 1
    with_u = (query_rows.astype(jnp.float32) + bias_first).astype(jnp.bfloat16)
    with_v = (query_rows.astype(jnp.float32) + bias_second).astype(jnp.bfloat16)

    def one_block(carried, block_index):
        grad_key, grad_value, grad_place = carried
        first_row = block_index * block_rows
        place_first = length - block_rows - first_row
        block_u = lax.dynamic_slice_in_dim(with_u, first_row, block_rows, 0)
        block_v = lax.dynamic_slice_in_dim(with_v, first_row, block_rows, 0)
        near_rows = lax.dynamic_slice_in_dim(place_rows, place_first, span, 0)
        block_total = lax.dynamic_slice_in_dim(log_total, first_row, block_rows, 0)
        block_grad = lax.dynamic_slice_in_dim(grad_mixed, first_row, block_rows, 0)
        scores = (
            mult_trans(block_u, key_rows) + skew_rows(mult_trans(block_v, near_rows))
        ) * score_scale
        scores = jnp.where(key_ok[None, :], scores, MASKED_SCORE)
        attend_prob = jnp.exp(scores - block_total[:, None])
        grad_prob = mult_trans(block_grad, value_rows)
        inner = jnp.sum(attend_prob * grad_prob, axis=1, keepdims=True)
        grad_score = jnp.where(key_ok[None, :], attend_prob * (grad_prob - inner), 0.0).astype(
            jnp.bfloat16
        )
        grad_value = grad_value + mult_rows(attend_prob.astype(jnp.bfloat16), block_grad)
        grad_with_u = mult_plain(grad_score, key_rows) * score_scale
        grad_key = grad_key + mult_rows(grad_score, block_u) * score_scale
        spread_grad = unskew_rows(grad_score, span)
        grad_with_v = mult_plain(spread_grad, near_rows) * score_scale
        place_part = (
            lax.dynamic_slice_in_dim(grad_place, place_first, span, 0)
            + mult_rows(spread_grad, block_v) * score_scale
        )
        grad_place = lax.dynamic_update_slice_in_dim(grad_place, place_part, place_first, 0)
        return ((grad_key, grad_value, grad_place), (grad_with_u, grad_with_v))

    zero_rows = jnp.zeros((length, head_width), jnp.float32)
    zero_place = jnp.zeros((2 * length - 1, head_width), jnp.float32)
    (grad_key, grad_value, grad_place), (grad_with_u, grad_with_v) = lax.scan(
        one_block,
        (zero_rows, zero_rows, zero_place),
        jnp.arange(length // block_rows, dtype=jnp.int32),
    )
    grad_with_u = grad_with_u.reshape(length, head_width)
    grad_with_v = grad_with_v.reshape(length, head_width)
    grad_query = (grad_with_u + grad_with_v).astype(jnp.bfloat16)
    return (
        grad_query,
        grad_key.astype(jnp.bfloat16),
        grad_value.astype(jnp.bfloat16),
        grad_place.astype(jnp.bfloat16),
        jnp.sum(grad_with_u, axis=0),
        jnp.sum(grad_with_v, axis=0),
    )


def biased(q_ref, bias_ref, scale):
    return ((q_ref[...].astype(jnp.float32) + bias_ref[...].astype(jnp.float32)).astype(jnp.bfloat16).astype(jnp.float32) * scale).astype(jnp.bfloat16)

def attend_fwd_kernel(len_ref, q_ref, k_ref, v_ref, place_ref, cb_ref, pb_ref, out_ref, prob_ref, *, scale):
    rows = q_ref.shape[0]
    length = k_ref.shape[0]
    span = rows + length
    first = pl.multiple_of(length - rows - pl.program_id(1) * rows, rows)
    lanes = lax.broadcasted_iota(jnp.int32, (rows, PAIR), 1)
    with_u = biased(q_ref, cb_ref, scale)
    with_v = biased(q_ref, pb_ref, scale)
    window = place_ref[pl.ds(first, span), :]
    key_ok = lax.broadcasted_iota(jnp.int32, (rows, length), 1) < len_ref[0]
    zero = jnp.zeros_like(with_u)
    mixed = []
    for head in range(2):
        mine = (lanes // HEAD_DIM) == head
        place_part = mult_trans(jnp.where(mine, with_v, zero), window)
        place_part = pltpu.roll(place_part, span - rows + 1, 1, stride=1, stride_axis=0)
        scores = mult_trans(jnp.where(mine, with_u, zero), k_ref[...]) + place_part[:, :length]
        scores = jnp.where(key_ok, scores, MASKED_SCORE)
        weights = jnp.exp(scores - jnp.max(scores, axis=1, keepdims=True))
        total = jnp.sum(weights, axis=1, keepdims=True)
        prob = (weights * (1.0 / total)).astype(jnp.bfloat16)
        prob_ref[head] = prob
        mixed.append(mult_plain(prob, v_ref[...]))
    out_ref[...] = jnp.where(lanes < HEAD_DIM, mixed[0], mixed[1]).astype(jnp.bfloat16)

def attend_fwd_gather_kernel(layers, count, blocks, *refs, scale):
    ins, shards, refs = refs[:7], refs[7 : 7 + count], refs[7 + count :]
    outs, fulls, sems = refs[:2], refs[2 : 2 + count], refs[2 + count :]
    at = pl.program_id(0) * pl.num_programs(1) + pl.program_id(1)
    plan = gather_plan(layers, shards, fulls, (), *sems)
    run_between(*plan, at, blocks, partial(attend_fwd_kernel, *ins, *outs, scale=scale))


def attend_fwd(length_arr, q, k, v, place, cb, pb, rows, layers, shards, collective_id):
    length, width = q.shape
    pairs = width // PAIR
    count = len(shards)
    shard = shards[0].shape
    part = pl.BlockSpec((rows, PAIR), lambda p, i: (i, p))
    full = pl.BlockSpec((length, PAIR), lambda p, i: (0, p))
    tall = pl.BlockSpec((2 * length, PAIR), lambda p, i: (0, p))
    vec = pl.BlockSpec((1, PAIR), lambda p, i: (0, p))
    far = [pl.BlockSpec(memory_space=pl.ANY)] * count
    blocks = pairs * (length // rows)
    attended, prob, *fulls = pl.pallas_call(
        partial(attend_fwd_gather_kernel, layers, count, blocks, scale=1.0 / math.sqrt(HEAD_DIM)),
        grid=(pairs, length // rows),
        in_specs=[pl.BlockSpec(memory_space=pltpu.SMEM), part, full, full, tall, vec, vec] + far,
        out_specs=[part, pl.BlockSpec((2, rows, length), lambda p, i: (p, i, 0))] + far,
        out_shape=[
            jax.ShapeDtypeStruct((length, width), jnp.bfloat16),
            jax.ShapeDtypeStruct((2 * pairs, length, length), jnp.bfloat16),
        ]
        + [jax.ShapeDtypeStruct((layers, 2, 2, 2, *shard), jnp.bfloat16)] * count,
        scratch_shapes=gather_sems(count, layers),
        compiler_params=pltpu.CompilerParams(
            vmem_limit_bytes=VMEM, collective_id=collective_id, has_side_effects=True
        ),
        cost_estimate=pl.CostEstimate(
            flops=40 * 10**9, bytes_accessed=20 * 2**20, transcendentals=2 * pairs * length * length
        ),
        name="attend_fwd",
    )(length_arr, q, k, v, place, cb, pb, *shards)
    return attended, prob, [full.reshape(-1, shard[1]) for full in fulls]


def attend_bwd_kernel(q_ref, k_ref, v_ref, place_ref, cb_ref, pb_ref, prob_ref, g_ref, gq_ref, gk_ref, gv_ref, gp_ref, gb_ref, gk_s, gv_s, gp_s, *, scale):
    rows = q_ref.shape[0]
    length = k_ref.shape[0]
    span = rows + length
    step = pl.program_id(1)
    first = pl.multiple_of(length - rows - step * rows, rows)
    lanes = lax.broadcasted_iota(jnp.int32, (rows, PAIR), 1)
    flip = (lax.broadcasted_iota(jnp.int32, (rows, rows), 0) + lax.broadcasted_iota(jnp.int32, (rows, rows), 1) == rows - 1).astype(jnp.bfloat16)
    with_u = biased(q_ref, cb_ref, scale)
    with_v = mult_plain(flip, biased(q_ref, pb_ref, scale)).astype(jnp.bfloat16)
    grad = g_ref[...]
    window = place_ref[pl.ds(first, span), :]
    zero = jnp.zeros_like(with_u)

    @pl.when(step == 0)
    def _():
        gk_s[...] = jnp.zeros_like(gk_s)
        gv_s[...] = jnp.zeros_like(gv_s)
        gp_s[...] = jnp.zeros_like(gp_s)
        gb_ref[...] = jnp.zeros_like(gb_ref)

    grad_t, with_u_t, with_v_t = grad.T, with_u.T, with_v.T
    gu = []
    gw = []
    for head in range(2):
        mine = (lanes // HEAD_DIM) == head
        prob = prob_ref[head]
        grad_h = jnp.where(mine, grad, zero)
        grad_prob = mult_trans(grad_h, v_ref[...])
        weighted = prob.astype(jnp.float32) * grad_prob
        inner = jnp.sum(weighted, axis=1, keepdims=True)
        grad_score = (weighted - prob.astype(jnp.float32) * inner).astype(jnp.bfloat16)
        turned = mult_plain(flip, grad_score).astype(jnp.bfloat16)
        turned = jnp.concatenate([turned, jnp.zeros((rows, rows), jnp.bfloat16)], axis=1)
        turned = pltpu.roll(turned, 0, 1, stride=1, stride_axis=0)
        gu.append(mult_plain(grad_score, k_ref[...]))
        gw.append(mult_plain(turned, window))
        band = slice(head * HEAD_DIM, (head + 1) * HEAD_DIM)
        gv_s[band, :] += mult_plain(grad_t[band, :], prob)
        gk_s[band, :] += mult_plain(with_u_t[band, :], grad_score)
        gp_s[band, pl.ds(first, span)] += mult_plain(with_v_t[band, :], turned)
    grad_u = jnp.where(lanes < HEAD_DIM, gu[0], gu[1]) * scale
    grad_w = jnp.where(lanes < HEAD_DIM, gw[0], gw[1]) * scale
    gb_ref[0:1, :] += jnp.sum(grad_u, axis=0, keepdims=True)
    gb_ref[1:2, :] += jnp.sum(grad_w, axis=0, keepdims=True)
    high = grad_w.astype(jnp.bfloat16)
    rest = (grad_w - high.astype(jnp.float32)).astype(jnp.bfloat16)
    gq_ref[...] = (grad_u + mult_plain(flip, high) + mult_plain(flip, rest)).astype(jnp.bfloat16)

    @pl.when(step == pl.num_programs(1) - 1)
    def _():
        gk_ref[...] = gk_s[...].T.astype(jnp.bfloat16)
        gv_ref[...] = gv_s[...].T.astype(jnp.bfloat16)
        gp_ref[...] = gp_s[...].T.astype(jnp.bfloat16)


def attend_bwd_sum_kernel(layers, shared, count, blocks, *refs, scale):
    ins, parts = refs[:8], refs[8 : 8 + count]
    refs = refs[8 + count :]
    outs, sums, scratch, own = refs[:5], refs[5 : 5 + count], refs[5 + count : 8 + count], refs[8 + count :]
    at = pl.program_id(0) * pl.num_programs(1) + pl.program_id(1)
    plan = reduce_plan(layers, shared, parts, sums, None, own)
    body = partial(attend_bwd_kernel, *ins, *outs, *scratch, scale=scale)
    run_between(*plan, at, blocks, body)


def attend_bwd(q, k, v, place, cb, pb, prob, grad, rows, layers, shared, parts, collective_id):
    length, width = q.shape
    pairs = width // PAIR
    count = len(parts)
    inputs, shapes = reduce_shapes(layers, shared, parts)
    shard, channels = shapes[shared].shape[2:]
    still = lambda shape: pl.BlockSpec(shape, lambda p, i: (0,) * len(shape))
    full = pl.BlockSpec((length, PAIR), lambda p, i: (0, p))
    part = pl.BlockSpec((rows, PAIR), lambda p, i: (i, p))
    vec = pl.BlockSpec((1, PAIR), lambda p, i: (0, p))
    tall = pl.BlockSpec((2 * length, PAIR), lambda p, i: (0, p))
    return pl.pallas_call(
        partial(attend_bwd_sum_kernel, layers, shared, count, pairs * (length // rows), scale=1.0 / math.sqrt(HEAD_DIM)),
        grid=(pairs, length // rows),
        in_specs=[
            part,
            full,
            full,
            tall,
            vec,
            vec,
            pl.BlockSpec((2, rows, length), lambda p, i: (p, i, 0)),
            part,
        ]
        + [pl.BlockSpec(memory_space=pl.ANY)] * count,
        out_specs=[part, full, full, tall, pl.BlockSpec((8, PAIR), lambda p, i: (0, p))]
        + [still(shape.shape) for shape in shapes],
        out_shape=[
            jax.ShapeDtypeStruct((length, width), jnp.bfloat16),
            jax.ShapeDtypeStruct((length, width), jnp.bfloat16),
            jax.ShapeDtypeStruct((length, width), jnp.bfloat16),
            jax.ShapeDtypeStruct((2 * length, width), jnp.bfloat16),
            jax.ShapeDtypeStruct((8, width), jnp.float32),
        ]
        + shapes,
        scratch_shapes=[
            pltpu.VMEM((PAIR, length), jnp.float32),
            pltpu.VMEM((PAIR, length), jnp.float32),
            pltpu.VMEM((PAIR, 2 * length), jnp.float32),
        ]
        + reduce_scratch(count, layers, shard, channels),
        compiler_params=pltpu.CompilerParams(
            vmem_limit_bytes=VMEM, collective_id=collective_id, has_side_effects=True
        ),
        cost_estimate=pl.CostEstimate(
            flops=100 * 10**9, bytes_accessed=40 * 2**20, transcendentals=0
        ),
        name="attend_bwd",
    )(
        q,
        k,
        v,
        place,
        cb,
        pb,
        prob,
        grad,
        *inputs,
    )


MESH = pl.DeviceIdType.MESH


def chip_place(layers):
    z, c, y, x = (lax.axis_index(axis) for axis in ("z", "core", "y", "x"))

    def at(dz=0, dc=0, dy=0, dx=0):
        return (
            lax.rem(z + dz, layers),
            lax.rem(c + dc, 2),
            lax.rem(y + dy, 2),
            lax.rem(x + dx, 2),
        )

    def spot(dz=0, dc=0, dy=0, dx=0):
        return at(layers - dz, dc, dy, dx)

    return at, spot


def greet(at, layers):
    barrier = pltpu.get_barrier_semaphore()
    peers = [at(dz=k) for k in range(1, layers)] + [at(dc=1), at(dy=1), at(dx=1)]
    for peer in peers:
        pl.semaphore_signal(barrier, inc=1, device_id=peer, device_id_type=MESH)
    pl.semaphore_wait(barrier, len(peers))


def remote(source, target, sems, index, device):
    return pltpu.make_async_remote_copy(
        src_ref=source,
        dst_ref=target,
        send_sem=sems.at[(0, *index)],
        recv_sem=sems.at[(1, *index)],
        device_id=device,
        device_id_type=MESH,
    )


def far_first(layers):
    return sorted(range(1, layers), key=lambda k: -min(k, layers - k)) + [0]


def gather_plan(layers, shards, fulls, flat_only, z_sem, p_sem, d_sem, c_sem, own_sem):
    at, spot = chip_place(layers)
    arrays = range(len(shards))
    z, _, _, _ = spot()
    odd = lax.rem(z, 2)
    pair = at(dz=1 + odd * (layers - 2))
    items = [(0, a) for a in flat_only]
    items += [(dz, a) for dz in reversed(far_first(layers)) for a in arrays if a not in flat_only]
    own, along, flat, cross, last = {}, {}, {}, {}, {}
    for dz, a in items:
        full = fulls[a]
        flat_at = a in flat_only
        place = (lambda *_, **by: (odd, *spot(**by)[2:])) if flat_at else (lambda **by: spot(dz, **by))
        half = shards[a].shape[0] // 32 * 16
        source = full.at[place()] if dz else shards[a]
        if dz:
            along[dz, a] = remote(shards[a], full.at[spot()], z_sem, (a, dz), at(dz=dz))
        else:
            own[dz, a] = pltpu.make_async_copy(shards[a], full.at[place()], own_sem.at[a])
        flat[dz, a] = (
            remote(source, full.at[place()], p_sem, (a, dz, 0), at(dx=1)),
            remote(source, full.at[place()], p_sem, (a, dz, 1), at(dy=1)),
        )
        from_x = full.at[(*place(dx=1), pl.ds(half, shards[a].shape[0] - half))]
        from_y = full.at[(*place(dy=1), pl.ds(0, half))]
        cross[dz, a] = (
            remote(from_x, from_x, d_sem, (a, dz, 0), at(dy=1)),
            remote(from_y, from_y, d_sem, (a, dz, 1), at(dx=1)),
        )
        plane = full.at[place()[:-2]]
        last[dz, a] = remote(plane, plane, c_sem, (a, dz), pair if flat_at else at(dc=1))

    def enter():
        greet(at, layers)
        for item in items:
            if item[0]:
                along[item].start()
        for copy in own.values():
            copy.start()

    def spread(item):
        if item in along:
            along[item].wait_recv()
        for copy in flat[item]:
            copy.start()

    def turn(item):
        for got, out in zip(flat[item], cross[item]):
            got.wait_recv()
            out.start()

    def share(item):
        for got in cross[item]:
            got.wait_recv()
        if item in own:
            own[item].wait()
        last[item].start()

    def step(turn_at):
        for action, lag in ((spread, 0), (turn, 2), (share, 4)):
            if 0 <= turn_at - lag < len(items):
                action(items[turn_at - lag])

    def leave():
        for item in items:
            last[item].wait_recv()
        for item in items:
            if item in along:
                along[item].wait_send()
            for copy in (*flat[item], *cross[item], last[item]):
                copy.wait_send()

    return enter, step, len(items) + 4, leave


def gather_sems(count, layers):
    dma = pltpu.SemaphoreType.DMA
    return [
        dma((2, count, layers)),
        dma((2, count, layers, 2)),
        dma((2, count, layers, 2)),
        dma((2, count, layers)),
        dma((count,)),
    ]


def gather_kernel(layers, count, *refs):
    enter, step, turns, leave = gather_plan(
        layers, refs[:count], refs[count : 2 * count], (count - 1,), *refs[2 * count :]
    )
    enter()
    for turn_at in range(turns):
        step(turn_at)
    leave()


def gather_all(layers, shards, flat_shard, collective_id):
    ins = [*shards, flat_shard]
    count = len(ins)
    width = flat_shard.shape[1]
    shapes = [(layers, 2, 2, 2, *shard.shape) for shard in shards] + [(2, 2, 2, *flat_shard.shape)]
    *fulls, flat_full = pl.pallas_call(
        partial(gather_kernel, layers, count),
        in_specs=[pl.BlockSpec(memory_space=pl.ANY)] * count,
        out_specs=[pl.BlockSpec(memory_space=pl.ANY)] * count,
        out_shape=[jax.ShapeDtypeStruct(shape, jnp.bfloat16) for shape in shapes],
        scratch_shapes=gather_sems(count, layers),
        compiler_params=pltpu.CompilerParams(collective_id=collective_id, has_side_effects=True),
        cost_estimate=pl.CostEstimate(flops=0, bytes_accessed=300 * 2**20, transcendentals=0),
        name="gather_all",
    )(*ins)
    return [full.reshape(-1, width) for full in fulls], flat_full


def add_rows(target, one, two):
    target[...] = (one[...].astype(jnp.float32) + two[...].astype(jnp.float32)).astype(target.dtype)


def reduce_plan(layers, shared, parts, outs, small, scratch, made=None, summed=None):
    at, spot = chip_place(layers)
    sums, got_c, got_d, got_p, got_z, got_s, load_sem, c_sem, d_sem, p_sem, z_sem, s_sem, *tiny = scratch
    arrays = range(len(parts))
    rows = sums.shape[4]
    half = rows // 2
    order = far_first(layers)
    items = [(dz, shared) for dz in order if summed is None]
    items += [(dz, a) for dz in order for a in arrays if a != shared]
    first, second = pl.ds(0, half), pl.ds(half, half)
    here, by_y, by_x, far = (spot(0, 0, dy, dx)[2:] for dy, dx in ((0, 0), (1, 0), (0, 1), (1, 1)))
    made = made or {}
    whole = [a in made or len(parts[a].shape) == 6 for a in arrays]
    core_at = spot()[1]
    load, core, cross, flat, along = {}, {}, {}, {}, {}
    for dz, a in items:
        total = sums.at[a, dz]
        if a not in made:
            source = parts[a].at[spot(dz)[:2]] if whole[a] else parts[a].at[spot(dz)[0]]
            load[dz, a] = pltpu.make_async_copy(source, total, load_sem.at[a, dz])
        if whole[a]:
            slot = order.index(dz) % 2
            source = parts[a].at[slot] if a in made else parts[a].at[spot(dz, dc=1)[:2]]
            core[dz, a] = remote(source, got_c.at[a, dz], c_sem, (a, dz), at(dc=1))
        cross[dz, a] = (
            remote(total.at[(*far, first)], got_d.at[a, dz, 0], d_sem, (a, dz, 0), at(dx=1)),
            remote(total.at[(*far, second)], got_d.at[a, dz, 1], d_sem, (a, dz, 1), at(dy=1)),
        )
        flat[dz, a] = (
            remote(total.at[by_y], got_p.at[a, dz, 0], p_sem, (a, dz, 0), at(dy=1)),
            remote(total.at[by_x], got_p.at[a, dz, 1], p_sem, (a, dz, 1), at(dx=1)),
        )
        if dz:
            along[dz, a] = remote(
                total.at[here], got_z.at[a, dz], z_sem, (a, dz), at(dz=layers - dz)
            )
    own = got_s.at[(core_at, spot()[0])]
    handed = {k: remote(own, own, s_sem, (k,), at(dz=k)) for k in range(1, layers)}
    swapped = remote(got_s.at[core_at], got_s.at[core_at], s_sem, (0,), at(dc=1))
    sent = {}
    if summed:
        got_m, m_sem = tiny[3:]
        sent = {
            k: remote(summed[0].at[spot(k)[0]], got_m.at[k], m_sem, (k,), at(dz=layers - k))
            for k in range(1, layers)
        }
    hops = []
    if small:
        level, got_t, t_sem = tiny[:3]
        hops = [
            remote(level.at[i], got_t.at[i], t_sem, (i,), device)
            for i, device in enumerate((at(dc=1), at(dx=1), at(dy=1)))
        ]
        hops += [
            remote(level.at[3], got_t.at[2 + k], t_sem, (2 + k,), at(dz=k)) for k in range(1, layers)
        ]

    def enter():
        greet(at, layers)
        if small:
            level[0] = small[0][...]
            hops[0].start()
        for copy in sent.values():
            copy.start()
        for item in items:
            if item in load:
                load[item].start()
                if item in core:
                    core[item].start()

    def make(item):
        dz, a = item
        if a not in made:
            return
        left, right = made[a]
        size = 4 * rows
        turn_of = order.index(dz)
        if turn_of >= 2:
            core[order[turn_of - 2], a].wait_send()
        for dc, target in ((1, parts[a].at[turn_of % 2]), (0, sums.at[a, dz])):
            z_at, c_at = spot(dz, dc)[:2]
            columns = pl.ds(pl.multiple_of((2 * z_at + c_at) * size, size), size)
            block = mult_rows(left[:, columns], right[...]).astype(jnp.bfloat16)
            for at_y in range(2):
                for at_x in range(2):
                    row = (2 * at_y + at_x) * rows
                    target[at_y, at_x] = block[row : row + rows]
            if dc:
                core[item].start()

    def join_core(item):
        dz, a = item
        if item in load:
            load[item].wait()
        if whole[a]:
            core[item].wait_recv()
        for place in (far, by_y, by_x, here):
            target = sums.at[(a, dz, *place)]
            if whole[a]:
                add_rows(target, target, got_c.at[(a, dz, *place)])
            if place is far:
                for copy in cross[item]:
                    copy.start()

    def join_cross(item):
        dz, a = item
        one, two = sums.at[(a, dz, *by_y, first)], sums.at[(a, dz, *by_x, second)]
        cross[item][0].wait_recv()
        add_rows(one, one, got_d.at[a, dz, 0])
        flat[item][0].start()
        cross[item][1].wait_recv()
        add_rows(two, two, got_d.at[a, dz, 1])
        flat[item][1].start()

    def join_flat(item):
        dz, a = item
        target = sums.at[(a, dz, *here)]
        for copy in flat[item]:
            copy.wait_recv()
        target[...] = (
            target[...].astype(jnp.float32)
            + got_p[a, dz, 0].astype(jnp.float32)
            + got_p[a, dz, 1].astype(jnp.float32)
        ).astype(jnp.bfloat16)
        if dz:
            along[item].start()

    def total_of(a):
        total = sums[(a, 0, *here)].astype(jnp.float32)
        for dz in range(1, layers):
            along[dz, a].wait_recv()
            total = total + got_z[a, dz].astype(jnp.float32)
        return total

    def join_small(turn_at):
        if turn_at < 3:
            hops[turn_at].wait_recv()
            level[turn_at + 1] = level[turn_at] + got_t[turn_at]
            for hop in hops[turn_at + 1 : turn_at + 2] if turn_at < 2 else hops[3:]:
                hop.start()
        else:
            total = level[3]
            for k in range(1, layers):
                hops[2 + k].wait_recv()
                total = total + got_t[2 + k]
            small[1][...] = total

    def hand_on():
        if summed:
            total = summed[0][spot()[0]].astype(jnp.float32)
            for k, copy in sent.items():
                copy.wait_recv()
                total = total + got_m[k].astype(jnp.float32)
        else:
            total = total_of(shared)
        own[...] = total.astype(jnp.bfloat16)
        for copy in handed.values():
            copy.start()

    def swap():
        for copy in handed.values():
            copy.wait_recv()
        swapped.start()

    lead, near, wide = (1, 1, 2) if made else (0, 2, 4)
    handed_at = 5 if summed else layers - 1 + wide + 2 + lead
    turns = max(len(items) + wide + lead, handed_at + 4)

    def step(turn_at):
        actions = ((make, 0), (join_core, lead), (join_cross, lead + near), (join_flat, lead + wide))
        for action, lag in actions:
            if 0 <= turn_at - lag < len(items):
                action(items[turn_at - lag])
        if small and 1 <= turn_at <= 4:
            join_small(turn_at - 1)
        if turn_at == handed_at:
            hand_on()
        if turn_at == handed_at + 3:
            swap()

    def leave():
        for a in arrays:
            if a != shared:
                outs[a][...] = total_of(a)
        swapped.wait_recv()
        (summed[1] if summed else outs[shared])[...] = got_s[...]
        for item in items:
            if item[0]:
                along[item].wait_send()
            for copy in (*cross[item], *flat[item]):
                copy.wait_send()
            if item in core and not (item[1] in made and item[0] in order[:-2]):
                core[item].wait_send()
        for copy in (*handed.values(), *sent.values(), swapped, *hops):
            copy.wait_send()

    return enter, step, turns, leave


def reduce_scratch(count, layers, rows, width, small=None):
    dma = pltpu.SemaphoreType.DMA
    low = lambda *shape: pltpu.VMEM((count, layers, *shape, width), jnp.bfloat16)
    scratch = [
        low(2, 2, rows),
        low(2, 2, rows),
        low(2, rows // 2),
        low(2, rows),
        low(rows),
        pltpu.VMEM((2, layers, rows, width), jnp.bfloat16),
        dma((count, layers)),
        dma((2, count, layers)),
        dma((2, count, layers, 2)),
        dma((2, count, layers, 2)),
        dma((2, count, layers)),
        dma((2, layers)),
    ]
    if small is not None:
        scratch += [
            pltpu.VMEM((4, *small.shape), jnp.float32),
            pltpu.VMEM((2 + layers, *small.shape), jnp.float32),
            dma((2, 2 + layers)),
            pltpu.VMEM((layers, rows, width), jnp.bfloat16),
            dma((2, layers)),
        ]
    return scratch


def reduce_shapes(layers, shared, parts):
    blocks, shapes = [], []
    for a, (part, count) in enumerate(parts):
        width = part.shape[-1]
        rows = part.size // width // (4 * count * layers)
        blocks.append(part.reshape(layers, *((2,) if count == 2 else ()), 2, 2, rows, width))
        if a == shared:
            shapes.append(jax.ShapeDtypeStruct((2, layers, rows, width), jnp.bfloat16))
        else:
            shapes.append(jax.ShapeDtypeStruct((rows, width), jnp.float32))
    return blocks, shapes


def reduce_kernel(layers, part, left_a, right_a, left_b, right_b, small, sum_a, sum_b, handed, total, ring_a, ring_b, *scratch):
    enter, step, turns, leave = reduce_plan(
        layers,
        None,
        (ring_a, ring_b),
        (sum_a, sum_b),
        (small, total),
        scratch,
        {0: (left_a, right_a), 1: (left_b, right_b)},
        (part, handed),
    )
    enter()
    for turn_at in range(turns):
        step(turn_at)
    leave()


def reduce_all(layers, part, products, small, collective_id):
    rows, width = part.shape[1:]
    near = pl.BlockSpec(memory_space=pltpu.VMEM)
    ring = pltpu.VMEM((2, 2, 2, rows, width), jnp.bfloat16)
    return pl.pallas_call(
        partial(reduce_kernel, layers),
        in_specs=[near] * 6,
        out_specs=[near] * 4,
        out_shape=[
            jax.ShapeDtypeStruct((rows, width), jnp.float32),
            jax.ShapeDtypeStruct((rows, width), jnp.float32),
            jax.ShapeDtypeStruct((2, layers, rows, width), jnp.bfloat16),
            jax.ShapeDtypeStruct(small.shape, jnp.float32),
        ],
        scratch_shapes=[ring, ring] + reduce_scratch(2, layers, rows, width, small),
        compiler_params=pltpu.CompilerParams(
            collective_id=collective_id, has_side_effects=True, vmem_limit_bytes=VMEM
        ),
        cost_estimate=pl.CostEstimate(
            flops=8 * 10**9, bytes_accessed=300 * 2**20, transcendentals=0
        ),
        name="reduce_all",
    )(part, *(matrix for product in products for matrix in product), small)


def run_between(enter, step, turns, leave, at, blocks, body):
    pl.when(at == 0)(enter)
    for turn_at in range(min(turns, blocks)):
        pl.when(at == turn_at)(partial(step, turn_at))
    body()

    @pl.when(at == blocks - 1)
    def _():
        for turn_at in range(blocks, turns):
            step(turn_at)
        leave()


def norm_stats(values):
    centred = values - jnp.mean(values, axis=-1, keepdims=True)
    inverse = lax.rsqrt(jnp.mean(centred * centred, axis=-1, keepdims=True) + EPSILON)
    return centred * inverse, inverse


def norm_back(normal, inverse, gain_vec, upstream):
    grad = upstream * gain_vec
    grad_mean = jnp.mean(grad, axis=-1, keepdims=True)
    grad_along = jnp.mean(grad * normal, axis=-1, keepdims=True)
    return (
        (grad - grad_mean - normal * grad_along) * inverse,
        jnp.sum(upstream * normal, axis=0, keepdims=True),
    )


def ffn_fwd_kernel(x_ref, gain_ref, up_ref, down_ref, y_ref, h_ref, act_ref, slope_ref):
    @pl.when(pl.program_id(0) == 0)
    def _():
        values = x_ref[...].astype(jnp.float32)
        normal, _ = norm_stats(values)
        h_ref[...] = (normal * gain_ref[...].astype(jnp.float32)).astype(jnp.bfloat16)
        y_ref[...] = values

    before = mult_trans(h_ref[...], up_ref[...])
    squash = 0.5 + 0.5 * jnp.tanh(0.5 * before)
    active = before * squash
    slope_ref[...] = (squash + active * (1.0 - squash)).astype(jnp.bfloat16)
    active_low = active.astype(jnp.bfloat16)
    act_ref[...] = active_low
    y_ref[...] += 0.5 * mult_plain(active_low, down_ref[...])


def ffn_blocks(rows, width, block):
    still = pl.BlockSpec((rows, width), lambda j: (0, 0))
    vec = pl.BlockSpec((1, width), lambda j: (0, 0))
    weight = pl.BlockSpec((block, width), lambda j: (j, 0))
    hidden = pl.BlockSpec((rows, block), lambda j: (0, j))
    return still, vec, weight, hidden


def ffn_fwd(x, gain_vec, up, down):
    rows, width = x.shape
    total = up.shape[0]
    still, vec, weight, hidden = ffn_blocks(rows, width, FF_BLOCK)
    return pl.pallas_call(
        ffn_fwd_kernel,
        grid=(total // FF_BLOCK,),
        in_specs=[still, vec, weight, weight],
        out_specs=[still, still, hidden, hidden],
        out_shape=[
            jax.ShapeDtypeStruct((rows, width), jnp.float32),
            jax.ShapeDtypeStruct((rows, width), jnp.bfloat16),
            jax.ShapeDtypeStruct((rows, total), jnp.bfloat16),
            jax.ShapeDtypeStruct((rows, total), jnp.bfloat16),
        ],
        compiler_params=pltpu.CompilerParams(vmem_limit_bytes=VMEM),
        cost_estimate=pl.CostEstimate(
            flops=4 * rows * width * total,
            bytes_accessed=4 * width * total + 4 * rows * total,
            transcendentals=rows * total,
        ),
        name="ffn_fwd",
    )(x, gain_vec, up, down)


def ffn_bwd_kernel(x_ref, gain_ref, g_ref, slope_ref, up_ref, down_ref, gx_ref, gf_ref, gp_ref, gain_out, sum_s):
    step = pl.program_id(0)

    @pl.when(step == 0)
    def _():
        gf_ref[...] = (0.5 * g_ref[...]).astype(jnp.bfloat16)
        sum_s[...] = jnp.zeros_like(sum_s)

    grad_act = mult_trans(gf_ref[...], down_ref[...])
    grad_before = (grad_act * slope_ref[...].astype(jnp.float32)).astype(jnp.bfloat16)
    gp_ref[...] = grad_before
    sum_s[...] += mult_plain(grad_before, up_ref[...])

    @pl.when(step == pl.num_programs(0) - 1)
    def _():
        normal, inverse = norm_stats(x_ref[...].astype(jnp.float32))
        grad, gain_grad = norm_back(normal, inverse, gain_ref[...].astype(jnp.float32), sum_s[...])
        gx_ref[...] = (g_ref[...] + grad).astype(gx_ref.dtype)
        gain_out[...] = gain_grad


def ffn_bwd(x, gain_vec, grad, slope, up, down, out_type):
    rows, width = x.shape
    total = up.shape[0]
    still, vec, weight, hidden = ffn_blocks(rows, width, FF_BLOCK)
    return pl.pallas_call(
        ffn_bwd_kernel,
        grid=(total // FF_BLOCK,),
        in_specs=[still, vec, still, hidden, weight, weight],
        out_specs=[still, still, hidden, vec],
        out_shape=[
            jax.ShapeDtypeStruct((rows, width), out_type),
            jax.ShapeDtypeStruct((rows, width), jnp.bfloat16),
            jax.ShapeDtypeStruct((rows, total), jnp.bfloat16),
            jax.ShapeDtypeStruct((1, width), jnp.float32),
        ],
        scratch_shapes=[pltpu.VMEM((rows, width), jnp.float32)],
        compiler_params=pltpu.CompilerParams(vmem_limit_bytes=VMEM),
        cost_estimate=pl.CostEstimate(
            flops=4 * rows * width * total,
            bytes_accessed=4 * width * total + 4 * rows * total,
            transcendentals=0,
        ),
        name="ffn_bwd",
    )(x, gain_vec, grad, slope, up, down)


class Hops:
    def __init__(self, layers):
        self.layers = layers

    def send(self, block, dz=0, dc=0, dy=0, dx=0):
        pairs = []
        for z in range(self.layers):
            for c in range(2):
                for w in range(4):
                    to = ((z + dz) % self.layers * 2 + (c ^ dc)) * 4 + (w ^ (2 * dy + dx))
                    pairs.append(((z * 2 + c) * 4 + w, to))
        return lax.ppermute(block, ("z", "core", "y", "x"), pairs)

    def turn(self, block, step):
        pairs = []
        for z in range(self.layers):
            for c in range(2):
                for w in range(4):
                    to = (z * 2 + w // 2) * 4 + 2 * c + ((w % 2) ^ step)
                    pairs.append(((z * 2 + c) * 4 + w, to))
        got = lax.ppermute(block, ("z", "core", "y", "x"), [pair for pair in pairs if pair[0] != pair[1]])
        if step:
            return got
        return jnp.where(lax.axis_index("core") == lax.axis_index("y"), block, got)


def relative_waves(length, channels):
    step = 32
    rates = jnp.exp(
        jnp.arange(channels // 2).astype(jnp.float32) * (-2.0 * math.log(10000.0) / channels)
    )
    coarse = (length - 1 - step * jnp.arange(2 * length // step)).astype(jnp.float32)
    fine = jnp.arange(step).astype(jnp.float32)
    coarse, fine = coarse[:, None, None] * rates, fine[None, :, None] * rates
    sin_c, cos_c, sin_f, cos_f = jnp.sin(coarse), jnp.cos(coarse), jnp.sin(fine), jnp.cos(fine)
    return jnp.concatenate(
        [sin_c * cos_f - cos_c * sin_f, cos_c * cos_f + sin_c * sin_f], axis=2
    ).reshape(2 * length, channels)


def taps_forward(padded, kernel_f, count):
    total = jnp.zeros((count, padded.shape[1]), jnp.float32)
    for offset in range(KERNEL):
        total = total + padded[offset : offset + count] * kernel_f[offset]
    return total


def with_rim(hops, block, core):
    edge = jnp.where(core == 0, block[-16:], block[:16])
    got = hops.send(edge, dc=1)
    zero = jnp.zeros_like(got)
    low = jnp.where(core == 0, zero, got)[1:]
    high = jnp.where(core == 0, got, zero)[:RIM]
    return jnp.concatenate([low, block, high])


def per_chip(
    frames,
    lengths,
    masked,
    cotangent,
    first_gain,
    first_up,
    first_down,
    attn_gain,
    query_weight,
    key_weight,
    value_weight,
    out_weight,
    place_weight,
    content_bias,
    place_bias,
    conv_gain,
    glu_weight,
    depth_kernel,
    middle_gain,
    point_weight,
    second_gain,
    second_up,
    second_down,
    final_gain,
):
    core, y, x = lax.axis_index("core"), lax.axis_index("y"), lax.axis_index("x")
    wide_at = 2 * y + x
    layers = lax.axis_size("z")
    hops = Hops(layers)
    groups, quarter, channels = frames.shape
    rows = groups * quarter
    length = 2 * rows
    f32 = lambda v: v.astype(jnp.float32)
    low = lambda v: v.astype(jnp.bfloat16)

    def pick(flag, one, two):
        return jnp.where(flag, one, two), jnp.where(flag, two, one)

    def turn_in(block):
        swap = [lax.dynamic_index_in_dim(block, x ^ step, 0, keepdims=False) for step in range(2)]
        got = [hops.turn(swap[step], step) for step in range(2)]
        return jnp.concatenate(pick(x == 0, *got))

    def turn_out(block):
        parts = pick(x == 0, block[:quarter], block[quarter:])
        got = [hops.turn(parts[step], step) for step in range(2)]
        return jnp.stack(pick(x == 0, *got))

    frames_own = turn_in(frames)
    positions = wide_at * quarter + jnp.arange(quarter, dtype=jnp.int32)
    seed_weight = f32(masked) * f32(positions[None, :] < lengths[:, None])
    seed_own_low = low(f32(cotangent) * seed_weight[:, :, None])
    near_lengths = jnp.where(core == y, lengths, hops.send(lengths, dc=1))
    own_length = lax.dynamic_slice_in_dim(near_lengths, x, 1)
    own_rows = core * rows + jnp.arange(rows, dtype=jnp.int32)
    frame_ok = f32(own_rows < own_length[0])[:, None]

    def own_half(weight):
        count = weight.shape[0] // 2
        return lax.dynamic_slice_in_dim(weight, core * count, count)

    band = query_weight.shape[0] // 2
    odd = lax.rem(lax.axis_index("z"), 2)
    piece = band // 2

    def own_quarter(weight):
        return lax.dynamic_slice_in_dim(weight, core * band + odd * piece, piece)

    own_bias = own_half(jnp.stack([content_bias, place_bias], axis=1)).T
    attn_chunk = jnp.concatenate(
        [own_quarter(weight) for weight in (query_weight, key_weight, value_weight, place_weight)]
        + [jnp.pad(own_bias, ((0, 14), (0, channels - band)))]
    )
    (up_first, down_first), attn_all = gather_all(layers, [first_up, first_down], attn_chunk, 1)
    conv_chunk = jnp.concatenate([own_half(out_weight), own_half(point_weight), own_half(glu_weight)])
    conv_chunk, attn_all = lax.optimization_barrier((conv_chunk, attn_all))
    conv_all = lax.all_gather(conv_chunk, ("y", "x"), axis=0)
    attn_all = attn_all.reshape(2, 4, -1, channels)

    def heads_of(at):
        rows_of = attn_all[:, :, at * piece : (at + 1) * piece]
        return rows_of.transpose(1, 0, 2, 3).reshape(4 * band, channels)

    query_own, key_own, value_own, place_own = (heads_of(at) for at in range(4))
    own_biases = attn_all[0, :, 4 * piece : 4 * piece + 2, :band].transpose(1, 0, 2).reshape(2, 4 * band)
    conv_other = hops.send(conv_all, dc=1)
    conv_both = jnp.stack(pick(core == 0, conv_all, conv_other), axis=1)
    full_out = conv_both[:, :, :band].reshape(8 * band, channels)
    full_point = conv_both[:, :, band : 2 * band].reshape(8 * band, channels)
    full_glu = conv_both[:, :, 2 * band :].reshape(16 * band, channels)

    stream1, first_low, first_act, first_slope = ffn_fwd(
        frames_own, first_gain[None], up_first, down_first
    )
    stream1, seed_own_low = lax.optimization_barrier((stream1, seed_own_low))
    normed_attn, attn_pull = jax.vjp(norm_rows, stream1, f32(attn_gain))
    attn_half = low(normed_attn)
    attn_other = hops.send(attn_half, dc=1)
    attn_low = jnp.concatenate(pick(core == 0, attn_half, attn_other))
    rel_table = low(relative_waves(length, channels))
    query = low(mult_trans(attn_low, query_own))
    key = low(mult_trans(attn_low, key_own))
    value = low(mult_trans(attn_low, value_own))
    place = low(mult_trans(rel_table, place_own))
    attended, prob, (up_second, down_second) = attend_fwd(
        own_length,
        query,
        key,
        value,
        place,
        own_biases[:1],
        own_biases[1:],
        ROWS_FWD,
        layers,
        [second_up, second_down],
        4,
    )

    def halves(matrix):
        own = lax.dynamic_slice_in_dim(matrix, core * rows, rows)
        other = lax.dynamic_slice_in_dim(matrix, (1 - core) * rows, rows)
        return own, other

    att_own, att_other = halves(attended)
    att_parts = pick(core == 0, att_own, hops.send(att_other, dc=1))
    framed = jnp.stack([part.reshape(rows, 4, band) for part in att_parts], axis=2)
    framed = framed.reshape(rows, 8 * band)
    stream2 = stream1 + mult_plain(framed, full_out)
    normed_conv, conv_pull = jax.vjp(norm_rows, stream2, f32(conv_gain))
    conv_low = low(normed_conv)
    glu_in = mult_trans(conv_low, full_glu)
    linear = glu_in[:, :channels]
    gating = jax.nn.sigmoid(glu_in[:, channels:])
    gated = low(linear * gating * frame_ok)
    padded = with_rim(hops, gated, core)
    kernel_f = f32(depth_kernel)
    conv_out = taps_forward(padded, kernel_f, rows)
    middle, middle_pull = jax.vjp(norm_rows, conv_out, f32(middle_gain))
    swished = low(jax.nn.silu(middle))
    stream3 = stream2 + mult_trans(swished, full_point)
    stream4, second_low, second_act, second_slope = ffn_fwd(
        stream3, second_gain[None], up_second, down_second
    )
    final_rows, final_pull = jax.vjp(norm_rows, stream4, f32(final_gain))
    output = turn_out(low(final_rows))

    seed_own = turn_in(seed_own_low)
    grad4, grad_final_gain = final_pull(f32(seed_own))

    grad3, grad_out2, grad_before2, grad_second_gain = ffn_bwd(
        stream3, second_gain[None], grad4, second_slope, up_second, down_second, jnp.float32
    )
    grad_down_second = low(mult_rows(second_act, grad_out2))
    grad_up_second = low(mult_rows(grad_before2, second_low))
    grad3, output = lax.optimization_barrier((grad3, output))
    grad_branch = low(grad3)
    grad_point = mult_rows(grad_branch, swished)
    grad_middle = mult_plain(grad_branch, full_point) * silu_slope(middle)
    grad_conv, grad_middle_gain = middle_pull(grad_middle)
    conv_grad_low = low(grad_conv)
    grad_padded = with_rim(hops, conv_grad_low, core)
    grad_gated = taps_forward(grad_padded, kernel_f[::-1], rows)
    grad_kernel = jnp.stack(
        [
            jnp.sum(f32(padded[offset : offset + rows]) * f32(conv_grad_low), axis=0)
            for offset in range(KERNEL)
        ]
    )
    grad_gated = grad_gated * frame_ok
    grad_glu_in = low(
        jnp.concatenate(
            [grad_gated * gating, grad_gated * linear * gating * (1.0 - gating)], axis=1
        )
    )
    grad_glu = mult_rows(grad_glu_in, conv_low)
    grad_conv_in, grad_conv_gain = conv_pull(mult_plain(grad_glu_in, full_glu))
    grad2 = grad3 + grad_conv_in
    grad_attn = low(grad2)
    grad_out = mult_rows(framed, grad_attn)
    grad_framed = low(mult_trans(grad_attn, full_out))
    grad_parts = grad_framed.reshape(rows, 4, 2, band)
    grad_parts = [grad_parts[:, :, at].reshape(rows, 4 * band) for at in range(2)]
    grad_kept, grad_sent = pick(core == 0, *grad_parts)
    grad_heads = jnp.concatenate(pick(core == 0, grad_kept, hops.send(grad_sent, dc=1)))

    def by_place(matrix, cores):
        blocks = low(matrix).reshape(4, cores, layers, -1, channels)
        return blocks.transpose(2, 1, 0, 3, 4)

    conv_part = jnp.concatenate(
        [by_place(part, 2) for part in (grad_out, grad_point, grad_glu)], axis=3
    )
    *attn_grads, sum_up_second, sum_down_second, conv_sums = attend_bwd(
        query,
        key,
        value,
        place,
        own_biases[:1],
        own_biases[1:],
        prob,
        grad_heads,
        ROWS_BWD,
        layers,
        2,
        [(grad_up_second, 2), (grad_down_second, 2), (conv_part, 2)],
        3,
    )
    grad_query, grad_key, grad_value, grad_place, grad_biases = attn_grads
    grad_query_w = mult_rows(grad_query, attn_low)
    grad_key_w = mult_rows(grad_key, attn_low)
    grad_value_w = mult_rows(grad_value, attn_low)
    grad_place_w = mult_rows(grad_place, rel_table)
    attn_part = jnp.concatenate(
        [
            low(part).reshape(4, layers, -1, channels)
            for part in (grad_query_w, grad_key_w, grad_value_w, grad_place_w)
        ],
        axis=2,
    )
    attn_part, grad_query = lax.optimization_barrier((attn_part, grad_query))
    attn_part = lax.psum_scatter(attn_part, ("y", "x"), scatter_dimension=0, tiled=False)
    grad_normed = (
        mult_plain(grad_query, query_own)
        + mult_plain(grad_key, key_own)
        + mult_plain(grad_value, value_own)
    )
    normed_own, normed_other = halves(grad_normed)
    grad_attn_in, grad_attn_gain = attn_pull(normed_own + f32(hops.send(low(normed_other), dc=1)))
    grad1 = grad2 + grad_attn_in
    grad0, grad_out1, grad_before1, grad_first_gain = ffn_bwd(
        frames_own, first_gain[None], grad1, first_slope, up_first, down_first, jnp.bfloat16
    )
    grad_input = turn_out(grad0)

    spread = jnp.zeros((2, 4, 2, band), jnp.float32)
    spread = lax.dynamic_update_slice(
        spread, grad_biases[:2].reshape(2, 4, 1, band), (0, 0, core, 0)
    ).reshape(2, channels)
    gains = (
        grad_conv_gain,
        grad_middle_gain,
        grad_second_gain[0],
        grad_final_gain,
        grad_first_gain[0],
        grad_attn_gain,
    )
    small = jnp.concatenate([jnp.stack(gains), spread, grad_kernel])
    small = jnp.pad(small, ((0, -small.shape[0] % 8), (0, 0)))
    sum_up_first, sum_down_first, attn_sums, small = reduce_all(
        layers,
        attn_part,
        [(grad_before1, first_low), (first_act, grad_out1)],
        small,
        2,
    )

    def owned(sums, start, count):
        return f32(sums[:, :, start : start + count]).reshape(-1, channels)

    step = band // layers
    total_out, total_point = owned(conv_sums, 0, step), owned(conv_sums, step, step)
    total_glu = owned(conv_sums, 2 * step, 2 * step)
    total_query, total_key, total_value, total_place = (
        owned(attn_sums, at * step, step) for at in range(4)
    )
    own_bias_grad = lax.dynamic_slice_in_dim(small[6:8], wide_at * 2 * band, 2 * band, 1)
    return (
        output,
        grad_input,
        small[4],
        sum_up_first,
        sum_down_first,
        small[5],
        total_query,
        total_key,
        total_value,
        total_out,
        total_place,
        own_bias_grad[0],
        own_bias_grad[1],
        small[0],
        total_glu,
        small[8 : 8 + KERNEL],
        small[1],
        total_point,
        small[2],
        sum_up_second,
        sum_down_second,
        small[3],
    )


def per_device(
    frames,
    lengths,
    masked,
    cotangent,
    first_gain,
    first_up,
    first_down,
    attn_gain,
    query_weight,
    key_weight,
    value_weight,
    out_weight,
    place_weight,
    content_bias,
    place_bias,
    conv_gain,
    glu_weight,
    depth_kernel,
    middle_gain,
    point_weight,
    second_gain,
    second_up,
    second_down,
    final_gain,
):
    groups, frames_dev, channels = frames.shape
    row_count = groups * frames_dev
    length = frames_dev * lax.axis_size("wide")
    score_scale = 1.0 / math.sqrt(HEAD_DIM)
    positions = lax.axis_index("wide") * frames_dev + jnp.arange(frames_dev, dtype=jnp.int32)
    frame_grid = (positions[None, :] < lengths[:, None]).astype(jnp.float32)
    frame_ok = frame_grid.reshape(row_count, 1)
    key_ok = jnp.arange(length, dtype=jnp.int32)[None, :] < lengths[:, None]
    stream0 = frames.reshape(row_count, channels).astype(jnp.float32)
    up_first, down_first = gather_ffn(first_up, first_down)
    stream1, saved_first = ffn_forward(
        stream0, first_gain.astype(jnp.float32), up_first, down_first
    )
    full_query, full_key, full_value, full_out, full_glu, full_point = (
        lax.all_gather(query_weight, "wide", axis=0, tiled=True),
        lax.all_gather(key_weight, "wide", axis=0, tiled=True),
        lax.all_gather(value_weight, "wide", axis=0, tiled=True),
        lax.all_gather(out_weight, "wide", axis=0, tiled=True),
        lax.all_gather(glu_weight, "wide", axis=0, tiled=True),
        lax.all_gather(point_weight, "wide", axis=0, tiled=True),
    )
    normed_attn, attn_pull = jax.vjp(norm_rows, stream1, attn_gain.astype(jnp.float32))
    attn_low = normed_attn.astype(jnp.bfloat16)
    query_frames = (
        mult_trans(attn_low, full_query).astype(jnp.bfloat16).reshape(groups, frames_dev, -1)
    )
    key_frames = mult_trans(attn_low, full_key).astype(jnp.bfloat16).reshape(groups, frames_dev, -1)
    value_frames = (
        mult_trans(attn_low, full_value).astype(jnp.bfloat16).reshape(groups, frames_dev, -1)
    )
    heads_query, heads_key, heads_value = (
        lax.all_to_all(query_frames, "wide", split_axis=2, concat_axis=1, tiled=True),
        lax.all_to_all(key_frames, "wide", split_axis=2, concat_axis=1, tiled=True),
        lax.all_to_all(value_frames, "wide", split_axis=2, concat_axis=1, tiled=True),
    )
    local_width = heads_query.shape[2]
    head_count = local_width // HEAD_DIM
    rel_table = relative_table(length, channels).astype(jnp.bfloat16)
    place_rows = (
        mult_trans(rel_table, place_weight)
        .astype(jnp.bfloat16)
        .reshape(2 * length - 1, head_count, HEAD_DIM)
    )
    bias_first = content_bias.astype(jnp.float32).reshape(head_count, HEAD_DIM)
    bias_second = place_bias.astype(jnp.float32).reshape(head_count, HEAD_DIM)
    split_query = heads_query.reshape(groups, length, head_count, HEAD_DIM)
    split_key = heads_key.reshape(groups, length, head_count, HEAD_DIM)
    split_value = heads_value.reshape(groups, length, head_count, HEAD_DIM)
    forward_heads = jax.vmap(
        partial(head_forward, block_rows=QBLK, score_scale=score_scale),
        in_axes=(1, 1, 1, 1, 0, 0, None),
        out_axes=(1, 0),
    )

    def attend_utt(unit_items):
        return forward_heads(
            unit_items[0],
            unit_items[1],
            unit_items[2],
            place_rows,
            bias_first,
            bias_second,
            unit_items[3],
        )

    attended, log_total = lax.map(attend_utt, (split_query, split_key, split_value, key_ok))
    framed = lax.all_to_all(
        attended.reshape(groups, length, local_width),
        "wide",
        split_axis=1,
        concat_axis=2,
        tiled=True,
    ).reshape(row_count, -1)
    stream2 = stream1 + mult_plain(framed, full_out)
    normed_conv, conv_pull = jax.vjp(norm_rows, stream2, conv_gain.astype(jnp.float32))
    conv_low = normed_conv.astype(jnp.bfloat16)
    glu_in = mult_trans(conv_low, full_glu)
    linear = glu_in[:, :channels]
    gating = jax.nn.sigmoid(glu_in[:, channels:])
    gated = (linear * gating * frame_ok).astype(jnp.bfloat16).reshape(groups, frames_dev, channels)
    padded = with_halo(gated, (("wide", 1),), RIM)
    kernel_f = depth_kernel.astype(jnp.float32)
    conv_out = jnp.zeros((groups, frames_dev, channels), jnp.float32)
    for offset in range(KERNEL):
        conv_out = conv_out + padded[:, offset : offset + frames_dev, :] * kernel_f[offset]
    conv_out = conv_out.reshape(row_count, channels)
    middle, middle_pull = jax.vjp(norm_rows, conv_out, middle_gain.astype(jnp.float32))
    swished = jax.nn.silu(middle).astype(jnp.bfloat16)
    stream3 = stream2 + mult_trans(swished, full_point)
    up_second, down_second = gather_ffn(second_up, second_down)
    stream4, saved_second = ffn_forward(
        stream3, second_gain.astype(jnp.float32), up_second, down_second
    )
    final_rows, final_pull = jax.vjp(norm_rows, stream4, final_gain.astype(jnp.float32))
    output = final_rows.astype(jnp.bfloat16).reshape(groups, frames_dev, channels)
    seed_weight = (masked.astype(jnp.float32) * frame_grid).reshape(row_count, 1)
    seed_grad = cotangent.reshape(row_count, channels).astype(jnp.float32) * seed_weight
    grad4, grad_final_gain = final_pull(seed_grad)
    back_up_second, back_down_second = gather_ffn(second_up, second_down)
    grad3, grad_second_gain, grad_up_second, grad_down_second = ffn_backward(
        grad4, saved_second, back_up_second, back_down_second
    )
    summed_second = sum_ffn(grad_up_second, grad_down_second)
    grad_branch = grad3.astype(jnp.bfloat16)
    grad_point = mult_rows(grad_branch, swished)
    grad_middle = mult_plain(grad_branch, full_point) * silu_slope(middle)
    grad_conv, grad_middle_gain = middle_pull(grad_middle)
    conv_grad_low = grad_conv.astype(jnp.bfloat16).reshape(groups, frames_dev, channels)
    grad_padded = with_halo(conv_grad_low, (("wide", 1),), RIM)
    grad_gated = jnp.zeros((groups, frames_dev, channels), jnp.float32)
    kernel_rows = []
    for offset in range(KERNEL):
        grad_gated = (
            grad_gated
            + grad_padded[:, 2 * RIM - offset : 2 * RIM - offset + frames_dev, :] * kernel_f[offset]
        )
        kernel_rows.append(
            jnp.einsum(
                "rzn,rzn->n",
                padded[:, offset : offset + frames_dev, :],
                conv_grad_low,
                preferred_element_type=jnp.float32,
            )
        )
    grad_kernel = jnp.stack(kernel_rows)
    grad_gated = grad_gated.reshape(row_count, channels) * frame_ok
    grad_glu_in = jnp.concatenate(
        [grad_gated * gating, grad_gated * linear * gating * (1.0 - gating)], axis=1
    ).astype(jnp.bfloat16)
    grad_glu = mult_rows(grad_glu_in, conv_low)
    grad_conv_in, grad_conv_gain = conv_pull(mult_plain(grad_glu_in, full_glu))
    grad2 = grad3 + grad_conv_in
    grad_attn = grad2.astype(jnp.bfloat16)
    grad_out = mult_rows(framed, grad_attn)
    grad_framed = (
        mult_trans(grad_attn, full_out).astype(jnp.bfloat16).reshape(groups, frames_dev, -1)
    )
    grad_heads = lax.all_to_all(grad_framed, "wide", split_axis=2, concat_axis=1, tiled=True)
    backward_heads = jax.vmap(
        partial(head_backward, block_rows=QBLK, score_scale=score_scale),
        in_axes=(1, 1, 1, 1, 0, 0, None, 0, 1),
        out_axes=(1, 1, 1, 1, 0, 0),
    )

    def attend_back(unit_items):
        return backward_heads(
            unit_items[0],
            unit_items[1],
            unit_items[2],
            place_rows,
            bias_first,
            bias_second,
            unit_items[3],
            unit_items[4],
            unit_items[5],
        )

    grad_query_h, grad_key_h, grad_value_h, grad_place_h, grad_bias_first, grad_bias_second = (
        lax.map(
            attend_back,
            (
                split_query,
                split_key,
                split_value,
                key_ok,
                log_total,
                grad_heads.reshape(groups, length, head_count, HEAD_DIM),
            ),
        )
    )
    back_query, back_key, back_value = (
        lax.all_to_all(
            grad_query_h.reshape(groups, length, local_width),
            "wide",
            split_axis=1,
            concat_axis=2,
            tiled=True,
        ),
        lax.all_to_all(
            grad_key_h.reshape(groups, length, local_width),
            "wide",
            split_axis=1,
            concat_axis=2,
            tiled=True,
        ),
        lax.all_to_all(
            grad_value_h.reshape(groups, length, local_width),
            "wide",
            split_axis=1,
            concat_axis=2,
            tiled=True,
        ),
    )
    back_query = back_query.reshape(row_count, -1)
    back_key = back_key.reshape(row_count, -1)
    back_value = back_value.reshape(row_count, -1)
    grad_query_w = mult_rows(back_query, attn_low)
    grad_key_w = mult_rows(back_key, attn_low)
    grad_value_w = mult_rows(back_value, attn_low)
    grad_normed = (
        mult_plain(back_query, full_query)
        + mult_plain(back_key, full_key)
        + mult_plain(back_value, full_value)
    )
    grad_attn_in, grad_attn_gain = attn_pull(grad_normed)
    grad1 = grad2 + grad_attn_in
    grad_place_w = jnp.einsum(
        "urc,rd->cd",
        grad_place_h.reshape(groups, 2 * length - 1, local_width),
        rel_table,
        preferred_element_type=jnp.float32,
    )
    grad_content = jnp.sum(grad_bias_first, axis=0).reshape(local_width)
    grad_place_b = jnp.sum(grad_bias_second, axis=0).reshape(local_width)
    back_up_first, back_down_first = gather_ffn(first_up, first_down)
    grad0, grad_first_gain, grad_up_first, grad_down_first = ffn_backward(
        grad1, saved_first, back_up_first, back_down_first
    )
    summed_first = sum_ffn(grad_up_first, grad_down_first)
    mixer_grads = (
        lax.psum_scatter(
            grad_query_w.astype(jnp.bfloat16), "wide", scatter_dimension=0, tiled=True
        ).astype(jnp.float32),
        lax.psum_scatter(
            grad_key_w.astype(jnp.bfloat16), "wide", scatter_dimension=0, tiled=True
        ).astype(jnp.float32),
        lax.psum_scatter(
            grad_value_w.astype(jnp.bfloat16), "wide", scatter_dimension=0, tiled=True
        ).astype(jnp.float32),
        lax.psum_scatter(
            grad_out.astype(jnp.bfloat16), "wide", scatter_dimension=0, tiled=True
        ).astype(jnp.float32),
        lax.psum_scatter(
            grad_glu.astype(jnp.bfloat16), "wide", scatter_dimension=0, tiled=True
        ).astype(jnp.float32),
        lax.psum_scatter(
            grad_point.astype(jnp.bfloat16), "wide", scatter_dimension=0, tiled=True
        ).astype(jnp.float32),
    )
    totals = (
        lax.psum(mixer_grads[0].astype(jnp.bfloat16), "utt").astype(jnp.float32),
        lax.psum(mixer_grads[1].astype(jnp.bfloat16), "utt").astype(jnp.float32),
        lax.psum(mixer_grads[2].astype(jnp.bfloat16), "utt").astype(jnp.float32),
        lax.psum(mixer_grads[3].astype(jnp.bfloat16), "utt").astype(jnp.float32),
        lax.psum(mixer_grads[4].astype(jnp.bfloat16), "utt").astype(jnp.float32),
        lax.psum(mixer_grads[5].astype(jnp.bfloat16), "utt").astype(jnp.float32),
        lax.psum(grad_place_w.astype(jnp.bfloat16), "utt").astype(jnp.float32),
        lax.psum(grad_content.astype(jnp.bfloat16), "utt").astype(jnp.float32),
        lax.psum(grad_place_b.astype(jnp.bfloat16), "utt").astype(jnp.float32),
    )
    small_grads = lax.psum(
        (
            grad_first_gain,
            grad_attn_gain,
            grad_conv_gain,
            grad_middle_gain,
            grad_second_gain,
            grad_final_gain,
            grad_kernel,
        ),
        ("utt", "wide"),
    )
    grad_input = grad0.astype(jnp.bfloat16).reshape(groups, frames_dev, channels)
    return (
        output,
        grad_input,
        small_grads[0],
        summed_first[0],
        summed_first[1],
        small_grads[1],
        totals[0],
        totals[1],
        totals[2],
        totals[3],
        totals[6],
        totals[7],
        totals[8],
        small_grads[2],
        totals[4],
        small_grads[6],
        small_grads[3],
        totals[5],
        small_grads[4],
        summed_second[0],
        summed_second[1],
        small_grads[5],
    )


def solution(mesh):
    shape = dict(mesh.shape)
    if shape["wide"] == 4 and shape["utt"] % 4 == 0:
        mesh = jax.sharding.Mesh(
            mesh.devices.reshape(shape["utt"] // 2, 2, 2, 2), ("z", "core", "y", "x")
        )
        utt, wide, body = ("z", "core"), ("y", "x"), per_chip
    else:
        utt, wide, body = "utt", "wide", per_device
    every = (utt, wide) if utt == "utt" else (*utt, *wide)
    in_specs = (
        P(utt, wide, None),
        P(utt),
        P(utt, wide),
        P(utt, wide, None),
        P(),
        P(every, None),
        P(every, None),
        P(),
        P(wide, None),
        P(wide, None),
        P(wide, None),
        P(wide, None),
        P(wide, None),
        P(wide),
        P(wide),
        P(),
        P(wide, None),
        P(),
        P(),
        P(wide, None),
        P(),
        P(every, None),
        P(every, None),
        P(),
    )
    out_specs = (
        P(utt, wide, None),
        P(utt, wide, None),
        P(),
        P(every, None),
        P(every, None),
        P(),
        P(wide, None),
        P(wide, None),
        P(wide, None),
        P(wide, None),
        P(wide, None),
        P(wide),
        P(wide),
        P(),
        P(wide, None),
        P(),
        P(),
        P(wide, None),
        P(),
        P(every, None),
        P(every, None),
        P(),
    )
    return jax.shard_map(
        body, mesh=mesh, in_specs=in_specs, out_specs=out_specs, check_vma=False
    )
```

```python
from functools import partial
import math

import jax
import jax.numpy as jnp
from jax import lax
from jax.experimental import pallas as pl
from jax.experimental.pallas import tpu as pltpu
from jax.sharding import PartitionSpec as P

HEAD_DIM = 64
KERNEL = 31
QBLK = 512
RIM = 15
PAIR = 128
ROWS_FWD = 256
ROWS_BWD = 256
FF_BLOCK = 1024
VMEM = 58 * 2**20


EPSILON = 1e-05
MASKED_SCORE = -1e30


def with_halo(block, sides, width):
    for axis, dim in sides:
        count = lax.axis_size(axis)
        forward = [(i, i + 1) for i in range(count - 1)]
        backward = [(target, source) for source, target in forward]
        low = lax.ppermute(
            lax.slice_in_dim(block, block.shape[dim] - width, None, axis=dim), axis, forward
        )
        high = lax.ppermute(lax.slice_in_dim(block, 0, width, axis=dim), axis, backward)
        block = jnp.concatenate([low, block, high], axis=dim)
    return block


def norm_rows(values, gain_vec):
    average = jnp.mean(values, axis=-1, keepdims=True)
    centred = values - average
    spread = jnp.mean(centred * centred, axis=-1, keepdims=True)
    return centred * lax.rsqrt(spread + EPSILON) * gain_vec


def silu_slope(before):
    squash = jax.nn.sigmoid(before)
    return squash * (1.0 + before * (1.0 - squash))


def mult_trans(first_mat, second_mat):
    return lax.dot_general(
        first_mat, second_mat, (((1,), (1,)), ((), ())), preferred_element_type=jnp.float32
    )


def mult_plain(first_mat, second_mat):
    return jnp.dot(first_mat, second_mat, preferred_element_type=jnp.float32)


def mult_rows(first_mat, second_mat):
    return lax.dot_general(
        first_mat, second_mat, (((0,), (0,)), ((), ())), preferred_element_type=jnp.float32
    )


def relative_table(length, channels):
    offsets = length - 1 - jnp.arange(2 * length - 1).astype(jnp.float32)
    rates = jnp.exp(
        jnp.arange(channels // 2).astype(jnp.float32) * (-2.0 * math.log(10000.0) / channels)
    )
    angles = offsets[:, None] * rates[None, :]
    return jnp.concatenate([jnp.sin(angles), jnp.cos(angles)], axis=1)


def skew_rows(reversed_scores):
    block_rows, span = reversed_scores.shape
    flat = reversed_scores.reshape(-1)[block_rows - 1 : block_rows - 1 + block_rows * (span - 1)]
    return flat.reshape(block_rows, span - 1)[:, : span - block_rows + 1]


def unskew_rows(grad_scores, span):
    block_rows, length = grad_scores.shape
    padded = jnp.pad(grad_scores, ((0, 0), (0, span - 1 - length)))
    flat = jnp.pad(padded.reshape(-1), (block_rows - 1, 1))
    return flat.reshape(block_rows, span)


def gather_ffn(up_rows, down_rows):
    return (
        lax.all_gather(up_rows, ("utt", "wide"), axis=0, tiled=True),
        lax.all_gather(down_rows, ("utt", "wide"), axis=0, tiled=True),
    )


def sum_ffn(grad_up, grad_down):
    return (
        lax.psum_scatter(grad_up, ("utt", "wide"), scatter_dimension=0, tiled=True),
        lax.psum_scatter(grad_down, ("utt", "wide"), scatter_dimension=0, tiled=True),
    )


def ffn_forward(stream, gain_vec, up_full, down_full):
    normed, norm_pull = jax.vjp(norm_rows, stream, gain_vec)
    normed_low = normed.astype(jnp.bfloat16)
    before = mult_trans(normed_low, up_full)
    active_low = jax.nn.silu(before).astype(jnp.bfloat16)
    return (
        stream + 0.5 * mult_plain(active_low, down_full),
        (norm_pull, normed_low, before, active_low),
    )


def ffn_backward(grad_stream, saved_ffn, up_full, down_full):
    norm_pull, normed_low, before, active_low = saved_ffn
    grad_out = (0.5 * grad_stream).astype(jnp.bfloat16)
    grad_down = mult_rows(active_low, grad_out)
    grad_before = (mult_trans(grad_out, down_full) * silu_slope(before)).astype(jnp.bfloat16)
    grad_up = mult_rows(grad_before, normed_low)
    grad_input, grad_gain = norm_pull(mult_plain(grad_before, up_full))
    return (grad_stream + grad_input, grad_gain, grad_up, grad_down)


def head_forward(
    query_rows,
    key_rows,
    value_rows,
    place_rows,
    bias_first,
    bias_second,
    key_ok,
    block_rows,
    score_scale,
):
    length, head_width = query_rows.shape
    with_u = (query_rows.astype(jnp.float32) + bias_first).astype(jnp.bfloat16)
    with_v = (query_rows.astype(jnp.float32) + bias_second).astype(jnp.bfloat16)

    def one_block(block_index):
        first_row = block_index * block_rows
        block_u = lax.dynamic_slice_in_dim(with_u, first_row, block_rows, 0)
        block_v = lax.dynamic_slice_in_dim(with_v, first_row, block_rows, 0)
        near_rows = lax.dynamic_slice_in_dim(
            place_rows, length - block_rows - first_row, block_rows + length - 1, 0
        )
        scores = (
            mult_trans(block_u, key_rows) + skew_rows(mult_trans(block_v, near_rows))
        ) * score_scale
        scores = jnp.where(key_ok[None, :], scores, MASKED_SCORE)
        highest = jnp.max(scores, axis=1, keepdims=True)
        weights = jnp.exp(scores - highest)
        running = jnp.sum(weights, axis=1, keepdims=True)
        attend_prob = (weights / running).astype(jnp.bfloat16)
        return (
            mult_plain(attend_prob, value_rows).astype(jnp.bfloat16),
            (highest + jnp.log(running))[:, 0],
        )

    attended, log_total = lax.map(one_block, jnp.arange(length // block_rows, dtype=jnp.int32))
    return (attended.reshape(length, head_width), log_total.reshape(length))


def head_backward(
    query_rows,
    key_rows,
    value_rows,
    place_rows,
    bias_first,
    bias_second,
    key_ok,
    log_total,
    grad_mixed,
    block_rows,
    score_scale,
):
    length, head_width = query_rows.shape
    span = block_rows + length - 1
    with_u = (query_rows.astype(jnp.float32) + bias_first).astype(jnp.bfloat16)
    with_v = (query_rows.astype(jnp.float32) + bias_second).astype(jnp.bfloat16)

    def one_block(carried, block_index):
        grad_key, grad_value, grad_place = carried
        first_row = block_index * block_rows
        place_first = length - block_rows - first_row
        block_u = lax.dynamic_slice_in_dim(with_u, first_row, block_rows, 0)
        block_v = lax.dynamic_slice_in_dim(with_v, first_row, block_rows, 0)
        near_rows = lax.dynamic_slice_in_dim(place_rows, place_first, span, 0)
        block_total = lax.dynamic_slice_in_dim(log_total, first_row, block_rows, 0)
        block_grad = lax.dynamic_slice_in_dim(grad_mixed, first_row, block_rows, 0)
        scores = (
            mult_trans(block_u, key_rows) + skew_rows(mult_trans(block_v, near_rows))
        ) * score_scale
        scores = jnp.where(key_ok[None, :], scores, MASKED_SCORE)
        attend_prob = jnp.exp(scores - block_total[:, None])
        grad_prob = mult_trans(block_grad, value_rows)
        inner = jnp.sum(attend_prob * grad_prob, axis=1, keepdims=True)
        grad_score = jnp.where(key_ok[None, :], attend_prob * (grad_prob - inner), 0.0).astype(
            jnp.bfloat16
        )
        grad_value = grad_value + mult_rows(attend_prob.astype(jnp.bfloat16), block_grad)
        grad_with_u = mult_plain(grad_score, key_rows) * score_scale
        grad_key = grad_key + mult_rows(grad_score, block_u) * score_scale
        spread_grad = unskew_rows(grad_score, span)
        grad_with_v = mult_plain(spread_grad, near_rows) * score_scale
        place_part = (
            lax.dynamic_slice_in_dim(grad_place, place_first, span, 0)
            + mult_rows(spread_grad, block_v) * score_scale
        )
        grad_place = lax.dynamic_update_slice_in_dim(grad_place, place_part, place_first, 0)
        return ((grad_key, grad_value, grad_place), (grad_with_u, grad_with_v))

    zero_rows = jnp.zeros((length, head_width), jnp.float32)
    zero_place = jnp.zeros((2 * length - 1, head_width), jnp.float32)
    (grad_key, grad_value, grad_place), (grad_with_u, grad_with_v) = lax.scan(
        one_block,
        (zero_rows, zero_rows, zero_place),
        jnp.arange(length // block_rows, dtype=jnp.int32),
    )
    grad_with_u = grad_with_u.reshape(length, head_width)
    grad_with_v = grad_with_v.reshape(length, head_width)
    grad_query = (grad_with_u + grad_with_v).astype(jnp.bfloat16)
    return (
        grad_query,
        grad_key.astype(jnp.bfloat16),
        grad_value.astype(jnp.bfloat16),
        grad_place.astype(jnp.bfloat16),
        jnp.sum(grad_with_u, axis=0),
        jnp.sum(grad_with_v, axis=0),
    )


def biased(q_ref, bias_ref, scale):
    return ((q_ref[...].astype(jnp.float32) + bias_ref[...].astype(jnp.float32)).astype(jnp.bfloat16).astype(jnp.float32) * scale).astype(jnp.bfloat16)

def attend_fwd_kernel(len_ref, q_ref, k_ref, v_ref, place_ref, cb_ref, pb_ref, out_ref, prob_ref, *, scale):
    rows = q_ref.shape[0]
    length = k_ref.shape[0]
    span = rows + length
    first = pl.multiple_of(length - rows - pl.program_id(1) * rows, rows)
    lanes = lax.broadcasted_iota(jnp.int32, (rows, PAIR), 1)
    with_u = biased(q_ref, cb_ref, scale)
    with_v = biased(q_ref, pb_ref, scale)
    window = place_ref[pl.ds(first, span), :]
    key_ok = lax.broadcasted_iota(jnp.int32, (rows, length), 1) < len_ref[0]
    zero = jnp.zeros_like(with_u)
    mixed = []
    for head in range(2):
        mine = (lanes // HEAD_DIM) == head
        place_part = mult_trans(jnp.where(mine, with_v, zero), window)
        place_part = pltpu.roll(place_part, span - rows + 1, 1, stride=1, stride_axis=0)
        scores = mult_trans(jnp.where(mine, with_u, zero), k_ref[...]) + place_part[:, :length]
        scores = jnp.where(key_ok, scores, MASKED_SCORE)
        weights = jnp.exp(scores - jnp.max(scores, axis=1, keepdims=True))
        total = jnp.sum(weights, axis=1, keepdims=True)
        prob = (weights * (1.0 / total)).astype(jnp.bfloat16)
        prob_ref[head] = prob
        mixed.append(mult_plain(prob, v_ref[...]))
    out_ref[...] = jnp.where(lanes < HEAD_DIM, mixed[0], mixed[1]).astype(jnp.bfloat16)

def attend_fwd_gather_kernel(layers, count, blocks, *refs, scale):
    ins, shards, refs = refs[:7], refs[7 : 7 + count], refs[7 + count :]
    outs, fulls, sems = refs[:2], refs[2 : 2 + count], refs[2 + count :]
    at = pl.program_id(0) * pl.num_programs(1) + pl.program_id(1)
    plan = gather_plan(layers, shards, fulls, (), *sems)
    run_between(*plan, at, blocks, partial(attend_fwd_kernel, *ins, *outs, scale=scale))


def attend_fwd(length_arr, q, k, v, place, cb, pb, rows, layers, shards, collective_id):
    length, width = q.shape
    pairs = width // PAIR
    count = len(shards)
    shard = shards[0].shape
    part = pl.BlockSpec((rows, PAIR), lambda p, i: (i, p))
    full = pl.BlockSpec((length, PAIR), lambda p, i: (0, p))
    tall = pl.BlockSpec((2 * length, PAIR), lambda p, i: (0, p))
    vec = pl.BlockSpec((1, PAIR), lambda p, i: (0, p))
    far = [pl.BlockSpec(memory_space=pl.ANY)] * count
    blocks = pairs * (length // rows)
    attended, prob, *fulls = pl.pallas_call(
        partial(attend_fwd_gather_kernel, layers, count, blocks, scale=1.0 / math.sqrt(HEAD_DIM)),
        grid=(pairs, length // rows),
        in_specs=[pl.BlockSpec(memory_space=pltpu.SMEM), part, full, full, tall, vec, vec] + far,
        out_specs=[part, pl.BlockSpec((2, rows, length), lambda p, i: (p, i, 0))] + far,
        out_shape=[
            jax.ShapeDtypeStruct((length, width), jnp.bfloat16),
            jax.ShapeDtypeStruct((2 * pairs, length, length), jnp.bfloat16),
        ]
        + [jax.ShapeDtypeStruct((layers, 2, 2, 2, *shard), jnp.bfloat16)] * count,
        scratch_shapes=gather_sems(count, layers),
        compiler_params=pltpu.CompilerParams(
            vmem_limit_bytes=VMEM, collective_id=collective_id, has_side_effects=True
        ),
        cost_estimate=pl.CostEstimate(
            flops=40 * 10**9, bytes_accessed=20 * 2**20, transcendentals=2 * pairs * length * length
        ),
        name="attend_fwd",
    )(length_arr, q, k, v, place, cb, pb, *shards)
    return attended, prob, [full.reshape(-1, shard[1]) for full in fulls]


def attend_bwd_kernel(q_ref, k_ref, v_ref, place_ref, cb_ref, pb_ref, prob_ref, g_ref, gq_ref, gk_ref, gv_ref, gp_ref, gb_ref, gk_s, gv_s, gp_s, *, scale):
    rows = q_ref.shape[0]
    length = k_ref.shape[0]
    span = rows + length
    step = pl.program_id(1)
    first = pl.multiple_of(length - rows - step * rows, rows)
    lanes = lax.broadcasted_iota(jnp.int32, (rows, PAIR), 1)
    flip = (lax.broadcasted_iota(jnp.int32, (rows, rows), 0) + lax.broadcasted_iota(jnp.int32, (rows, rows), 1) == rows - 1).astype(jnp.bfloat16)
    with_u = biased(q_ref, cb_ref, scale)
    with_v = mult_plain(flip, biased(q_ref, pb_ref, scale)).astype(jnp.bfloat16)
    grad = g_ref[...]
    window = place_ref[pl.ds(first, span), :]
    zero = jnp.zeros_like(with_u)

    @pl.when(step == 0)
    def _():
        gk_s[...] = jnp.zeros_like(gk_s)
        gv_s[...] = jnp.zeros_like(gv_s)
        gp_s[...] = jnp.zeros_like(gp_s)
        gb_ref[...] = jnp.zeros_like(gb_ref)

    grad_t, with_u_t, with_v_t = grad.T, with_u.T, with_v.T
    gu = []
    gw = []
    for head in range(2):
        mine = (lanes // HEAD_DIM) == head
        prob = prob_ref[head]
        grad_h = jnp.where(mine, grad, zero)
        grad_prob = mult_trans(grad_h, v_ref[...])
        weighted = prob.astype(jnp.float32) * grad_prob
        inner = jnp.sum(weighted, axis=1, keepdims=True)
        grad_score = (weighted - prob.astype(jnp.float32) * inner).astype(jnp.bfloat16)
        turned = mult_plain(flip, grad_score).astype(jnp.bfloat16)
        turned = jnp.concatenate([turned, jnp.zeros((rows, rows), jnp.bfloat16)], axis=1)
        turned = pltpu.roll(turned, 0, 1, stride=1, stride_axis=0)
        gu.append(mult_plain(grad_score, k_ref[...]))
        gw.append(mult_plain(turned, window))
        band = slice(head * HEAD_DIM, (head + 1) * HEAD_DIM)
        gv_s[band, :] += mult_plain(grad_t[band, :], prob)
        gk_s[band, :] += mult_plain(with_u_t[band, :], grad_score)
        gp_s[band, pl.ds(first, span)] += mult_plain(with_v_t[band, :], turned)
    grad_u = jnp.where(lanes < HEAD_DIM, gu[0], gu[1]) * scale
    grad_w = jnp.where(lanes < HEAD_DIM, gw[0], gw[1]) * scale
    gb_ref[0:1, :] += jnp.sum(grad_u, axis=0, keepdims=True)
    gb_ref[1:2, :] += jnp.sum(grad_w, axis=0, keepdims=True)
    high = grad_w.astype(jnp.bfloat16)
    rest = (grad_w - high.astype(jnp.float32)).astype(jnp.bfloat16)
    gq_ref[...] = (grad_u + mult_plain(flip, high) + mult_plain(flip, rest)).astype(jnp.bfloat16)

    @pl.when(step == pl.num_programs(1) - 1)
    def _():
        gk_ref[...] = gk_s[...].T.astype(jnp.bfloat16)
        gv_ref[...] = gv_s[...].T.astype(jnp.bfloat16)
        gp_ref[...] = gp_s[...].T.astype(jnp.bfloat16)


def attend_bwd_sum_kernel(layers, shared, count, blocks, *refs, scale):
    ins, parts = refs[:8], refs[8 : 8 + count]
    refs = refs[8 + count :]
    outs, sums, scratch, own = refs[:5], refs[5 : 5 + count], refs[5 + count : 8 + count], refs[8 + count :]
    at = pl.program_id(0) * pl.num_programs(1) + pl.program_id(1)
    plan = reduce_plan(layers, shared, parts, sums, None, own)
    body = partial(attend_bwd_kernel, *ins, *outs, *scratch, scale=scale)
    run_between(*plan, at, blocks, body)


def attend_bwd(q, k, v, place, cb, pb, prob, grad, rows, layers, shared, parts, collective_id):
    length, width = q.shape
    pairs = width // PAIR
    count = len(parts)
    inputs, shapes = reduce_shapes(layers, shared, parts)
    shard, channels = shapes[shared].shape[2:]
    still = lambda shape: pl.BlockSpec(shape, lambda p, i: (0,) * len(shape))
    full = pl.BlockSpec((length, PAIR), lambda p, i: (0, p))
    part = pl.BlockSpec((rows, PAIR), lambda p, i: (i, p))
    vec = pl.BlockSpec((1, PAIR), lambda p, i: (0, p))
    tall = pl.BlockSpec((2 * length, PAIR), lambda p, i: (0, p))
    return pl.pallas_call(
        partial(attend_bwd_sum_kernel, layers, shared, count, pairs * (length // rows), scale=1.0 / math.sqrt(HEAD_DIM)),
        grid=(pairs, length // rows),
        in_specs=[
            part,
            full,
            full,
            tall,
            vec,
            vec,
            pl.BlockSpec((2, rows, length), lambda p, i: (p, i, 0)),
            part,
        ]
        + [pl.BlockSpec(memory_space=pl.ANY)] * count,
        out_specs=[part, full, full, tall, pl.BlockSpec((8, PAIR), lambda p, i: (0, p))]
        + [still(shape.shape) for shape in shapes],
        out_shape=[
            jax.ShapeDtypeStruct((length, width), jnp.bfloat16),
            jax.ShapeDtypeStruct((length, width), jnp.bfloat16),
            jax.ShapeDtypeStruct((length, width), jnp.bfloat16),
            jax.ShapeDtypeStruct((2 * length, width), jnp.bfloat16),
            jax.ShapeDtypeStruct((8, width), jnp.float32),
        ]
        + shapes,
        scratch_shapes=[
            pltpu.VMEM((PAIR, length), jnp.float32),
            pltpu.VMEM((PAIR, length), jnp.float32),
            pltpu.VMEM((PAIR, 2 * length), jnp.float32),
        ]
        + reduce_scratch(count, layers, shard, channels),
        compiler_params=pltpu.CompilerParams(
            vmem_limit_bytes=VMEM, collective_id=collective_id, has_side_effects=True
        ),
        cost_estimate=pl.CostEstimate(
            flops=100 * 10**9, bytes_accessed=40 * 2**20, transcendentals=0
        ),
        name="attend_bwd",
    )(
        q,
        k,
        v,
        place,
        cb,
        pb,
        prob,
        grad,
        *inputs,
    )


MESH = pl.DeviceIdType.MESH


def chip_place(layers):
    z, c, y, x = (lax.axis_index(axis) for axis in ("z", "core", "y", "x"))

    def at(dz=0, dc=0, dy=0, dx=0):
        return (
            lax.rem(z + dz, layers),
            lax.rem(c + dc, 2),
            lax.rem(y + dy, 2),
            lax.rem(x + dx, 2),
        )

    def spot(dz=0, dc=0, dy=0, dx=0):
        return at(layers - dz, dc, dy, dx)

    return at, spot


def greet(at, layers):
    barrier = pltpu.get_barrier_semaphore()
    peers = [at(dz=k) for k in range(1, layers)] + [at(dc=1), at(dy=1), at(dx=1)]
    for peer in peers:
        pl.semaphore_signal(barrier, inc=1, device_id=peer, device_id_type=MESH)
    pl.semaphore_wait(barrier, len(peers))


def remote(source, target, sems, index, device):
    return pltpu.make_async_remote_copy(
        src_ref=source,
        dst_ref=target,
        send_sem=sems.at[(0, *index)],
        recv_sem=sems.at[(1, *index)],
        device_id=device,
        device_id_type=MESH,
    )


def far_first(layers):
    return sorted(range(1, layers), key=lambda k: -min(k, layers - k)) + [0]


def gather_plan(layers, shards, fulls, flat_only, z_sem, p_sem, d_sem, c_sem, own_sem):
    at, spot = chip_place(layers)
    arrays = range(len(shards))
    z, _, _, _ = spot()
    odd = lax.rem(z, 2)
    pair = at(dz=1 + odd * (layers - 2))
    items = [(0, a) for a in flat_only]
    items += [(dz, a) for dz in reversed(far_first(layers)) for a in arrays if a not in flat_only]
    own, along, flat, cross, last = {}, {}, {}, {}, {}
    for dz, a in items:
        full = fulls[a]
        flat_at = a in flat_only
        place = (lambda *_, **by: (odd, *spot(**by)[2:])) if flat_at else (lambda **by: spot(dz, **by))
        half = shards[a].shape[0] // 32 * 16
        source = full.at[place()] if dz else shards[a]
        if dz:
            along[dz, a] = remote(shards[a], full.at[spot()], z_sem, (a, dz), at(dz=dz))
        else:
            own[dz, a] = pltpu.make_async_copy(shards[a], full.at[place()], own_sem.at[a])
        flat[dz, a] = (
            remote(source, full.at[place()], p_sem, (a, dz, 0), at(dx=1)),
            remote(source, full.at[place()], p_sem, (a, dz, 1), at(dy=1)),
        )
        from_x = full.at[(*place(dx=1), pl.ds(half, shards[a].shape[0] - half))]
        from_y = full.at[(*place(dy=1), pl.ds(0, half))]
        cross[dz, a] = (
            remote(from_x, from_x, d_sem, (a, dz, 0), at(dy=1)),
            remote(from_y, from_y, d_sem, (a, dz, 1), at(dx=1)),
        )
        plane = full.at[place()[:-2]]
        last[dz, a] = remote(plane, plane, c_sem, (a, dz), pair if flat_at else at(dc=1))

    def enter():
        greet(at, layers)
        for item in items:
            if item[0]:
                along[item].start()
        for copy in own.values():
            copy.start()

    def spread(item):
        if item in along:
            along[item].wait_recv()
        for copy in flat[item]:
            copy.start()

    def turn(item):
        for got, out in zip(flat[item], cross[item]):
            got.wait_recv()
            out.start()

    def share(item):
        for got in cross[item]:
            got.wait_recv()
        if item in own:
            own[item].wait()
        last[item].start()

    def step(turn_at):
        for action, lag in ((spread, 0), (turn, 2), (share, 4)):
            if 0 <= turn_at - lag < len(items):
                action(items[turn_at - lag])

    def leave():
        for item in items:
            last[item].wait_recv()
        for item in items:
            if item in along:
                along[item].wait_send()
            for copy in (*flat[item], *cross[item], last[item]):
                copy.wait_send()

    return enter, step, len(items) + 4, leave


def gather_sems(count, layers):
    dma = pltpu.SemaphoreType.DMA
    return [
        dma((2, count, layers)),
        dma((2, count, layers, 2)),
        dma((2, count, layers, 2)),
        dma((2, count, layers)),
        dma((count,)),
    ]


def gather_kernel(layers, count, *refs):
    enter, step, turns, leave = gather_plan(
        layers, refs[:count], refs[count : 2 * count], (count - 1,), *refs[2 * count :]
    )
    enter()
    for turn_at in range(turns):
        step(turn_at)
    leave()


def gather_all(layers, shards, flat_shard, collective_id):
    ins = [*shards, flat_shard]
    count = len(ins)
    width = flat_shard.shape[1]
    shapes = [(layers, 2, 2, 2, *shard.shape) for shard in shards] + [(2, 2, 2, *flat_shard.shape)]
    *fulls, flat_full = pl.pallas_call(
        partial(gather_kernel, layers, count),
        in_specs=[pl.BlockSpec(memory_space=pl.ANY)] * count,
        out_specs=[pl.BlockSpec(memory_space=pl.ANY)] * count,
        out_shape=[jax.ShapeDtypeStruct(shape, jnp.bfloat16) for shape in shapes],
        scratch_shapes=gather_sems(count, layers),
        compiler_params=pltpu.CompilerParams(collective_id=collective_id, has_side_effects=True),
        cost_estimate=pl.CostEstimate(flops=0, bytes_accessed=300 * 2**20, transcendentals=0),
        name="gather_all",
    )(*ins)
    return [full.reshape(-1, width) for full in fulls], flat_full


def add_rows(target, one, two):
    target[...] = (one[...].astype(jnp.float32) + two[...].astype(jnp.float32)).astype(target.dtype)


def reduce_plan(layers, shared, parts, outs, small, scratch, made=None, summed=None):
    at, spot = chip_place(layers)
    sums, got_c, got_d, got_p, got_z, got_s, load_sem, c_sem, d_sem, p_sem, z_sem, s_sem, *tiny = scratch
    arrays = range(len(parts))
    rows = sums.shape[4]
    half = rows // 2
    order = far_first(layers)
    items = [(dz, shared) for dz in order if summed is None]
    items += [(dz, a) for dz in order for a in arrays if a != shared]
    first, second = pl.ds(0, half), pl.ds(half, half)
    here, by_y, by_x, far = (spot(0, 0, dy, dx)[2:] for dy, dx in ((0, 0), (1, 0), (0, 1), (1, 1)))
    made = made or {}
    whole = [a in made or len(parts[a].shape) == 6 for a in arrays]
    core_at = spot()[1]
    load, core, cross, flat, along = {}, {}, {}, {}, {}
    for dz, a in items:
        total = sums.at[a, dz]
        if a not in made:
            source = parts[a].at[spot(dz)[:2]] if whole[a] else parts[a].at[spot(dz)[0]]
            load[dz, a] = pltpu.make_async_copy(source, total, load_sem.at[a, dz])
        if whole[a]:
            slot = order.index(dz) % 2
            source = parts[a].at[slot] if a in made else parts[a].at[spot(dz, dc=1)[:2]]
            core[dz, a] = remote(source, got_c.at[a, dz], c_sem, (a, dz), at(dc=1))
        cross[dz, a] = (
            remote(total.at[(*far, first)], got_d.at[a, dz, 0], d_sem, (a, dz, 0), at(dx=1)),
            remote(total.at[(*far, second)], got_d.at[a, dz, 1], d_sem, (a, dz, 1), at(dy=1)),
        )
        flat[dz, a] = (
            remote(total.at[by_y], got_p.at[a, dz, 0], p_sem, (a, dz, 0), at(dy=1)),
            remote(total.at[by_x], got_p.at[a, dz, 1], p_sem, (a, dz, 1), at(dx=1)),
        )
        if dz:
            along[dz, a] = remote(
                total.at[here], got_z.at[a, dz], z_sem, (a, dz), at(dz=layers - dz)
            )
    own = got_s.at[(core_at, spot()[0])]
    handed = {k: remote(own, own, s_sem, (k,), at(dz=k)) for k in range(1, layers)}
    swapped = remote(got_s.at[core_at], got_s.at[core_at], s_sem, (0,), at(dc=1))
    sent = {}
    if summed:
        got_m, m_sem = tiny[3:]
        sent = {
            k: remote(summed[0].at[spot(k)[0]], got_m.at[k], m_sem, (k,), at(dz=layers - k))
            for k in range(1, layers)
        }
    hops = []
    if small:
        level, got_t, t_sem = tiny[:3]
        hops = [
            remote(level.at[i], got_t.at[i], t_sem, (i,), device)
            for i, device in enumerate((at(dc=1), at(dx=1), at(dy=1)))
        ]
        hops += [
            remote(level.at[3], got_t.at[2 + k], t_sem, (2 + k,), at(dz=k)) for k in range(1, layers)
        ]

    def enter():
        greet(at, layers)
        if small:
            level[0] = small[0][...]
            hops[0].start()
        for copy in sent.values():
            copy.start()
        for item in items:
            if item in load:
                load[item].start()
                if item in core:
                    core[item].start()

    def make(item):
        dz, a = item
        if a not in made:
            return
        left, right = made[a]
        size = 4 * rows
        turn_of = order.index(dz)
        if turn_of >= 2:
            core[order[turn_of - 2], a].wait_send()
        for dc, target in ((1, parts[a].at[turn_of % 2]), (0, sums.at[a, dz])):
            z_at, c_at = spot(dz, dc)[:2]
            columns = pl.ds(pl.multiple_of((2 * z_at + c_at) * size, size), size)
            block = mult_rows(left[:, columns], right[...]).astype(jnp.bfloat16)
            for at_y in range(2):
                for at_x in range(2):
                    row = (2 * at_y + at_x) * rows
                    target[at_y, at_x] = block[row : row + rows]
            if dc:
                core[item].start()

    def join_core(item):
        dz, a = item
        if item in load:
            load[item].wait()
        if whole[a]:
            core[item].wait_recv()
        for place in (far, by_y, by_x, here):
            target = sums.at[(a, dz, *place)]
            if whole[a]:
                add_rows(target, target, got_c.at[(a, dz, *place)])
            if place is far:
                for copy in cross[item]:
                    copy.start()

    def join_cross(item):
        dz, a = item
        one, two = sums.at[(a, dz, *by_y, first)], sums.at[(a, dz, *by_x, second)]
        cross[item][0].wait_recv()
        add_rows(one, one, got_d.at[a, dz, 0])
        flat[item][0].start()
        cross[item][1].wait_recv()
        add_rows(two, two, got_d.at[a, dz, 1])
        flat[item][1].start()

    def join_flat(item):
        dz, a = item
        target = sums.at[(a, dz, *here)]
        for copy in flat[item]:
            copy.wait_recv()
        target[...] = (
            target[...].astype(jnp.float32)
            + got_p[a, dz, 0].astype(jnp.float32)
            + got_p[a, dz, 1].astype(jnp.float32)
        ).astype(jnp.bfloat16)
        if dz:
            along[item].start()

    def total_of(a):
        total = sums[(a, 0, *here)].astype(jnp.float32)
        for dz in range(1, layers):
            along[dz, a].wait_recv()
            total = total + got_z[a, dz].astype(jnp.float32)
        return total

    def join_small(turn_at):
        if turn_at < 3:
            hops[turn_at].wait_recv()
            level[turn_at + 1] = level[turn_at] + got_t[turn_at]
            for hop in hops[turn_at + 1 : turn_at + 2] if turn_at < 2 else hops[3:]:
                hop.start()
        else:
            total = level[3]
            for k in range(1, layers):
                hops[2 + k].wait_recv()
                total = total + got_t[2 + k]
            small[1][...] = total

    def hand_on():
        if summed:
            total = summed[0][spot()[0]].astype(jnp.float32)
            for k, copy in sent.items():
                copy.wait_recv()
                total = total + got_m[k].astype(jnp.float32)
        else:
            total = total_of(shared)
        own[...] = total.astype(jnp.bfloat16)
        for copy in handed.values():
            copy.start()

    def swap():
        for copy in handed.values():
            copy.wait_recv()
        swapped.start()

    lead, near, wide = (1, 1, 2) if made else (0, 2, 4)
    handed_at = 5 if summed else layers - 1 + wide + 2 + lead
    turns = max(len(items) + wide + lead, handed_at + 4)

    def step(turn_at):
        actions = ((make, 0), (join_core, lead), (join_cross, lead + near), (join_flat, lead + wide))
        for action, lag in actions:
            if 0 <= turn_at - lag < len(items):
                action(items[turn_at - lag])
        if small and 1 <= turn_at <= 4:
            join_small(turn_at - 1)
        if turn_at == handed_at:
            hand_on()
        if turn_at == handed_at + 3:
            swap()

    def leave():
        for a in arrays:
            if a != shared:
                outs[a][...] = total_of(a)
        swapped.wait_recv()
        (summed[1] if summed else outs[shared])[...] = got_s[...]
        for item in items:
            if item[0]:
                along[item].wait_send()
            for copy in (*cross[item], *flat[item]):
                copy.wait_send()
            if item in core and not (item[1] in made and item[0] in order[:-2]):
                core[item].wait_send()
        for copy in (*handed.values(), *sent.values(), swapped, *hops):
            copy.wait_send()

    return enter, step, turns, leave


def reduce_scratch(count, layers, rows, width, small=None):
    dma = pltpu.SemaphoreType.DMA
    low = lambda *shape: pltpu.VMEM((count, layers, *shape, width), jnp.bfloat16)
    scratch = [
        low(2, 2, rows),
        low(2, 2, rows),
        low(2, rows // 2),
        low(2, rows),
        low(rows),
        pltpu.VMEM((2, layers, rows, width), jnp.bfloat16),
        dma((count, layers)),
        dma((2, count, layers)),
        dma((2, count, layers, 2)),
        dma((2, count, layers, 2)),
        dma((2, count, layers)),
        dma((2, layers)),
    ]
    if small is not None:
        scratch += [
            pltpu.VMEM((4, *small.shape), jnp.float32),
            pltpu.VMEM((2 + layers, *small.shape), jnp.float32),
            dma((2, 2 + layers)),
            pltpu.VMEM((layers, rows, width), jnp.bfloat16),
            dma((2, layers)),
        ]
    return scratch


def reduce_shapes(layers, shared, parts):
    blocks, shapes = [], []
    for a, (part, count) in enumerate(parts):
        width = part.shape[-1]
        rows = part.size // width // (4 * count * layers)
        blocks.append(part.reshape(layers, *((2,) if count == 2 else ()), 2, 2, rows, width))
        if a == shared:
            shapes.append(jax.ShapeDtypeStruct((2, layers, rows, width), jnp.bfloat16))
        else:
            shapes.append(jax.ShapeDtypeStruct((rows, width), jnp.float32))
    return blocks, shapes


def reduce_kernel(layers, part, left_a, right_a, left_b, right_b, small, sum_a, sum_b, handed, total, ring_a, ring_b, *scratch):
    enter, step, turns, leave = reduce_plan(
        layers,
        None,
        (ring_a, ring_b),
        (sum_a, sum_b),
        (small, total),
        scratch,
        {0: (left_a, right_a), 1: (left_b, right_b)},
        (part, handed),
    )
    enter()
    for turn_at in range(turns):
        step(turn_at)
    leave()


def reduce_all(layers, part, products, small, collective_id):
    rows, width = part.shape[1:]
    near = pl.BlockSpec(memory_space=pltpu.VMEM)
    ring = pltpu.VMEM((2, 2, 2, rows, width), jnp.bfloat16)
    return pl.pallas_call(
        partial(reduce_kernel, layers),
        in_specs=[near] * 6,
        out_specs=[near] * 4,
        out_shape=[
            jax.ShapeDtypeStruct((rows, width), jnp.float32),
            jax.ShapeDtypeStruct((rows, width), jnp.float32),
            jax.ShapeDtypeStruct((2, layers, rows, width), jnp.bfloat16),
            jax.ShapeDtypeStruct(small.shape, jnp.float32),
        ],
        scratch_shapes=[ring, ring] + reduce_scratch(2, layers, rows, width, small),
        compiler_params=pltpu.CompilerParams(
            collective_id=collective_id, has_side_effects=True, vmem_limit_bytes=VMEM
        ),
        cost_estimate=pl.CostEstimate(
            flops=8 * 10**9, bytes_accessed=300 * 2**20, transcendentals=0
        ),
        name="reduce_all",
    )(part, *(matrix for product in products for matrix in product), small)


def run_between(enter, step, turns, leave, at, blocks, body):
    pl.when(at == 0)(enter)
    for turn_at in range(min(turns, blocks)):
        pl.when(at == turn_at)(partial(step, turn_at))
    body()

    @pl.when(at == blocks - 1)
    def _():
        for turn_at in range(blocks, turns):
            step(turn_at)
        leave()


def norm_stats(values):
    centred = values - jnp.mean(values, axis=-1, keepdims=True)
    inverse = lax.rsqrt(jnp.mean(centred * centred, axis=-1, keepdims=True) + EPSILON)
    return centred * inverse, inverse


def norm_back(normal, inverse, gain_vec, upstream):
    grad = upstream * gain_vec
    grad_mean = jnp.mean(grad, axis=-1, keepdims=True)
    grad_along = jnp.mean(grad * normal, axis=-1, keepdims=True)
    return (
        (grad - grad_mean - normal * grad_along) * inverse,
        jnp.sum(upstream * normal, axis=0, keepdims=True),
    )


def ffn_fwd_kernel(x_ref, gain_ref, up_ref, down_ref, y_ref, h_ref, act_ref, slope_ref):
    @pl.when(pl.program_id(0) == 0)
    def _():
        values = x_ref[...].astype(jnp.float32)
        normal, _ = norm_stats(values)
        h_ref[...] = (normal * gain_ref[...].astype(jnp.float32)).astype(jnp.bfloat16)
        y_ref[...] = values

    before = mult_trans(h_ref[...], up_ref[...])
    squash = 0.5 + 0.5 * jnp.tanh(0.5 * before)
    active = before * squash
    slope_ref[...] = (squash + active * (1.0 - squash)).astype(jnp.bfloat16)
    active_low = active.astype(jnp.bfloat16)
    act_ref[...] = active_low
    y_ref[...] += 0.5 * mult_plain(active_low, down_ref[...])


def ffn_blocks(rows, width, block):
    still = pl.BlockSpec((rows, width), lambda j: (0, 0))
    vec = pl.BlockSpec((1, width), lambda j: (0, 0))
    weight = pl.BlockSpec((block, width), lambda j: (j, 0))
    hidden = pl.BlockSpec((rows, block), lambda j: (0, j))
    return still, vec, weight, hidden


def ffn_fwd(x, gain_vec, up, down):
    rows, width = x.shape
    total = up.shape[0]
    still, vec, weight, hidden = ffn_blocks(rows, width, FF_BLOCK)
    return pl.pallas_call(
        ffn_fwd_kernel,
        grid=(total // FF_BLOCK,),
        in_specs=[still, vec, weight, weight],
        out_specs=[still, still, hidden, hidden],
        out_shape=[
            jax.ShapeDtypeStruct((rows, width), jnp.float32),
            jax.ShapeDtypeStruct((rows, width), jnp.bfloat16),
            jax.ShapeDtypeStruct((rows, total), jnp.bfloat16),
            jax.ShapeDtypeStruct((rows, total), jnp.bfloat16),
        ],
        compiler_params=pltpu.CompilerParams(vmem_limit_bytes=VMEM),
        cost_estimate=pl.CostEstimate(
            flops=4 * rows * width * total,
            bytes_accessed=4 * width * total + 4 * rows * total,
            transcendentals=rows * total,
        ),
        name="ffn_fwd",
    )(x, gain_vec, up, down)


def ffn_bwd_kernel(x_ref, gain_ref, g_ref, slope_ref, up_ref, down_ref, gx_ref, gf_ref, gp_ref, gain_out, sum_s):
    step = pl.program_id(0)

    @pl.when(step == 0)
    def _():
        gf_ref[...] = (0.5 * g_ref[...]).astype(jnp.bfloat16)
        sum_s[...] = jnp.zeros_like(sum_s)

    grad_act = mult_trans(gf_ref[...], down_ref[...])
    grad_before = (grad_act * slope_ref[...].astype(jnp.float32)).astype(jnp.bfloat16)
    gp_ref[...] = grad_before
    sum_s[...] += mult_plain(grad_before, up_ref[...])

    @pl.when(step == pl.num_programs(0) - 1)
    def _():
        normal, inverse = norm_stats(x_ref[...].astype(jnp.float32))
        grad, gain_grad = norm_back(normal, inverse, gain_ref[...].astype(jnp.float32), sum_s[...])
        gx_ref[...] = (g_ref[...] + grad).astype(gx_ref.dtype)
        gain_out[...] = gain_grad


def ffn_bwd(x, gain_vec, grad, slope, up, down, out_type):
    rows, width = x.shape
    total = up.shape[0]
    still, vec, weight, hidden = ffn_blocks(rows, width, FF_BLOCK)
    return pl.pallas_call(
        ffn_bwd_kernel,
        grid=(total // FF_BLOCK,),
        in_specs=[still, vec, still, hidden, weight, weight],
        out_specs=[still, still, hidden, vec],
        out_shape=[
            jax.ShapeDtypeStruct((rows, width), out_type),
            jax.ShapeDtypeStruct((rows, width), jnp.bfloat16),
            jax.ShapeDtypeStruct((rows, total), jnp.bfloat16),
            jax.ShapeDtypeStruct((1, width), jnp.float32),
        ],
        scratch_shapes=[pltpu.VMEM((rows, width), jnp.float32)],
        compiler_params=pltpu.CompilerParams(vmem_limit_bytes=VMEM),
        cost_estimate=pl.CostEstimate(
            flops=4 * rows * width * total,
            bytes_accessed=4 * width * total + 4 * rows * total,
            transcendentals=0,
        ),
        name="ffn_bwd",
    )(x, gain_vec, grad, slope, up, down)


class Hops:
    def __init__(self, layers):
        self.layers = layers

    def send(self, block, dz=0, dc=0, dy=0, dx=0):
        pairs = []
        for z in range(self.layers):
            for c in range(2):
                for w in range(4):
                    to = ((z + dz) % self.layers * 2 + (c ^ dc)) * 4 + (w ^ (2 * dy + dx))
                    pairs.append(((z * 2 + c) * 4 + w, to))
        return lax.ppermute(block, ("z", "core", "y", "x"), pairs)

    def turn(self, block, step):
        pairs = []
        for z in range(self.layers):
            for c in range(2):
                for w in range(4):
                    to = (z * 2 + w // 2) * 4 + 2 * c + ((w % 2) ^ step)
                    pairs.append(((z * 2 + c) * 4 + w, to))
        got = lax.ppermute(block, ("z", "core", "y", "x"), [pair for pair in pairs if pair[0] != pair[1]])
        if step:
            return got
        return jnp.where(lax.axis_index("core") == lax.axis_index("y"), block, got)


def relative_waves(length, channels):
    step = 32
    rates = jnp.exp(
        jnp.arange(channels // 2).astype(jnp.float32) * (-2.0 * math.log(10000.0) / channels)
    )
    coarse = (length - 1 - step * jnp.arange(2 * length // step)).astype(jnp.float32)
    fine = jnp.arange(step).astype(jnp.float32)
    coarse, fine = coarse[:, None, None] * rates, fine[None, :, None] * rates
    sin_c, cos_c, sin_f, cos_f = jnp.sin(coarse), jnp.cos(coarse), jnp.sin(fine), jnp.cos(fine)
    return jnp.concatenate(
        [sin_c * cos_f - cos_c * sin_f, cos_c * cos_f + sin_c * sin_f], axis=2
    ).reshape(2 * length, channels)


def taps_forward(padded, kernel_f, count):
    total = jnp.zeros((count, padded.shape[1]), jnp.float32)
    for offset in range(KERNEL):
        total = total + padded[offset : offset + count] * kernel_f[offset]
    return total


def with_rim(hops, block, core):
    edge = jnp.where(core == 0, block[-16:], block[:16])
    got = hops.send(edge, dc=1)
    zero = jnp.zeros_like(got)
    low = jnp.where(core == 0, zero, got)[1:]
    high = jnp.where(core == 0, got, zero)[:RIM]
    return jnp.concatenate([low, block, high])


def per_chip(
    frames,
    lengths,
    masked,
    cotangent,
    first_gain,
    first_up,
    first_down,
    attn_gain,
    query_weight,
    key_weight,
    value_weight,
    out_weight,
    place_weight,
    content_bias,
    place_bias,
    conv_gain,
    glu_weight,
    depth_kernel,
    middle_gain,
    point_weight,
    second_gain,
    second_up,
    second_down,
    final_gain,
):
    core, y, x = lax.axis_index("core"), lax.axis_index("y"), lax.axis_index("x")
    wide_at = 2 * y + x
    layers = lax.axis_size("z")
    hops = Hops(layers)
    groups, quarter, channels = frames.shape
    rows = groups * quarter
    length = 2 * rows
    f32 = lambda v: v.astype(jnp.float32)
    low = lambda v: v.astype(jnp.bfloat16)

    def pick(flag, one, two):
        return jnp.where(flag, one, two), jnp.where(flag, two, one)

    def turn_in(block):
        swap = [lax.dynamic_index_in_dim(block, x ^ step, 0, keepdims=False) for step in range(2)]
        got = [hops.turn(swap[step], step) for step in range(2)]
        return jnp.concatenate(pick(x == 0, *got))

    def turn_out(block):
        parts = pick(x == 0, block[:quarter], block[quarter:])
        got = [hops.turn(parts[step], step) for step in range(2)]
        return jnp.stack(pick(x == 0, *got))

    frames_own = turn_in(frames)
    positions = wide_at * quarter + jnp.arange(quarter, dtype=jnp.int32)
    seed_weight = f32(masked) * f32(positions[None, :] < lengths[:, None])
    seed_own_low = low(f32(cotangent) * seed_weight[:, :, None])
    near_lengths = jnp.where(core == y, lengths, hops.send(lengths, dc=1))
    own_length = lax.dynamic_slice_in_dim(near_lengths, x, 1)
    own_rows = core * rows + jnp.arange(rows, dtype=jnp.int32)
    frame_ok = f32(own_rows < own_length[0])[:, None]

    def own_half(weight):
        count = weight.shape[0] // 2
        return lax.dynamic_slice_in_dim(weight, core * count, count)

    band = query_weight.shape[0] // 2
    odd = lax.rem(lax.axis_index("z"), 2)
    piece = band // 2

    def own_quarter(weight):
        return lax.dynamic_slice_in_dim(weight, core * band + odd * piece, piece)

    own_bias = own_half(jnp.stack([content_bias, place_bias], axis=1)).T
    attn_chunk = jnp.concatenate(
        [own_quarter(weight) for weight in (query_weight, key_weight, value_weight, place_weight)]
        + [jnp.pad(own_bias, ((0, 14), (0, channels - band)))]
    )
    (up_first, down_first), attn_all = gather_all(layers, [first_up, first_down], attn_chunk, 1)
    conv_chunk = jnp.concatenate([own_half(out_weight), own_half(point_weight), own_half(glu_weight)])
    conv_chunk, attn_all = lax.optimization_barrier((conv_chunk, attn_all))
    conv_all = lax.all_gather(conv_chunk, ("y", "x"), axis=0)
    attn_all = attn_all.reshape(2, 4, -1, channels)

    def heads_of(at):
        rows_of = attn_all[:, :, at * piece : (at + 1) * piece]
        return rows_of.transpose(1, 0, 2, 3).reshape(4 * band, channels)

    query_own, key_own, value_own, place_own = (heads_of(at) for at in range(4))
    own_biases = attn_all[0, :, 4 * piece : 4 * piece + 2, :band].transpose(1, 0, 2).reshape(2, 4 * band)
    conv_other = hops.send(conv_all, dc=1)
    conv_both = jnp.stack(pick(core == 0, conv_all, conv_other), axis=1)
    full_out = conv_both[:, :, :band].reshape(8 * band, channels)
    full_point = conv_both[:, :, band : 2 * band].reshape(8 * band, channels)
    full_glu = conv_both[:, :, 2 * band :].reshape(16 * band, channels)

    stream1, first_low, first_act, first_slope = ffn_fwd(
        frames_own, first_gain[None], up_first, down_first
    )
    stream1, seed_own_low = lax.optimization_barrier((stream1, seed_own_low))
    normed_attn, attn_pull = jax.vjp(norm_rows, stream1, f32(attn_gain))
    attn_half = low(normed_attn)
    attn_other = hops.send(attn_half, dc=1)
    attn_low = jnp.concatenate(pick(core == 0, attn_half, attn_other))
    rel_table = low(relative_waves(length, channels))
    query = low(mult_trans(attn_low, query_own))
    key = low(mult_trans(attn_low, key_own))
    value = low(mult_trans(attn_low, value_own))
    place = low(mult_trans(rel_table, place_own))
    attended, prob, (up_second, down_second) = attend_fwd(
        own_length,
        query,
        key,
        value,
        place,
        own_biases[:1],
        own_biases[1:],
        ROWS_FWD,
        layers,
        [second_up, second_down],
        4,
    )

    def halves(matrix):
        own = lax.dynamic_slice_in_dim(matrix, core * rows, rows)
        other = lax.dynamic_slice_in_dim(matrix, (1 - core) * rows, rows)
        return own, other

    att_own, att_other = halves(attended)
    att_parts = pick(core == 0, att_own, hops.send(att_other, dc=1))
    framed = jnp.stack([part.reshape(rows, 4, band) for part in att_parts], axis=2)
    framed = framed.reshape(rows, 8 * band)
    stream2 = stream1 + mult_plain(framed, full_out)
    normed_conv, conv_pull = jax.vjp(norm_rows, stream2, f32(conv_gain))
    conv_low = low(normed_conv)
    glu_in = mult_trans(conv_low, full_glu)
    linear = glu_in[:, :channels]
    gating = jax.nn.sigmoid(glu_in[:, channels:])
    gated = low(linear * gating * frame_ok)
    padded = with_rim(hops, gated, core)
    kernel_f = f32(depth_kernel)
    conv_out = taps_forward(padded, kernel_f, rows)
    middle, middle_pull = jax.vjp(norm_rows, conv_out, f32(middle_gain))
    swished = low(jax.nn.silu(middle))
    stream3 = stream2 + mult_trans(swished, full_point)
    stream4, second_low, second_act, second_slope = ffn_fwd(
        stream3, second_gain[None], up_second, down_second
    )
    final_rows, final_pull = jax.vjp(norm_rows, stream4, f32(final_gain))
    output = turn_out(low(final_rows))

    seed_own = turn_in(seed_own_low)
    grad4, grad_final_gain = final_pull(f32(seed_own))

    grad3, grad_out2, grad_before2, grad_second_gain = ffn_bwd(
        stream3, second_gain[None], grad4, second_slope, up_second, down_second, jnp.float32
    )
    grad_down_second = low(mult_rows(second_act, grad_out2))
    grad_up_second = low(mult_rows(grad_before2, second_low))
    grad3, output = lax.optimization_barrier((grad3, output))
    grad_branch = low(grad3)
    grad_point = mult_rows(grad_branch, swished)
    grad_middle = mult_plain(grad_branch, full_point) * silu_slope(middle)
    grad_conv, grad_middle_gain = middle_pull(grad_middle)
    conv_grad_low = low(grad_conv)
    grad_padded = with_rim(hops, conv_grad_low, core)
    grad_gated = taps_forward(grad_padded, kernel_f[::-1], rows)
    grad_kernel = jnp.stack(
        [
            jnp.sum(f32(padded[offset : offset + rows]) * f32(conv_grad_low), axis=0)
            for offset in range(KERNEL)
        ]
    )
    grad_gated = grad_gated * frame_ok
    grad_glu_in = low(
        jnp.concatenate(
            [grad_gated * gating, grad_gated * linear * gating * (1.0 - gating)], axis=1
        )
    )
    grad_glu = mult_rows(grad_glu_in, conv_low)
    grad_conv_in, grad_conv_gain = conv_pull(mult_plain(grad_glu_in, full_glu))
    grad2 = grad3 + grad_conv_in
    grad_attn = low(grad2)
    grad_out = mult_rows(framed, grad_attn)
    grad_framed = low(mult_trans(grad_attn, full_out))
    grad_parts = grad_framed.reshape(rows, 4, 2, band)
    grad_parts = [grad_parts[:, :, at].reshape(rows, 4 * band) for at in range(2)]
    grad_kept, grad_sent = pick(core == 0, *grad_parts)
    grad_heads = jnp.concatenate(pick(core == 0, grad_kept, hops.send(grad_sent, dc=1)))

    def by_place(matrix, cores):
        blocks = low(matrix).reshape(4, cores, layers, -1, channels)
        return blocks.transpose(2, 1, 0, 3, 4)

    conv_part = jnp.concatenate(
        [by_place(part, 2) for part in (grad_out, grad_point, grad_glu)], axis=3
    )
    *attn_grads, sum_up_second, sum_down_second, conv_sums = attend_bwd(
        query,
        key,
        value,
        place,
        own_biases[:1],
        own_biases[1:],
        prob,
        grad_heads,
        ROWS_BWD,
        layers,
        2,
        [(grad_up_second, 2), (grad_down_second, 2), (conv_part, 2)],
        3,
    )
    grad_query, grad_key, grad_value, grad_place, grad_biases = attn_grads
    grad_query_w = mult_rows(grad_query, attn_low)
    grad_key_w = mult_rows(grad_key, attn_low)
    grad_value_w = mult_rows(grad_value, attn_low)
    grad_place_w = mult_rows(grad_place, rel_table)
    attn_part = jnp.concatenate(
        [
            low(part).reshape(4, layers, -1, channels)
            for part in (grad_query_w, grad_key_w, grad_value_w, grad_place_w)
        ],
        axis=2,
    )
    attn_part, grad_query = lax.optimization_barrier((attn_part, grad_query))
    attn_part = lax.psum_scatter(attn_part, ("y", "x"), scatter_dimension=0, tiled=False)
    grad_normed = (
        mult_plain(grad_query, query_own)
        + mult_plain(grad_key, key_own)
        + mult_plain(grad_value, value_own)
    )
    normed_own, normed_other = halves(grad_normed)
    grad_attn_in, grad_attn_gain = attn_pull(normed_own + f32(hops.send(low(normed_other), dc=1)))
    grad1 = grad2 + grad_attn_in
    grad0, grad_out1, grad_before1, grad_first_gain = ffn_bwd(
        frames_own, first_gain[None], grad1, first_slope, up_first, down_first, jnp.bfloat16
    )
    grad_input = turn_out(grad0)

    spread = jnp.zeros((2, 4, 2, band), jnp.float32)
    spread = lax.dynamic_update_slice(
        spread, grad_biases[:2].reshape(2, 4, 1, band), (0, 0, core, 0)
    ).reshape(2, channels)
    gains = (
        grad_conv_gain,
        grad_middle_gain,
        grad_second_gain[0],
        grad_final_gain,
        grad_first_gain[0],
        grad_attn_gain,
    )
    small = jnp.concatenate([jnp.stack(gains), spread, grad_kernel])
    small = jnp.pad(small, ((0, -small.shape[0] % 8), (0, 0)))
    sum_up_first, sum_down_first, attn_sums, small = reduce_all(
        layers,
        attn_part,
        [(grad_before1, first_low), (first_act, grad_out1)],
        small,
        2,
    )

    def owned(sums, start, count):
        return f32(sums[:, :, start : start + count]).reshape(-1, channels)

    step = band // layers
    total_out, total_point = owned(conv_sums, 0, step), owned(conv_sums, step, step)
    total_glu = owned(conv_sums, 2 * step, 2 * step)
    total_query, total_key, total_value, total_place = (
        owned(attn_sums, at * step, step) for at in range(4)
    )
    own_bias_grad = lax.dynamic_slice_in_dim(small[6:8], wide_at * 2 * band, 2 * band, 1)
    return (
        output,
        grad_input,
        small[4],
        sum_up_first,
        sum_down_first,
        small[5],
        total_query,
        total_key,
        total_value,
        total_out,
        total_place,
        own_bias_grad[0],
        own_bias_grad[1],
        small[0],
        total_glu,
        small[8 : 8 + KERNEL],
        small[1],
        total_point,
        small[2],
        sum_up_second,
        sum_down_second,
        small[3],
    )


def per_device(
    frames,
    lengths,
    masked,
    cotangent,
    first_gain,
    first_up,
    first_down,
    attn_gain,
    query_weight,
    key_weight,
    value_weight,
    out_weight,
    place_weight,
    content_bias,
    place_bias,
    conv_gain,
    glu_weight,
    depth_kernel,
    middle_gain,
    point_weight,
    second_gain,
    second_up,
    second_down,
    final_gain,
):
    groups, frames_dev, channels = frames.shape
    row_count = groups * frames_dev
    length = frames_dev * lax.axis_size("wide")
    score_scale = 1.0 / math.sqrt(HEAD_DIM)
    positions = lax.axis_index("wide") * frames_dev + jnp.arange(frames_dev, dtype=jnp.int32)
    frame_grid = (positions[None, :] < lengths[:, None]).astype(jnp.float32)
    frame_ok = frame_grid.reshape(row_count, 1)
    key_ok = jnp.arange(length, dtype=jnp.int32)[None, :] < lengths[:, None]
    stream0 = frames.reshape(row_count, channels).astype(jnp.float32)
    up_first, down_first = gather_ffn(first_up, first_down)
    stream1, saved_first = ffn_forward(
        stream0, first_gain.astype(jnp.float32), up_first, down_first
    )
    full_query, full_key, full_value, full_out, full_glu, full_point = (
        lax.all_gather(query_weight, "wide", axis=0, tiled=True),
        lax.all_gather(key_weight, "wide", axis=0, tiled=True),
        lax.all_gather(value_weight, "wide", axis=0, tiled=True),
        lax.all_gather(out_weight, "wide", axis=0, tiled=True),
        lax.all_gather(glu_weight, "wide", axis=0, tiled=True),
        lax.all_gather(point_weight, "wide", axis=0, tiled=True),
    )
    normed_attn, attn_pull = jax.vjp(norm_rows, stream1, attn_gain.astype(jnp.float32))
    attn_low = normed_attn.astype(jnp.bfloat16)
    query_frames = (
        mult_trans(attn_low, full_query).astype(jnp.bfloat16).reshape(groups, frames_dev, -1)
    )
    key_frames = mult_trans(attn_low, full_key).astype(jnp.bfloat16).reshape(groups, frames_dev, -1)
    value_frames = (
        mult_trans(attn_low, full_value).astype(jnp.bfloat16).reshape(groups, frames_dev, -1)
    )
    heads_query, heads_key, heads_value = (
        lax.all_to_all(query_frames, "wide", split_axis=2, concat_axis=1, tiled=True),
        lax.all_to_all(key_frames, "wide", split_axis=2, concat_axis=1, tiled=True),
        lax.all_to_all(value_frames, "wide", split_axis=2, concat_axis=1, tiled=True),
    )
    local_width = heads_query.shape[2]
    head_count = local_width // HEAD_DIM
    rel_table = relative_table(length, channels).astype(jnp.bfloat16)
    place_rows = (
        mult_trans(rel_table, place_weight)
        .astype(jnp.bfloat16)
        .reshape(2 * length - 1, head_count, HEAD_DIM)
    )
    bias_first = content_bias.astype(jnp.float32).reshape(head_count, HEAD_DIM)
    bias_second = place_bias.astype(jnp.float32).reshape(head_count, HEAD_DIM)
    split_query = heads_query.reshape(groups, length, head_count, HEAD_DIM)
    split_key = heads_key.reshape(groups, length, head_count, HEAD_DIM)
    split_value = heads_value.reshape(groups, length, head_count, HEAD_DIM)
    forward_heads = jax.vmap(
        partial(head_forward, block_rows=QBLK, score_scale=score_scale),
        in_axes=(1, 1, 1, 1, 0, 0, None),
        out_axes=(1, 0),
    )

    def attend_utt(unit_items):
        return forward_heads(
            unit_items[0],
            unit_items[1],
            unit_items[2],
            place_rows,
            bias_first,
            bias_second,
            unit_items[3],
        )

    attended, log_total = lax.map(attend_utt, (split_query, split_key, split_value, key_ok))
    framed = lax.all_to_all(
        attended.reshape(groups, length, local_width),
        "wide",
        split_axis=1,
        concat_axis=2,
        tiled=True,
    ).reshape(row_count, -1)
    stream2 = stream1 + mult_plain(framed, full_out)
    normed_conv, conv_pull = jax.vjp(norm_rows, stream2, conv_gain.astype(jnp.float32))
    conv_low = normed_conv.astype(jnp.bfloat16)
    glu_in = mult_trans(conv_low, full_glu)
    linear = glu_in[:, :channels]
    gating = jax.nn.sigmoid(glu_in[:, channels:])
    gated = (linear * gating * frame_ok).astype(jnp.bfloat16).reshape(groups, frames_dev, channels)
    padded = with_halo(gated, (("wide", 1),), RIM)
    kernel_f = depth_kernel.astype(jnp.float32)
    conv_out = jnp.zeros((groups, frames_dev, channels), jnp.float32)
    for offset in range(KERNEL):
        conv_out = conv_out + padded[:, offset : offset + frames_dev, :] * kernel_f[offset]
    conv_out = conv_out.reshape(row_count, channels)
    middle, middle_pull = jax.vjp(norm_rows, conv_out, middle_gain.astype(jnp.float32))
    swished = jax.nn.silu(middle).astype(jnp.bfloat16)
    stream3 = stream2 + mult_trans(swished, full_point)
    up_second, down_second = gather_ffn(second_up, second_down)
    stream4, saved_second = ffn_forward(
        stream3, second_gain.astype(jnp.float32), up_second, down_second
    )
    final_rows, final_pull = jax.vjp(norm_rows, stream4, final_gain.astype(jnp.float32))
    output = final_rows.astype(jnp.bfloat16).reshape(groups, frames_dev, channels)
    seed_weight = (masked.astype(jnp.float32) * frame_grid).reshape(row_count, 1)
    seed_grad = cotangent.reshape(row_count, channels).astype(jnp.float32) * seed_weight
    grad4, grad_final_gain = final_pull(seed_grad)
    back_up_second, back_down_second = gather_ffn(second_up, second_down)
    grad3, grad_second_gain, grad_up_second, grad_down_second = ffn_backward(
        grad4, saved_second, back_up_second, back_down_second
    )
    summed_second = sum_ffn(grad_up_second, grad_down_second)
    grad_branch = grad3.astype(jnp.bfloat16)
    grad_point = mult_rows(grad_branch, swished)
    grad_middle = mult_plain(grad_branch, full_point) * silu_slope(middle)
    grad_conv, grad_middle_gain = middle_pull(grad_middle)
    conv_grad_low = grad_conv.astype(jnp.bfloat16).reshape(groups, frames_dev, channels)
    grad_padded = with_halo(conv_grad_low, (("wide", 1),), RIM)
    grad_gated = jnp.zeros((groups, frames_dev, channels), jnp.float32)
    kernel_rows = []
    for offset in range(KERNEL):
        grad_gated = (
            grad_gated
            + grad_padded[:, 2 * RIM - offset : 2 * RIM - offset + frames_dev, :] * kernel_f[offset]
        )
        kernel_rows.append(
            jnp.einsum(
                "rzn,rzn->n",
                padded[:, offset : offset + frames_dev, :],
                conv_grad_low,
                preferred_element_type=jnp.float32,
            )
        )
    grad_kernel = jnp.stack(kernel_rows)
    grad_gated = grad_gated.reshape(row_count, channels) * frame_ok
    grad_glu_in = jnp.concatenate(
        [grad_gated * gating, grad_gated * linear * gating * (1.0 - gating)], axis=1
    ).astype(jnp.bfloat16)
    grad_glu = mult_rows(grad_glu_in, conv_low)
    grad_conv_in, grad_conv_gain = conv_pull(mult_plain(grad_glu_in, full_glu))
    grad2 = grad3 + grad_conv_in
    grad_attn = grad2.astype(jnp.bfloat16)
    grad_out = mult_rows(framed, grad_attn)
    grad_framed = (
        mult_trans(grad_attn, full_out).astype(jnp.bfloat16).reshape(groups, frames_dev, -1)
    )
    grad_heads = lax.all_to_all(grad_framed, "wide", split_axis=2, concat_axis=1, tiled=True)
    backward_heads = jax.vmap(
        partial(head_backward, block_rows=QBLK, score_scale=score_scale),
        in_axes=(1, 1, 1, 1, 0, 0, None, 0, 1),
        out_axes=(1, 1, 1, 1, 0, 0),
    )

    def attend_back(unit_items):
        return backward_heads(
            unit_items[0],
            unit_items[1],
            unit_items[2],
            place_rows,
            bias_first,
            bias_second,
            unit_items[3],
            unit_items[4],
            unit_items[5],
        )

    grad_query_h, grad_key_h, grad_value_h, grad_place_h, grad_bias_first, grad_bias_second = (
        lax.map(
            attend_back,
            (
                split_query,
                split_key,
                split_value,
                key_ok,
                log_total,
                grad_heads.reshape(groups, length, head_count, HEAD_DIM),
            ),
        )
    )
    back_query, back_key, back_value = (
        lax.all_to_all(
            grad_query_h.reshape(groups, length, local_width),
            "wide",
            split_axis=1,
            concat_axis=2,
            tiled=True,
        ),
        lax.all_to_all(
            grad_key_h.reshape(groups, length, local_width),
            "wide",
            split_axis=1,
            concat_axis=2,
            tiled=True,
        ),
        lax.all_to_all(
            grad_value_h.reshape(groups, length, local_width),
            "wide",
            split_axis=1,
            concat_axis=2,
            tiled=True,
        ),
    )
    back_query = back_query.reshape(row_count, -1)
    back_key = back_key.reshape(row_count, -1)
    back_value = back_value.reshape(row_count, -1)
    grad_query_w = mult_rows(back_query, attn_low)
    grad_key_w = mult_rows(back_key, attn_low)
    grad_value_w = mult_rows(back_value, attn_low)
    grad_normed = (
        mult_plain(back_query, full_query)
        + mult_plain(back_key, full_key)
        + mult_plain(back_value, full_value)
    )
    grad_attn_in, grad_attn_gain = attn_pull(grad_normed)
    grad1 = grad2 + grad_attn_in
    grad_place_w = jnp.einsum(
        "urc,rd->cd",
        grad_place_h.reshape(groups, 2 * length - 1, local_width),
        rel_table,
        preferred_element_type=jnp.float32,
    )
    grad_content = jnp.sum(grad_bias_first, axis=0).reshape(local_width)
    grad_place_b = jnp.sum(grad_bias_second, axis=0).reshape(local_width)
    back_up_first, back_down_first = gather_ffn(first_up, first_down)
    grad0, grad_first_gain, grad_up_first, grad_down_first = ffn_backward(
        grad1, saved_first, back_up_first, back_down_first
    )
    summed_first = sum_ffn(grad_up_first, grad_down_first)
    mixer_grads = (
        lax.psum_scatter(
            grad_query_w.astype(jnp.bfloat16), "wide", scatter_dimension=0, tiled=True
        ).astype(jnp.float32),
        lax.psum_scatter(
            grad_key_w.astype(jnp.bfloat16), "wide", scatter_dimension=0, tiled=True
        ).astype(jnp.float32),
        lax.psum_scatter(
            grad_value_w.astype(jnp.bfloat16), "wide", scatter_dimension=0, tiled=True
        ).astype(jnp.float32),
        lax.psum_scatter(
            grad_out.astype(jnp.bfloat16), "wide", scatter_dimension=0, tiled=True
        ).astype(jnp.float32),
        lax.psum_scatter(
            grad_glu.astype(jnp.bfloat16), "wide", scatter_dimension=0, tiled=True
        ).astype(jnp.float32),
        lax.psum_scatter(
            grad_point.astype(jnp.bfloat16), "wide", scatter_dimension=0, tiled=True
        ).astype(jnp.float32),
    )
    totals = (
        lax.psum(mixer_grads[0].astype(jnp.bfloat16), "utt").astype(jnp.float32),
        lax.psum(mixer_grads[1].astype(jnp.bfloat16), "utt").astype(jnp.float32),
        lax.psum(mixer_grads[2].astype(jnp.bfloat16), "utt").astype(jnp.float32),
        lax.psum(mixer_grads[3].astype(jnp.bfloat16), "utt").astype(jnp.float32),
        lax.psum(mixer_grads[4].astype(jnp.bfloat16), "utt").astype(jnp.float32),
        lax.psum(mixer_grads[5].astype(jnp.bfloat16), "utt").astype(jnp.float32),
        lax.psum(grad_place_w.astype(jnp.bfloat16), "utt").astype(jnp.float32),
        lax.psum(grad_content.astype(jnp.bfloat16), "utt").astype(jnp.float32),
        lax.psum(grad_place_b.astype(jnp.bfloat16), "utt").astype(jnp.float32),
    )
    small_grads = lax.psum(
        (
            grad_first_gain,
            grad_attn_gain,
            grad_conv_gain,
            grad_middle_gain,
            grad_second_gain,
            grad_final_gain,
            grad_kernel,
        ),
        ("utt", "wide"),
    )
    grad_input = grad0.astype(jnp.bfloat16).reshape(groups, frames_dev, channels)
    return (
        output,
        grad_input,
        small_grads[0],
        summed_first[0],
        summed_first[1],
        small_grads[1],
        totals[0],
        totals[1],
        totals[2],
        totals[3],
        totals[6],
        totals[7],
        totals[8],
        small_grads[2],
        totals[4],
        small_grads[6],
        small_grads[3],
        totals[5],
        small_grads[4],
        summed_second[0],
        summed_second[1],
        small_grads[5],
    )


def solution(mesh):
    shape = dict(mesh.shape)
    if shape["wide"] == 4 and shape["utt"] % 4 == 0:
        mesh = jax.sharding.Mesh(
            mesh.devices.reshape(shape["utt"] // 2, 2, 2, 2), ("z", "core", "y", "x")
        )
        utt, wide, body = ("z", "core"), ("y", "x"), per_chip
    else:
        utt, wide, body = "utt", "wide", per_device
    every = (utt, wide) if utt == "utt" else (*utt, *wide)
    in_specs = (
        P(utt, wide, None),
        P(utt),
        P(utt, wide),
        P(utt, wide, None),
        P(),
        P(every, None),
        P(every, None),
        P(),
        P(wide, None),
        P(wide, None),
        P(wide, None),
        P(wide, None),
        P(wide, None),
        P(wide),
        P(wide),
        P(),
        P(wide, None),
        P(),
        P(),
        P(wide, None),
        P(),
        P(every, None),
        P(every, None),
        P(),
    )
    out_specs = (
        P(utt, wide, None),
        P(utt, wide, None),
        P(),
        P(every, None),
        P(every, None),
        P(),
        P(wide, None),
        P(wide, None),
        P(wide, None),
        P(wide, None),
        P(wide, None),
        P(wide),
        P(wide),
        P(),
        P(wide, None),
        P(),
        P(),
        P(wide, None),
        P(),
        P(every, None),
        P(every, None),
        P(),
    )
    return jax.shard_map(
        body, mesh=mesh, in_specs=in_specs, out_specs=out_specs, check_vma=False
    )
```
